32 devices in a mesh: dp: 8 (over y, x, core), seq: 4 (over z).
Axes of the slice: x: 2, y: 2, z: 4, core: 2. Of those that a mesh axis runs over, the one named last changes fastest.
Arguments:
- frames_in: bfloat16 [8, 2048, 1024], P('dp', 'seq'), may hold values from -6 to 6
- skip_in: bfloat16 [8, 2048, 1024], P('dp', 'seq'), may hold values from -6 to 6
- condition: bfloat16 [8, 2048, 1024], P('dp', 'seq'), may hold values from -6 to 6
- flow_time: float32 [8], replicated, may hold values from 0 to 1
- span_start: int32 [8], P('dp'), may hold values from 0 to 614, as said below
- span_length: int32 [8], P('dp'), may hold values from 1434 to 2048
- out_grad: bfloat16 [8, 2048, 1024], P('dp', 'seq'), may hold values from -0.0234375 to 0.0234375
- skip_proj_state: float32 [3, 2048, 1024], P(None, ('dp', 'seq')), as said below
- attn_qkv_state: float32 [3, 1024, 3072], P(None, ('dp', 'seq')), as said below
- attn_out_state: float32 [3, 1024, 1024], P(None, ('dp', 'seq')), as said below
- ffn_up_state: float32 [3, 1024, 4096], P(None, ('dp', 'seq')), as said below
- ffn_down_state: float32 [3, 4096, 1024], P(None, ('dp', 'seq')), as said below
- ada_mod_state: float32 [3, 1024, 6144], P(None, ('dp', 'seq')), as said below
Outputs:
- block_out: bfloat16 [8, 2048, 1024], P('dp', 'seq')
- frames_grad: bfloat16 [8, 2048, 1024], P('dp', 'seq')
- skip_grad: bfloat16 [8, 2048, 1024], P('dp', 'seq')
- skip_proj_new: float32 [2048, 1024], P(('dp', 'seq'))
- skip_proj_moments: float32 [2, 2048, 1024], P(None, ('dp', 'seq'))
- attn_qkv_new: float32 [1024, 3072], P(('dp', 'seq'))
- attn_qkv_moments: float32 [2, 1024, 3072], P(None, ('dp', 'seq'))
- attn_out_new: float32 [1024, 1024], P(('dp', 'seq'))
- attn_out_moments: float32 [2, 1024, 1024], P(None, ('dp', 'seq'))
- ffn_up_new: float32 [1024, 4096], P(('dp', 'seq'))
- ffn_up_moments: float32 [2, 1024, 4096], P(None, ('dp', 'seq'))
- ffn_down_new: float32 [4096, 1024], P(('dp', 'seq'))
- ffn_down_moments: float32 [2, 4096, 1024], P(None, ('dp', 'seq'))
- ada_mod_new: float32 [1024, 6144], P(('dp', 'seq'))
- ada_mod_moments: float32 [2, 1024, 6144], P(None, ('dp', 'seq'))
The draws below stay inside these ranges and needn't reach their ends.
Inputs may be any that keep to these rules, and one draw needn't show every extreme that they name: span_start + span_length <= 2048 for every utterance. `skip_proj_state`: the second moment (index 2) is positive. `attn_qkv_state`: the second moment (index 2) is positive. `attn_out_state`: the second moment (index 2) is positive. `ffn_up_state`: the second moment (index 2) is positive. `ffn_down_state`: the second moment (index 2) is positive. `ada_mod_state`: the second moment (index 2) is positive.
All inputs are finite; a program needn't handle non-finite values.
Results may differ from the reference program's by a relative error of at most 0.025.
The reference program's roundings to bfloat16 on the way count: a program that leaves them out, or rounds other values in their place, can miss the bound.
Values may be sent and summed in bfloat16 or wider, within the bound.
No kernel may reach another device: no remote copies, remote signals or barrier semaphores. Data moves between devices by JAX's collectives and lax.ppermute only.
A program may use at most 384 MiB of HBM per device.

```python
import math
import jax
import jax.numpy as jnp
from jax import lax

D = 1024
HEADS = 16
DH = 64
FF = 4096
LEN = 2048
STEP = 3
UTTS = 8
TOKENS = 16384
SPAN_MIN = 1434


def span_pair(key):
    folded = jax.random.fold_in(key, 7)
    length_key, ranking_key, start_key = jax.random.split(folded, 3)
    lengths = jax.random.randint(length_key, (UTTS,), SPAN_MIN, LEN + 1)
    ranking = jax.random.permutation(ranking_key, UTTS)
    lengths = lengths.at[ranking[0]].set(LEN).at[ranking[1]].set(SPAN_MIN)
    starts = jax.random.randint(start_key, (UTTS,), 0, LEN + 1) % (LEN - lengths + 1)
    starts = starts.at[ranking[1]].set(LEN - SPAN_MIN)
    return (starts.astype(jnp.int32), lengths.astype(jnp.int32))


def draw_span_start(key, part):
    return span_pair(key)[0]


def draw_span_length(key, part):
    return span_pair(key)[1]


def weight_state(key, row_total, col_total, spread, grad_size):
    first_key, second_key, third_key = jax.random.split(key, 3)
    master = spread * jax.random.normal(first_key, (row_total, col_total), jnp.float32)
    moment_one = grad_size * jax.random.normal(second_key, (row_total, col_total), jnp.float32)
    factor = jnp.exp(jax.random.uniform(third_key, (row_total, col_total), jnp.float32, math.log(0.5), math.log(4.0)))
    moment_two = grad_size * grad_size * factor
    return jnp.stack([master, moment_one, moment_two])


def draw_skip_proj_state(key, part):
    return weight_state(jax.random.fold_in(key, 101), 2 * D, D, (2 * D) ** (-0.5), 1.0)


def draw_attn_qkv_state(key, part):
    return weight_state(jax.random.fold_in(key, 102), D, 3 * D, D ** (-0.5), 1.0)


def draw_attn_out_state(key, part):
    return weight_state(jax.random.fold_in(key, 103), D, D, (D // 16) ** (-0.5), 0.2)


def draw_ffn_up_state(key, part):
    return weight_state(jax.random.fold_in(key, 104), D, FF, D ** (-0.5), 0.3)


def draw_ffn_down_state(key, part):
    return weight_state(jax.random.fold_in(key, 105), FF, D, FF ** (-0.5), 0.5)


def draw_ada_mod_state(key, part):
    return weight_state(jax.random.fold_in(key, 106), D, 6 * D, (D // 8) ** (-0.5), 0.35)


def level_of(rng, dims, shards, low, largest):
    gain = 1.0
    for dim, blocks in shards:
        draws = jax.random.uniform(jax.random.fold_in(jax.random.fold_in(rng, 6), dim), (blocks,), jnp.float32, low / len(shards), largest / len(shards))
        gain = gain * jnp.repeat(jnp.exp(draws), dims[dim] // blocks).reshape((-1,) + (1,) * (len(dims) - 1 - dim))
    return gain


def gaussian(own_key, shape, scale, bound, cuts=(), kind=jnp.bfloat16):
    values = scale * jax.random.normal(own_key, shape, jnp.float32)
    if cuts:
        values = values * level_of(own_key, shape, cuts, -0.22, 0.18)
    return jnp.clip(values, -bound, bound).astype(kind)


def setup_inputs(seed: int = 0) -> dict:
    streams_of = jax.random.split(jax.random.key(seed), 14)
    return {
        "frames_in": gaussian(streams_of[0], (UTTS, LEN, D), 1.0, 6.0, ((0, 8), (1, 4))),
        "skip_in": gaussian(streams_of[1], (UTTS, LEN, D), 1.0, 6.0, ((0, 8), (1, 4))),
        "condition": gaussian(streams_of[2], (UTTS, LEN, D), 1.0, 6.0, ((0, 8), (1, 4))),
        "flow_time": jnp.clip(jax.random.uniform(streams_of[3], (UTTS,), jnp.float32, 0.0, 1.0), 0.0, 1.0),
        "span_start": draw_span_start(jax.random.fold_in(streams_of[13], 71), 0),
        "span_length": draw_span_length(jax.random.fold_in(streams_of[13], 71), 0),
        "out_grad": gaussian(streams_of[6], (UTTS, LEN, D), (0.5 * TOKENS ** -0.5), 0.0234375, ((0, 8), (1, 4))),
        "skip_proj_state": draw_skip_proj_state(jax.random.fold_in(streams_of[13], 71), 0),
        "attn_qkv_state": draw_attn_qkv_state(jax.random.fold_in(streams_of[13], 71), 0),
        "attn_out_state": draw_attn_out_state(jax.random.fold_in(streams_of[13], 71), 0),
        "ffn_up_state": draw_ffn_up_state(jax.random.fold_in(streams_of[13], 71), 0),
        "ffn_down_state": draw_ffn_down_state(jax.random.fold_in(streams_of[13], 71), 0),
        "ada_mod_state": draw_ada_mod_state(jax.random.fold_in(streams_of[13], 71), 0),
    }


@jax.custom_vjp
def low(v):
    return lax.optimization_barrier(v.astype(jnp.bfloat16)).astype(jnp.float32)

@jax.custom_vjp
def low_back(v):
    return v

def low_keep(v):
    return (low(v), None)

def low_pass(kept, grad):
    return (grad,)

def back_keep(v):
    return (v, None)

def back_low(kept, grad):
    return (low(grad),)
low.defvjp(low_keep, low_pass)
low_back.defvjp(back_keep, back_low)
highest = lax.Precision.HIGHEST

def layer_norm(values):
    centre = values - lax.optimization_barrier(jnp.mean(values, axis=-1, keepdims=True))
    spread = lax.optimization_barrier(jnp.mean(centre * centre, axis=-1, keepdims=True))
    return centre * lax.rsqrt(spread + 1e-06)

def modulate(values, scale_mod, shift_mod):
    return layer_norm(values) * (1.0 + scale_mod[:, None, :]) + shift_mod[:, None, :]

def time_features(flow_values, model_width):
    half_size = model_width // 2
    frequency = jnp.exp(-math.log(10000.0) * jnp.arange(half_size, dtype=jnp.float32) / half_size)
    angles = 1000.0 * flow_values[:, None] * frequency[None, :]
    return jax.nn.silu(jnp.concatenate([jnp.sin(angles), jnp.cos(angles)], axis=-1))

def rotary_tables(positions, head_size):
    half_size = head_size // 2
    frequency = jnp.exp(-math.log(10000.0) * jnp.arange(half_size, dtype=jnp.float32) / half_size)
    angles = positions.astype(jnp.float32)[:, None] * frequency[None, :]
    return (jnp.concatenate([jnp.cos(angles), jnp.cos(angles)], axis=-1), jnp.concatenate([jnp.sin(angles), jnp.sin(angles)], axis=-1))

def rotate(values, cosine, sine_table):
    half_size = values.shape[-1] // 2
    turned = jnp.concatenate([-values[..., half_size:], values[..., :half_size]], axis=-1)
    return values * cosine[:, None, :] + turned * sine_table[:, None, :]

def learning_rates():
    fans = (2 * D, D, D // 16, D, FF, D // 8)
    return tuple((2.0 * fan_value ** (-0.5) for fan_value in fans))

def adamw_step(state, gradient, rate):
    master, first_moment, second_moment = (state[0], state[1], state[2])
    first_moment = 0.5 * first_moment + 0.5 * gradient
    second_moment = 0.5 * second_moment + 0.5 * gradient * gradient
    correction = 1.0 - 0.5 ** STEP
    master = master - rate * (first_moment / correction / (jnp.sqrt(second_moment / correction) + 1e-08) + 0.01 * master)
    return (master, jnp.stack([first_moment, second_moment]))

def attend(inputs):
    queries, key_rows, value_rows = inputs
    scores = low_back(jnp.einsum('qhd,khd->hqk', queries, key_rows, precision=highest) * 0.125)
    log_total = jax.nn.logsumexp(scores, axis=-1, keepdims=True)
    probs = low(jnp.exp(scores - log_total))
    return jnp.einsum('hqk,khd->qhd', probs, value_rows, precision=highest)

def layer_group(weights, inputs):
    w_skip, w_qkv, w_out, w_up, w_down = weights
    joined, condition, inside, modulation = inputs
    shift_one, scale_one, gate_one, shift_two, scale_two, gate_two = jnp.split(modulation, 6, axis=-1)
    linear = low_back(jnp.einsum('gle,ed->gld', joined, w_skip, precision=highest))
    hidden = linear + condition * (1.0 - inside[..., None])
    normed = low(modulate(hidden, scale_one, shift_one))
    packed = low_back(jnp.einsum('gld,de->gle', normed, w_qkv, precision=highest))
    group_size, length_all = (hidden.shape[0], hidden.shape[1])
    shaped = packed.reshape(group_size, length_all, 3, HEADS, DH)
    cosine, sine_table = rotary_tables(jnp.arange(length_all, dtype=jnp.int32), DH)
    queries = low(rotate(shaped[:, :, 0], cosine, sine_table))
    key_rows = low(rotate(shaped[:, :, 1], cosine, sine_table))
    value_rows = low(shaped[:, :, 2])
    attended = lax.map(jax.checkpoint(attend), (queries, key_rows, value_rows))
    attended = low_back(low(attended.reshape(group_size, length_all, HEADS * DH)))
    branch = low_back(jnp.einsum('gld,de->gle', attended, w_out, precision=highest))
    middle = hidden + gate_one[:, None, :] * branch
    normed_two = low(modulate(middle, scale_two, shift_two))
    upward = low_back(jnp.einsum('gld,df->glf', normed_two, w_up, precision=highest))
    activated = low(jax.nn.gelu(upward, approximate=True))
    downward = low_back(jnp.einsum('glf,fd->gld', activated, w_down, precision=highest))
    return middle + gate_two[:, None, :] * downward

def reference(frames_in, skip_in, condition, flow_time, span_start, span_length, out_grad, skip_proj_state, attn_qkv_state, attn_out_state, ffn_up_state, ffn_down_state, ada_mod_state):
    states = (skip_proj_state, attn_qkv_state, attn_out_state, ffn_up_state, ffn_down_state, ada_mod_state)
    frame_index = jnp.arange(LEN, dtype=jnp.int32)
    span_stop = span_start + span_length
    inside = ((frame_index[None, :] >= span_start[:, None]) & (frame_index[None, :] < span_stop[:, None])).astype(jnp.float32)
    time_code = low(time_features(flow_time, D))
    cond_values = condition.astype(jnp.float32)
    masters = tuple((state[0] for state in states))
    group_total = UTTS // 2

    def forward(master_list, frames_values, skip_values):
        weights = tuple((low(master) for master in master_list))
        modulation = jnp.dot(time_code, weights[5], precision=highest)
        joined = jnp.concatenate([frames_values, skip_values], axis=-1)

        def one_group(inputs):
            return layer_group(weights[:5], inputs)
        grouped = (joined.reshape(group_total, 2, LEN, 2 * D), cond_values.reshape(group_total, 2, LEN, D), inside.reshape(group_total, 2, LEN), modulation.reshape(group_total, 2, 6 * D))
        outputs = lax.map(jax.checkpoint(one_group), grouped)
        return outputs.reshape(UTTS, LEN, D)
    result, pullback = jax.vjp(forward, masters, frames_in.astype(jnp.float32), skip_in.astype(jnp.float32))
    weight_grads, frames_cot, skip_cot = pullback(out_grad.astype(jnp.float32) * inside[..., None])
    rates = learning_rates()
    updated = []
    for state, gradient, rate in zip(states, weight_grads, rates):
        new_master, new_moments = adamw_step(state, gradient, rate)
        updated.append(new_master)
        updated.append(new_moments)
    return (result.astype(jnp.bfloat16), frames_cot.astype(jnp.bfloat16), skip_cot.astype(jnp.bfloat16), updated[0], updated[1], updated[2], updated[3], updated[4], updated[5], updated[6], updated[7], updated[8], updated[9], updated[10], updated[11])
```

```python
import functools
import math

import jax
import jax.numpy as jnp
from jax import lax
from jax.experimental import pallas as pl
from jax.experimental.pallas import tpu as pltpu
from jax.sharding import PartitionSpec as P

D = 1024
HEADS = 16
DH = 64
FF = 4096
STEP = 3
LOG2E = 1.4426950408889634
BF = jnp.bfloat16
F32 = jnp.float32
MIB = 2**20
highest = lax.Precision.HIGHEST


def dot_nn(a, b):
    return lax.dot_general(a, b, (((1,), (0,)), ((), ())), preferred_element_type=F32)


def dot_nt(a, b):
    return lax.dot_general(a, b, (((1,), (1,)), ((), ())), preferred_element_type=F32)


def dot_tn(a, b):
    return lax.dot_general(a, b, (((0,), (0,)), ((), ())), preferred_element_type=F32)


def params(mib):
    return pltpu.CompilerParams(vmem_limit_bytes=mib * MIB)


def cost(flops, moved):
    return pl.CostEstimate(flops=int(flops), bytes_accessed=int(moved), transcendentals=0)


def whole(shape):
    return pl.BlockSpec(shape, lambda i: (0,) * len(shape))


def time_features(flow_values, model_width):
    half_size = model_width // 2
    frequency = jnp.exp(-math.log(10000.0) * jnp.arange(half_size, dtype=F32) / half_size)
    angles = 1000.0 * flow_values[:, None] * frequency[None, :]
    return jax.nn.silu(jnp.concatenate([jnp.sin(angles), jnp.cos(angles)], axis=-1))


def rotary_tables(positions, heads):
    half = DH // 2
    frequency = jnp.exp(-math.log(10000.0) * jnp.arange(half, dtype=F32) / half)
    angles = positions.astype(F32)[:, None] * frequency[None, :]
    cosine, sine = jnp.cos(angles), jnp.sin(angles)
    return (
        jnp.concatenate([cosine, cosine] * heads, axis=-1),
        jnp.concatenate([-sine, sine] * heads, axis=-1),
    )


def swap_halves(values):
    width = values.shape[1]
    half = DH // 2
    if width == DH:
        return jnp.concatenate([values[:, half:], values[:, :half]], axis=1)
    lane = lax.broadcasted_iota(jnp.int32, (1, width), 1)
    first = (lane % DH) < half
    return jnp.where(
        first, pltpu.roll(values, width - half, 1), pltpu.roll(values, half, 1)
    )


def normalise(values):
    centre = values - jnp.mean(values, axis=-1, keepdims=True)
    spread = jnp.mean(centre * centre, axis=-1, keepdims=True)
    inverse = lax.rsqrt(spread + 1e-06)
    return centre * inverse, inverse


def norm_back(normal, inverse, scaled):
    return inverse * (
        scaled
        - jnp.mean(scaled, axis=-1, keepdims=True)
        - normal * jnp.mean(scaled * normal, axis=-1, keepdims=True)
    )


def gelu_and_slope(u):
    root = math.sqrt(2.0 / math.pi)
    square = u * u
    t = jnp.tanh(root * u * (1.0 + 0.044715 * square))
    half = 0.5 * (1.0 + t)
    slope = half + 0.5 * u * (1.0 - t * t) * (root * (1.0 + 3.0 * 0.044715 * square))
    return u * half, slope


def learning_rates():
    fans = (2 * D, D, D // 16, D, FF, D // 8)
    return tuple((2.0 * fan_value ** (-0.5) for fan_value in fans))


def adamw_step(state, gradient, rate):
    master, first_moment, second_moment = (state[0], state[1], state[2])
    first_moment = 0.5 * first_moment + 0.5 * gradient
    second_moment = 0.5 * second_moment + 0.5 * gradient * gradient
    correction = 1.0 - 0.5**STEP
    master = master - rate * (
        first_moment / correction / (jnp.sqrt(second_moment / correction) + 1e-08) + 0.01 * master
    )
    return (master, jnp.stack([first_moment, second_moment]))


def skip_kernel(fr_ref, sk_ref, cond_ref, w_ref, mod_ref, hidden_ref, normed_ref):
    width = fr_ref.shape[1]
    hidden = (
        dot_nn(fr_ref[...], w_ref[:width])
        + dot_nn(sk_ref[...], w_ref[width:])
        + cond_ref[...].astype(F32)
    )
    hidden_ref[...] = hidden
    normal, _ = normalise(hidden)
    normed_ref[...] = (normal * (1.0 + mod_ref[1:2]) + mod_ref[0:1]).astype(BF)


def skip_forward(frames, skips, cond, weight, mod):
    rows, width = frames.shape
    block = min(256, rows)
    row_spec = pl.BlockSpec((block, width), lambda i: (i, 0))
    return pl.pallas_call(
        skip_kernel,
        grid=(rows // block,),
        in_specs=[row_spec, row_spec, row_spec, whole(weight.shape), whole(mod.shape)],
        out_specs=[row_spec, row_spec],
        out_shape=[
            jax.ShapeDtypeStruct((rows, width), F32),
            jax.ShapeDtypeStruct((rows, width), BF),
        ],
        compiler_params=params(40),
        cost_estimate=cost(4 * rows * width * width, 12 * rows * width + 4 * width * width),
    )(frames, skips, cond, weight, mod)


def qkv_kernel(x_ref, wq_ref, wk_ref, wv_ref, cos_ref, sin_ref, out_ref):
    x = x_ref[...]
    cosine, sine = cos_ref[...], sin_ref[...]
    pairs = out_ref.shape[0]
    q, k, v = dot_nn(x, wq_ref[...]), dot_nn(x, wk_ref[...]), dot_nn(x, wv_ref[...])
    for j in range(pairs):
        part = slice(j * 128, (j + 1) * 128)
        out_ref[j, :, 0:128] = (q[:, part] * cosine + swap_halves(q[:, part]) * sine).astype(BF)
        out_ref[j, :, 128:256] = (k[:, part] * cosine + swap_halves(k[:, part]) * sine).astype(BF)
        out_ref[j, :, 256:384] = v[:, part].astype(BF)


def qkv_forward(normed, weight, cosine, sine):
    rows, width = normed.shape
    pairs = width // 128
    per_step = 2
    cols = 128 * per_step
    steps = pairs // per_step

    def columns(part):
        return pl.BlockSpec((width, cols), lambda i: (0, part * steps + i))

    return pl.pallas_call(
        qkv_kernel,
        grid=(steps,),
        in_specs=[
            whole(normed.shape),
            columns(0),
            columns(1),
            columns(2),
            whole(cosine.shape),
            whole(sine.shape),
        ],
        out_specs=pl.BlockSpec((per_step, rows, 384), lambda i: (i, 0, 0)),
        out_shape=jax.ShapeDtypeStruct((pairs, rows, 384), BF),
        compiler_params=params(40),
        cost_estimate=cost(6 * rows * width * width, 8 * rows * width + 6 * width * width),
    )(normed, weight, weight, weight, cosine, sine)


def attend_kernel(heads, block, qkv_ref, out_ref, log_ref):
    width = heads * DH
    i = pl.program_id(0)
    q = qkv_ref[pl.ds(pl.multiple_of(i * block, block), block), 0:width]
    k = qkv_ref[:, width : 2 * width]
    v = qkv_ref[:, 2 * width : 3 * width]
    lane = lax.broadcasted_iota(jnp.int32, (1, width), 1) // DH
    outs = []
    for h in range(heads):
        own = jnp.where(lane == h, q, jnp.zeros_like(q)) if heads > 1 else q
        scores = dot_nt(k, own) * (0.125 * LOG2E)
        top = jnp.max(scores, axis=0, keepdims=True)
        probs = jnp.exp2(scores - top)
        total = jnp.sum(probs, axis=0, keepdims=True)
        outs.append(dot_tn(v[:, h * DH : (h + 1) * DH], probs.astype(BF)) * (1.0 / total))
        log_ref[h : h + 1, :] = top + jnp.log2(total)
    out_ref[...] = (jnp.concatenate(outs, axis=0) if heads > 1 else outs[0]).T.astype(BF)


def attend(qkv, heads):
    length = qkv.shape[0]
    width = heads * DH
    block = min(512, length)
    return pl.pallas_call(
        functools.partial(attend_kernel, heads, block),
        grid=(length // block,),
        in_specs=[whole(qkv.shape)],
        out_specs=[
            pl.BlockSpec((block, width), lambda i: (i, 0)),
            pl.BlockSpec((heads, block), lambda i: (0, i)),
        ],
        out_shape=[
            jax.ShapeDtypeStruct((length, width), BF),
            jax.ShapeDtypeStruct((heads, length), F32),
        ],
        compiler_params=params(50),
        cost_estimate=cost(16 * length * length * DH * heads, 8 * length * width),
    )(qkv)


def attend_back_kernel(
    heads, block, qkv_ref, do_ref, o_ref, log_ref, cos_ref, sin_ref, out_ref, dq_sum, delta
):
    width = heads * DH
    i = pl.program_id(0)
    lane = lax.broadcasted_iota(jnp.int32, (1, width), 1) // DH

    @pl.when(i == 0)
    def _():
        dq_sum[...] = jnp.zeros_like(dq_sum)
        product = (do_ref[...].astype(F32) * o_ref[...].astype(F32)).T
        for h in range(heads):
            delta[h : h + 1, :] = jnp.sum(product[h * DH : (h + 1) * DH], axis=0, keepdims=True)

    here = pl.ds(pl.multiple_of(i * block, block), block)
    q = qkv_ref[:, 0:width]
    k = qkv_ref[here, width : 2 * width]
    v = qkv_ref[here, 2 * width : 3 * width]
    do = do_ref[...]
    k_turned = k.T
    dk = dv = None
    for h in range(heads):
        own = lane == h
        k_own = jnp.where(own, k, jnp.zeros_like(k)) if heads > 1 else k
        v_own = jnp.where(own, v, jnp.zeros_like(v)) if heads > 1 else v
        scores = dot_nt(k_own, q) * (0.125 * LOG2E)
        probs = jnp.exp2(scores - log_ref[h : h + 1, :])
        prob_grad = dot_nt(v_own, do)
        score_grad = (probs * (prob_grad - delta[h : h + 1, :])).astype(BF)
        part = slice(h * DH, (h + 1) * DH)
        dq_sum[part, :] += dot_nn(k_turned[part], score_grad)
        dv_own = dot_nn(probs.astype(BF), do)
        dk_own = dot_nn(score_grad, q)
        dv = dv_own if dv is None else jnp.where(own, dv_own, dv)
        dk = dk_own if dk is None else jnp.where(own, dk_own, dk)
    dk = dk * 0.125
    out_ref[here, width : 2 * width] = (
        dk * cos_ref[here, :] - swap_halves(dk) * sin_ref[here, :]
    ).astype(BF)
    out_ref[here, 2 * width : 3 * width] = dv.astype(BF)

    @pl.when(i == pl.num_programs(0) - 1)
    def _():
        dq = (dq_sum[...] * 0.125).T
        out_ref[:, 0:width] = (dq * cos_ref[...] - swap_halves(dq) * sin_ref[...]).astype(BF)


def attend_back(qkv, do, o, log_total, cosine, sine, heads):
    length = qkv.shape[0]
    width = heads * DH
    block = min(512, length)
    return pl.pallas_call(
        functools.partial(attend_back_kernel, heads, block),
        grid=(length // block,),
        in_specs=[whole(a.shape) for a in (qkv, do, o, log_total, cosine, sine)],
        out_specs=whole(qkv.shape),
        out_shape=jax.ShapeDtypeStruct(qkv.shape, BF),
        scratch_shapes=[pltpu.VMEM((width, length), F32), pltpu.VMEM((heads, length), F32)],
        compiler_params=params(58),
        cost_estimate=cost(24 * length * length * DH * heads, 20 * length * width),
    )(qkv, do, o, log_total, cosine, sine)


def gather_columns(refs, out_ref, heads):
    count = len(refs)
    groups = refs[0].shape[0]
    width = heads * DH
    for j in range(groups):
        for c in range(count):
            at = (j * count + c) * width
            out_ref[:, at : at + width] = refs[c][j]


def out_kernel(count, heads, *refs):
    o_refs = refs[:count]
    w_ref, hidden_ref, mod_ref, attended_ref, branch_ref, middle_ref, normed_ref = refs[count:]
    gather_columns(o_refs, attended_ref, heads)
    branch = dot_nn(attended_ref[...], w_ref[...])
    branch_ref[...] = branch
    middle = hidden_ref[...] + mod_ref[2:3] * branch
    middle_ref[...] = middle
    normal, _ = normalise(middle)
    normed_ref[...] = (normal * (1.0 + mod_ref[4:5]) + mod_ref[3:4]).astype(BF)


def out_forward(o_chunks, heads, weight, hidden, mod):
    rows, width = hidden.shape
    block = min(256, rows)
    row_spec = pl.BlockSpec((block, width), lambda i: (i, 0))
    groups = o_chunks[0].shape[0]
    o_spec = pl.BlockSpec((groups, block, heads * DH), lambda i: (0, i, 0))
    return pl.pallas_call(
        functools.partial(out_kernel, len(o_chunks), heads),
        grid=(rows // block,),
        in_specs=[o_spec] * len(o_chunks) + [whole(weight.shape), row_spec, whole(mod.shape)],
        out_specs=[row_spec] * 4,
        out_shape=[
            jax.ShapeDtypeStruct((rows, width), BF),
            jax.ShapeDtypeStruct((rows, width), F32),
            jax.ShapeDtypeStruct((rows, width), F32),
            jax.ShapeDtypeStruct((rows, width), BF),
        ],
        compiler_params=params(40),
        cost_estimate=cost(2 * rows * width * width, 18 * rows * width + 2 * width * width),
    )(*o_chunks, weight, hidden, mod)


def ffn_kernel(x_ref, dc_ref, up_ref, dn_ref, y_ref, dx_ref, gu_ref, gd_ref, x_turned):
    @pl.when(pl.program_id(0) == 0)
    def _():
        x_turned[...] = x_ref[...].T
        y_ref[...] = jnp.zeros_like(y_ref)
        dx_ref[...] = jnp.zeros_like(dx_ref)

    dc = dc_ref[...]
    up, dn = up_ref[...], dn_ref[...]
    value, slope = gelu_and_slope(dot_nn(x_ref[...], up))
    activated = value.astype(BF)
    up_cot = (dot_nt(dc, dn) * slope).astype(BF)
    y_ref[...] += dot_nn(activated, dn)
    dx_ref[...] += dot_nt(up_cot, up)
    gu_ref[...] = dot_nn(x_turned[...], up_cot).astype(BF)
    gd_ref[...] = dot_tn(activated, dc).astype(BF)


def ffn(x, dc, up, dn):
    rows, width = x.shape
    hidden_width = up.shape[1]
    block = min(512, hidden_width)
    up_spec = pl.BlockSpec((width, block), lambda i: (0, i))
    dn_spec = pl.BlockSpec((block, width), lambda i: (i, 0))
    return pl.pallas_call(
        ffn_kernel,
        grid=(hidden_width // block,),
        in_specs=[whole(x.shape), whole(x.shape), up_spec, dn_spec],
        out_specs=[whole(x.shape), whole(x.shape), up_spec, dn_spec],
        out_shape=[
            jax.ShapeDtypeStruct((rows, width), F32),
            jax.ShapeDtypeStruct((rows, width), F32),
            jax.ShapeDtypeStruct(up.shape, BF),
            jax.ShapeDtypeStruct(dn.shape, BF),
        ],
        scratch_shapes=[pltpu.VMEM((width, rows), BF)],
        compiler_params=params(60),
        cost_estimate=cost(12 * rows * width * hidden_width, 8 * width * hidden_width),
    )(x, dc, up, dn)


def mid_kernel(count, heads, *refs):
    y_ref, dx_ref, middle_ref, branch_ref, grad_ref, w_ref, mod_ref = refs[:7]
    block_ref, mgrad_ref, bcot_ref, sums_ref = refs[7:11]
    chunk_refs = refs[11:]

    @pl.when(pl.program_id(0) == 0)
    def _():
        sums_ref[...] = jnp.zeros_like(sums_ref)

    y, middle, w = y_ref[...], middle_ref[...], dx_ref[...]
    grad = grad_ref[...].astype(F32)
    block_ref[...] = (middle + mod_ref[5:6] * y).astype(BF)
    normal, inverse = normalise(middle)
    middle_grad = grad + norm_back(normal, inverse, w * (1.0 + mod_ref[4:5]))
    mgrad_ref[...] = middle_grad
    branch_cot = (middle_grad * mod_ref[2:3]).astype(BF)
    bcot_ref[...] = branch_cot
    sums_ref[0:1] += jnp.sum(middle_grad * branch_ref[...], axis=0, keepdims=True)
    sums_ref[1:2] += jnp.sum(w, axis=0, keepdims=True)
    sums_ref[2:3] += jnp.sum(w * normal, axis=0, keepdims=True)
    sums_ref[3:4] += jnp.sum(grad * y, axis=0, keepdims=True)
    attended_grad = dot_nt(branch_cot, w_ref[...]).astype(BF)
    width = heads * DH
    for j in range(chunk_refs[0].shape[0]):
        for c in range(count):
            at = (j * count + c) * width
            chunk_refs[c][j] = attended_grad[:, at : at + width]


def mid_back(y, dx, middle, branch, grad, weight, mod, groups, count, heads):
    rows, width = y.shape
    block = min(256, rows)
    row_spec = pl.BlockSpec((block, width), lambda i: (i, 0))
    chunk_spec = pl.BlockSpec((groups, block, heads * DH), lambda i: (0, i, 0))
    return pl.pallas_call(
        functools.partial(mid_kernel, count, heads),
        grid=(rows // block,),
        in_specs=[row_spec] * 5 + [whole(weight.shape), whole(mod.shape)],
        out_specs=[row_spec] * 3 + [whole((8, width))] + [chunk_spec] * count,
        out_shape=[
            jax.ShapeDtypeStruct((rows, width), BF),
            jax.ShapeDtypeStruct((rows, width), F32),
            jax.ShapeDtypeStruct((rows, width), BF),
            jax.ShapeDtypeStruct((8, width), F32),
        ]
        + [jax.ShapeDtypeStruct((groups, rows, heads * DH), BF)] * count,
        compiler_params=params(50),
        cost_estimate=cost(2 * rows * width * width, 28 * rows * width + 2 * width * width),
    )(y, dx, middle, branch, grad, weight, mod)


def last_kernel(count, heads, *refs):
    chunk_refs = refs[:count]
    hidden_ref, mgrad_ref, wqkv_ref, wskip_ref, mod_ref = refs[count : count + 5]
    cot_ref, hgrad_ref, frames_ref, skips_ref, sums_ref = refs[count + 5 :]

    @pl.when(pl.program_id(0) == 0)
    def _():
        sums_ref[...] = jnp.zeros_like(sums_ref)

    width = heads * DH
    model = hidden_ref.shape[1]
    for j in range(chunk_refs[0].shape[0]):
        for c in range(count):
            at = (j * count + c) * width
            for part in range(3):
                cot_ref[:, part * model + at : part * model + at + width] = chunk_refs[c][
                    j, :, part * width : (part + 1) * width
                ]
    w = dot_nt(cot_ref[...], wqkv_ref[...])
    normal, inverse = normalise(hidden_ref[...])
    sums_ref[0:1] += jnp.sum(w, axis=0, keepdims=True)
    sums_ref[1:2] += jnp.sum(w * normal, axis=0, keepdims=True)
    hidden_grad = (
        mgrad_ref[...] + norm_back(normal, inverse, w * (1.0 + mod_ref[1:2]))
    ).astype(BF)
    hgrad_ref[...] = hidden_grad
    frames_ref[...] = dot_nt(hidden_grad, wskip_ref[:model]).astype(BF)
    skips_ref[...] = dot_nt(hidden_grad, wskip_ref[model:]).astype(BF)


def last_back(chunks, heads, hidden, middle_grad, w_qkv, w_skip, mod):
    rows, width = hidden.shape
    block = min(256, rows)
    row_spec = pl.BlockSpec((block, width), lambda i: (i, 0))
    groups = chunks[0].shape[0]
    chunk_spec = pl.BlockSpec((groups, block, 3 * heads * DH), lambda i: (0, i, 0))
    return pl.pallas_call(
        functools.partial(last_kernel, len(chunks), heads),
        grid=(rows // block,),
        in_specs=[chunk_spec] * len(chunks)
        + [row_spec, row_spec, whole(w_qkv.shape), whole(w_skip.shape), whole(mod.shape)],
        out_specs=[
            pl.BlockSpec((block, 3 * width), lambda i: (i, 0)),
            row_spec,
            row_spec,
            row_spec,
            whole((8, width)),
        ],
        out_shape=[
            jax.ShapeDtypeStruct((rows, 3 * width), BF),
            jax.ShapeDtypeStruct((rows, width), BF),
            jax.ShapeDtypeStruct((rows, width), BF),
            jax.ShapeDtypeStruct((rows, width), BF),
            jax.ShapeDtypeStruct((8, width), F32),
        ],
        compiler_params=params(58),
        cost_estimate=cost(10 * rows * width * width, 26 * rows * width + 10 * width * width),
    )(*chunks, hidden, middle_grad, w_qkv, w_skip, mod)


def bits_of(axis):
    size = lax.axis_size(axis)
    return [(axis, b) for b in reversed(range(size.bit_length() - 1))]


def my_bit(level):
    axis, bit = level
    return (lax.axis_index(axis) >> bit) & 1


def swap(values, level):
    axis, bit = level
    return lax.ppermute(values, axis, [(i, i ^ (1 << bit)) for i in range(lax.axis_size(axis))])


def scatter_sum(grad, order):
    dims = bits_of("dp") + bits_of("seq")
    rows, cols = grad.shape
    terms = [grad.reshape([2] * len(dims) + [rows // 2 ** len(dims), cols])]
    for level in order:
        at, mine = dims.index(level), my_bit(level)
        dims.pop(at)

        def halves(side):
            return [lax.dynamic_index_in_dim(t, side, at, keepdims=False) for t in terms]

        leaving = halves(1 - mine)
        total = leaving[0]
        if len(leaving) > 1:
            total = sum(t.astype(F32) for t in leaving).astype(grad.dtype)
        arrived = swap(total, level)
        terms = halves(mine) + [arrived]
    return sum(t.astype(F32) for t in terms)


def exchange(values, axis):
    return lax.all_to_all(values, axis, 0, 0, tiled=True)


def modulation_rows(partial, order):
    dims = bits_of("dp")
    count, cols = partial.shape
    held = partial.reshape([2] * len(dims) + [count // 2 ** len(dims), cols])
    for level in order:
        at, mine = dims.index(level), my_bit(level)
        dims.pop(at)
        leaving = lax.dynamic_index_in_dim(held, 1 - mine, at, keepdims=False)
        held = lax.dynamic_index_in_dim(held, mine, at, keepdims=False) + swap(leaving, level)
    for level in bits_of("seq"):
        held = held + swap(held, level)
    return held


def modulation_cots(own, total_count):
    for level in bits_of("seq"):
        own = own + swap(own, level)
    for level in reversed(bits_of("dp")):
        other = swap(own, level)
        mine = my_bit(level)
        own = jnp.where(
            mine == 0,
            jnp.concatenate([own, other], axis=0),
            jnp.concatenate([other, own], axis=0),
        )
    return own


def per_device(
    frames_in,
    skip_in,
    condition,
    flow_time,
    span_start,
    span_length,
    out_grad,
    skip_proj_state,
    attn_qkv_state,
    attn_out_state,
    ffn_up_state,
    ffn_down_state,
    ada_mod_state,
):
    utter_count, rows, width = frames_in.shape
    seq = lax.axis_size("seq")
    everyone = ("dp", "seq")
    owned = attn_qkv_state.shape[1]
    length = rows * seq
    me = lax.axis_index(everyone)
    positions = lax.axis_index("seq") * rows + jnp.arange(rows, dtype=jnp.int32)

    group_heads = HEADS // seq
    heads = min(2, group_heads)
    count = group_heads // heads

    skip_full = lax.all_gather(skip_proj_state[0].astype(BF), everyone, axis=0, tiled=True)
    qkv_full = lax.all_gather(attn_qkv_state[0].astype(BF), everyone, axis=0, tiled=True)
    out_full = lax.all_gather(attn_out_state[0].astype(BF), everyone, axis=0, tiled=True)
    up_full = lax.all_gather(ffn_up_state[0].astype(BF), everyone, axis=0, tiled=True)
    down_full = lax.all_gather(ffn_down_state[0].astype(BF), everyone, axis=0, tiled=True)

    dp_bits, seq_bits = bits_of("dp"), bits_of("seq")
    core, planes = dp_bits[-1], dp_bits[:-1]

    time_code = time_features(flow_time, width).astype(BF)
    time_own = lax.dynamic_slice_in_dim(time_code, me * owned, owned, 1)
    mod_part = jnp.dot(time_own, ada_mod_state[0].astype(BF), preferred_element_type=F32)
    modulation = modulation_rows(mod_part, [core] + planes)

    cos_all, sin_all = rotary_tables(jnp.arange(length, dtype=jnp.int32), heads)
    cos_own, sin_own = rotary_tables(positions, 2)
    span_stop = span_start + span_length

    outs = []
    assert utter_count == 1
    mod = modulation.reshape(6, width)
    inside = (positions >= span_start[0]) & (positions < span_stop[0])
    frames, skips = frames_in[0], skip_in[0]
    cond = jnp.where(inside[:, None], jnp.zeros_like(condition[0]), condition[0])
    grad = jnp.where(inside[:, None], out_grad[0], jnp.zeros_like(out_grad[0]))
    down_cot = (grad.astype(F32) * mod[5:6]).astype(BF)

    hidden, normed = skip_forward(frames, skips, cond, skip_full, mod)
    packed = qkv_forward(normed, qkv_full, cos_own, sin_own)
    if heads == 2:
        packed = packed.reshape(seq, count, rows, 3 * heads * DH)
    else:
        packed = packed.reshape(HEADS // 2, rows, 3, 2, DH).transpose(0, 3, 1, 2, 4)
        packed = packed.reshape(seq, count, rows, 3 * heads * DH)
    qkv_chunks = [exchange(packed[:, c], "seq").reshape(length, -1) for c in range(count)]
    attended = [attend(chunk, heads) for chunk in qkv_chunks]
    o_chunks = [exchange(o.reshape(seq, rows, heads * DH), "seq") for o, _ in attended]

    attended_low, branch, middle, normed_two = out_forward(
        o_chunks, heads, out_full, hidden, mod
    )
    downward, normed_two_grad, up_part, down_part = ffn(normed_two, down_cot, up_full, down_full)
    mid = mid_back(
        downward, normed_two_grad, middle, branch, grad, out_full, mod, seq, count, heads
    )
    block_out, middle_grad, branch_cot, mid_sums = mid[:4]
    up_wgrad = scatter_sum(up_part, [core] + planes + seq_bits)
    down_wgrad = scatter_sum(down_part, [core] + planes[::-1] + seq_bits)

    cot_chunks = []
    for c in range(count):
        do = exchange(mid[4 + c], "seq").reshape(length, heads * DH)
        o, log_total = attended[c]
        back = attend_back(qkv_chunks[c], do, o, log_total, cos_all, sin_all, heads)
        cot_chunks.append(exchange(back.reshape(seq, rows, 3 * heads * DH), "seq"))
    out_part = dot_tn(attended_low, branch_cot).astype(BF)
    out_wgrad = scatter_sum(out_part, [core] + planes[::-1] + seq_bits)

    packed_cot, hidden_grad, frames_grad, skip_grad, last_sums = last_back(
        cot_chunks, heads, hidden, middle_grad, qkv_full, skip_full, mod
    )
    skip_part = jnp.concatenate(
        [dot_tn(frames, hidden_grad).astype(BF), dot_tn(skips, hidden_grad).astype(BF)], axis=0
    )
    skip_wgrad = scatter_sum(skip_part, [core] + planes[::-1] + seq_bits)
    qkv_part = dot_tn(normed, packed_cot).astype(BF)
    qkv_wgrad = scatter_sum(qkv_part, [core] + planes + seq_bits)

    mod_cot = jnp.concatenate(
        [last_sums[0], last_sums[1], mid_sums[0], mid_sums[1], mid_sums[2], mid_sums[3]]
    ).reshape(1, 6 * width)
    mod_cots = modulation_cots(mod_cot, flow_time.shape[0])
    mod_wgrad = lax.dot_general(
        time_own.astype(F32),
        mod_cots,
        (((0,), (0,)), ((), ())),
        precision=highest,
        preferred_element_type=F32,
    )

    states = (
        skip_proj_state,
        attn_qkv_state,
        attn_out_state,
        ffn_up_state,
        ffn_down_state,
        ada_mod_state,
    )
    grads = (skip_wgrad, qkv_wgrad, out_wgrad, up_wgrad, down_wgrad, mod_wgrad)
    outs = [block_out[None], frames_grad[None], skip_grad[None]]
    for state, gradient, rate in zip(states, grads, learning_rates()):
        outs.extend(adamw_step(state, gradient, rate))
    return tuple(outs)


def solution(mesh):
    tokens = P("dp", "seq", None)
    state = P(None, ("dp", "seq"), None)
    master = P(("dp", "seq"), None)
    return jax.shard_map(
        per_device,
        mesh=mesh,
        in_specs=(tokens, tokens, tokens, P(), P("dp"), P("dp"), tokens) + (state,) * 6,
        out_specs=(tokens,) * 3 + (master, state) * 6,
        check_vma=False,
    )
```

```python
import functools
import math

import jax
import jax.numpy as jnp
from jax import lax
from jax.experimental import pallas as pl
from jax.experimental.pallas import tpu as pltpu
from jax.sharding import PartitionSpec as P

D = 1024
HEADS = 16
DH = 64
FF = 4096
STEP = 3
LOG2E = 1.4426950408889634
BF = jnp.bfloat16
F32 = jnp.float32
MIB = 2**20
highest = lax.Precision.HIGHEST


def dot_nn(a, b):
    return lax.dot_general(a, b, (((1,), (0,)), ((), ())), preferred_element_type=F32)


def dot_nt(a, b):
    return lax.dot_general(a, b, (((1,), (1,)), ((), ())), preferred_element_type=F32)


def dot_tn(a, b):
    return lax.dot_general(a, b, (((0,), (0,)), ((), ())), preferred_element_type=F32)


def params(mib):
    return pltpu.CompilerParams(vmem_limit_bytes=mib * MIB)


def cost(flops, moved):
    return pl.CostEstimate(flops=int(flops), bytes_accessed=int(moved), transcendentals=0)


def whole(shape):
    return pl.BlockSpec(shape, lambda i: (0,) * len(shape))


def time_features(flow_values, model_width):
    half_size = model_width // 2
    frequency = jnp.exp(-math.log(10000.0) * jnp.arange(half_size, dtype=F32) / half_size)
    angles = 1000.0 * flow_values[:, None] * frequency[None, :]
    return jax.nn.silu(jnp.concatenate([jnp.sin(angles), jnp.cos(angles)], axis=-1))


def rotary_tables(positions, heads):
    half = DH // 2
    frequency = jnp.exp(-math.log(10000.0) * jnp.arange(half, dtype=F32) / half)
    angles = positions.astype(F32)[:, None] * frequency[None, :]
    cosine, sine = jnp.cos(angles), jnp.sin(angles)
    return (
        jnp.concatenate([cosine, cosine] * heads, axis=-1),
        jnp.concatenate([-sine, sine] * heads, axis=-1),
    )


def swap_halves(values):
    width = values.shape[1]
    half = DH // 2
    if width == DH:
        return jnp.concatenate([values[:, half:], values[:, :half]], axis=1)
    lane = lax.broadcasted_iota(jnp.int32, (1, width), 1)
    first = (lane % DH) < half
    return jnp.where(
        first, pltpu.roll(values, width - half, 1), pltpu.roll(values, half, 1)
    )


def normalise(values):
    centre = values - jnp.mean(values, axis=-1, keepdims=True)
    spread = jnp.mean(centre * centre, axis=-1, keepdims=True)
    inverse = lax.rsqrt(spread + 1e-06)
    return centre * inverse, inverse


def norm_back(normal, inverse, scaled):
    return inverse * (
        scaled
        - jnp.mean(scaled, axis=-1, keepdims=True)
        - normal * jnp.mean(scaled * normal, axis=-1, keepdims=True)
    )


def gelu_and_slope(u):
    root = math.sqrt(2.0 / math.pi)
    square = u * u
    t = jnp.tanh(root * u * (1.0 + 0.044715 * square))
    half = 0.5 * (1.0 + t)
    slope = half + 0.5 * u * (1.0 - t * t) * (root * (1.0 + 3.0 * 0.044715 * square))
    return u * half, slope


def learning_rates():
    fans = (2 * D, D, D // 16, D, FF, D // 8)
    return tuple((2.0 * fan_value ** (-0.5) for fan_value in fans))


def adamw_step(state, gradient, rate):
    master, first_moment, second_moment = (state[0], state[1], state[2])
    first_moment = 0.5 * first_moment + 0.5 * gradient
    second_moment = 0.5 * second_moment + 0.5 * gradient * gradient
    correction = 1.0 - 0.5**STEP
    master = master - rate * (
        first_moment / correction / (jnp.sqrt(second_moment / correction) + 1e-08) + 0.01 * master
    )
    return (master, jnp.stack([first_moment, second_moment]))


def stack_rows(packed_ref, out_ref, owned):
    cols = out_ref.shape[1]
    pieces = packed_ref.shape[1] // cols
    for r in range(packed_ref.shape[0] // owned):
        for q in range(pieces):
            at = (r * pieces + q) * owned
            out_ref[at : at + owned] = packed_ref[
                r * owned : (r + 1) * owned, q * cols : (q + 1) * cols
            ]


def skip_kernel(
    owned, fr_ref, sk_ref, cond_ref, packed_ref, mod_ref, hidden_ref, normed_ref, w_ref
):
    @pl.when(pl.program_id(0) == 0)
    def _():
        stack_rows(packed_ref, w_ref, owned)

    width = fr_ref.shape[1]
    hidden = (
        dot_nn(fr_ref[...], w_ref[:width])
        + dot_nn(sk_ref[...], w_ref[width:])
        + cond_ref[...].astype(F32)
    )
    hidden_ref[...] = hidden
    normal, _ = normalise(hidden)
    normed_ref[...] = (normal * (1.0 + mod_ref[1:2]) + mod_ref[0:1]).astype(BF)


def skip_weight(weight, owned, width):
    if owned % 16 == 0:
        return weight, pl.BlockSpec((width, 2 * width), lambda i: (0, 0)), owned
    full = stacked(weight[:, : 2 * width], owned, width)
    return full, whole(full.shape), 2 * width


def skip_forward(frames, skips, cond, weight, mod, owned):
    rows, width = frames.shape
    block = min(256, rows)
    row_spec = pl.BlockSpec((block, width), lambda i: (i, 0))
    weight, weight_spec, piece = skip_weight(weight, owned, width)
    return pl.pallas_call(
        functools.partial(skip_kernel, piece),
        grid=(rows // block,),
        in_specs=[row_spec, row_spec, row_spec, weight_spec, whole(mod.shape)],
        out_specs=[row_spec, row_spec],
        out_shape=[
            jax.ShapeDtypeStruct((rows, width), F32),
            jax.ShapeDtypeStruct((rows, width), BF),
        ],
        scratch_shapes=[pltpu.VMEM((2 * width, width), BF)],
        compiler_params=params(40),
        cost_estimate=cost(4 * rows * width * width, 12 * rows * width + 4 * width * width),
    )(frames, skips, cond, weight, mod)


def qkv_kernel(x_ref, wq_ref, wk_ref, wv_ref, cos_ref, sin_ref, out_ref, w_ref):
    for part, ref in enumerate((wq_ref, wk_ref, wv_ref)):
        w_ref[:, part * 128 : (part + 1) * 128] = ref[...]
    packed = dot_nn(x_ref[...], w_ref[...])
    cosine, sine = cos_ref[...], sin_ref[...]
    for part in range(2):
        raw = packed[:, part * 128 : (part + 1) * 128]
        out_ref[0, :, part * 128 : (part + 1) * 128] = (
            raw * cosine + swap_halves(raw) * sine
        ).astype(BF)
    out_ref[0, :, 256:384] = packed[:, 256:384].astype(BF)


def qkv_forward(normed, weight, cosine, sine, first, stride):
    rows, width = normed.shape
    pairs = width // 128
    steps = pairs // stride

    def columns(part):
        return pl.BlockSpec((width, 128), lambda i: (0, (2 + part) * pairs + i * stride + first))

    return pl.pallas_call(
        qkv_kernel,
        grid=(steps,),
        in_specs=[
            whole(normed.shape),
            columns(0),
            columns(1),
            columns(2),
            whole(cosine.shape),
            whole(sine.shape),
        ],
        out_specs=pl.BlockSpec((1, rows, 384), lambda i: (i, 0, 0)),
        out_shape=jax.ShapeDtypeStruct((steps, rows, 384), BF),
        scratch_shapes=[pltpu.VMEM((width, 384), BF)],
        compiler_params=params(40),
        cost_estimate=cost(
            6 * rows * width * 128 * steps, 8 * rows * 128 * steps + 6 * width * 128 * steps
        ),
    )(normed, weight, weight, weight, cosine, sine)


def attend_kernel(heads, block, qkv_ref, out_ref, log_ref):
    width = heads * DH
    i = pl.program_id(0)
    q = qkv_ref[pl.ds(pl.multiple_of(i * block, block), block), 0:width]
    k = qkv_ref[:, width : 2 * width]
    v = qkv_ref[:, 2 * width : 3 * width]
    lane = lax.broadcasted_iota(jnp.int32, (1, width), 1) // DH
    outs = []
    for h in range(heads):
        own = jnp.where(lane == h, q, jnp.zeros_like(q)) if heads > 1 else q
        scores = dot_nt(k, own) * (0.125 * LOG2E)
        top = jnp.max(scores, axis=0, keepdims=True)
        probs = jnp.exp2(scores - top)
        total = jnp.sum(probs, axis=0, keepdims=True)
        outs.append(dot_tn(v[:, h * DH : (h + 1) * DH], probs.astype(BF)) * (1.0 / total))
        log_ref[h : h + 1, :] = top + jnp.log2(total)
    out_ref[...] = (jnp.concatenate(outs, axis=0) if heads > 1 else outs[0]).T.astype(BF)


def attend(qkv, heads):
    length = qkv.shape[0]
    width = heads * DH
    block = min(512, length)
    return pl.pallas_call(
        functools.partial(attend_kernel, heads, block),
        grid=(length // block,),
        in_specs=[whole(qkv.shape)],
        out_specs=[
            pl.BlockSpec((block, width), lambda i: (i, 0)),
            pl.BlockSpec((heads, block), lambda i: (0, i)),
        ],
        out_shape=[
            jax.ShapeDtypeStruct((length, width), BF),
            jax.ShapeDtypeStruct((heads, length), F32),
        ],
        compiler_params=params(50),
        cost_estimate=cost(16 * length * length * DH * heads, 8 * length * width),
    )(qkv)


def attend_back_kernel(
    heads, block, qkv_ref, do_ref, o_ref, log_ref, cos_ref, sin_ref, out_ref, dq_sum, delta
):
    width = heads * DH
    i = pl.program_id(0)
    lane = lax.broadcasted_iota(jnp.int32, (1, width), 1) // DH

    @pl.when(i == 0)
    def _():
        dq_sum[...] = jnp.zeros_like(dq_sum)
        product = (do_ref[...].astype(F32) * o_ref[...].astype(F32)).T
        for h in range(heads):
            delta[h : h + 1, :] = jnp.sum(product[h * DH : (h + 1) * DH], axis=0, keepdims=True)

    here = pl.ds(pl.multiple_of(i * block, block), block)
    q = qkv_ref[:, 0:width]
    k = qkv_ref[here, width : 2 * width]
    v = qkv_ref[here, 2 * width : 3 * width]
    do = do_ref[...]
    k_turned = k.T
    dk = dv = None
    for h in range(heads):
        own = lane == h
        k_own = jnp.where(own, k, jnp.zeros_like(k)) if heads > 1 else k
        v_own = jnp.where(own, v, jnp.zeros_like(v)) if heads > 1 else v
        scores = dot_nt(k_own, q) * (0.125 * LOG2E)
        probs = jnp.exp2(scores - log_ref[h : h + 1, :])
        prob_grad = dot_nt(v_own, do)
        score_grad = (probs * (prob_grad - delta[h : h + 1, :])).astype(BF)
        part = slice(h * DH, (h + 1) * DH)
        dq_sum[part, :] += dot_nn(k_turned[part], score_grad)
        dv_own = dot_nn(probs.astype(BF), do)
        dk_own = dot_nn(score_grad, q)
        dv = dv_own if dv is None else jnp.where(own, dv_own, dv)
        dk = dk_own if dk is None else jnp.where(own, dk_own, dk)
    dk = dk * 0.125
    out_ref[here, width : 2 * width] = (
        dk * cos_ref[here, :] - swap_halves(dk) * sin_ref[here, :]
    ).astype(BF)
    out_ref[here, 2 * width : 3 * width] = dv.astype(BF)

    @pl.when(i == pl.num_programs(0) - 1)
    def _():
        dq = (dq_sum[...] * 0.125).T
        out_ref[:, 0:width] = (dq * cos_ref[...] - swap_halves(dq) * sin_ref[...]).astype(BF)


def attend_back(qkv, do, o, log_total, cosine, sine, heads):
    length = qkv.shape[0]
    width = heads * DH
    block = min(512, length)
    return pl.pallas_call(
        functools.partial(attend_back_kernel, heads, block),
        grid=(length // block,),
        in_specs=[whole(a.shape) for a in (qkv, do, o, log_total, cosine, sine)],
        out_specs=whole(qkv.shape),
        out_shape=jax.ShapeDtypeStruct(qkv.shape, BF),
        scratch_shapes=[pltpu.VMEM((width, length), F32), pltpu.VMEM((heads, length), F32)],
        compiler_params=params(58),
        cost_estimate=cost(24 * length * length * DH * heads, 20 * length * width),
    )(qkv, do, o, log_total, cosine, sine)


def gather_columns(refs, out_ref, heads):
    count = len(refs)
    groups = refs[0].shape[0]
    width = heads * DH
    for j in range(groups):
        for c in range(count):
            at = (j * count + c) * width
            out_ref[:, at : at + width] = refs[c][j]


def out_kernel(count, heads, *refs):
    o_refs = refs[:count]
    w_ref, hidden_ref, mod_ref, attended_ref, branch_ref, middle_ref, normed_ref = refs[count:]
    gather_columns(o_refs, attended_ref, heads)
    branch = dot_nn(attended_ref[...], w_ref[...])
    branch_ref[...] = branch
    middle = hidden_ref[...] + mod_ref[2:3] * branch
    middle_ref[...] = middle
    normal, _ = normalise(middle)
    normed_ref[...] = (normal * (1.0 + mod_ref[4:5]) + mod_ref[3:4]).astype(BF)


def out_forward(o_chunks, heads, weight, hidden, mod, at):
    rows, width = hidden.shape
    block = min(256, rows)
    row_spec = pl.BlockSpec((block, width), lambda i: (i, 0))
    groups = o_chunks[0].shape[0]
    o_spec = pl.BlockSpec((groups, block, heads * DH), lambda i: (0, i, 0))
    return pl.pallas_call(
        functools.partial(out_kernel, len(o_chunks), heads),
        grid=(rows // block,),
        in_specs=[o_spec] * len(o_chunks)
        + [pl.BlockSpec((width, width), lambda i: (0, at)), row_spec, whole(mod.shape)],
        out_specs=[row_spec] * 4,
        out_shape=[
            jax.ShapeDtypeStruct((rows, width), BF),
            jax.ShapeDtypeStruct((rows, width), F32),
            jax.ShapeDtypeStruct((rows, width), F32),
            jax.ShapeDtypeStruct((rows, width), BF),
        ],
        compiler_params=params(40),
        cost_estimate=cost(2 * rows * width * width, 18 * rows * width + 2 * width * width),
    )(*o_chunks, weight, hidden, mod)


def ffn_kernel(
    owned, x_ref, dc_ref, up_ref, packed_ref, y_ref, dx_ref, grads_ref, x_turned, dn_ref, gu, gd, sems
):
    i, last = pl.program_id(0), pl.num_programs(0) - 1
    slot = lax.rem(i, 2)
    block = up_ref.shape[1]
    part = packed_ref.shape[0]
    pieces = block // part

    def sends(step, at):
        across = pl.ds(pl.multiple_of(step * block, block), block)
        down = pl.ds(pl.multiple_of(step * part, part), part)
        half = grads_ref.shape[1] // 2
        return (
            pltpu.make_async_copy(gu.at[at], grads_ref.at[:, across], sems.at[0, at]),
            pltpu.make_async_copy(gd.at[at], grads_ref.at[down, pl.ds(half, half)], sems.at[1, at]),
        )

    @pl.when(i == 0)
    def _():
        x_turned[...] = x_ref[...].T
        y_ref[...] = jnp.zeros_like(y_ref)
        dx_ref[...] = jnp.zeros_like(dx_ref)

    stack_rows(packed_ref, dn_ref, owned)
    dc = dc_ref[...]
    up, dn = up_ref[...], dn_ref[...]
    value, slope = gelu_and_slope(dot_nn(x_ref[...], up))
    activated = value.astype(BF)
    up_cot = (dot_nt(dc, dn) * slope).astype(BF)
    y_ref[...] += dot_nn(activated, dn)
    dx_ref[...] += dot_nt(up_cot, up)

    @pl.when(i >= 2)
    def _():
        for copy in sends(i - 2, slot):
            copy.wait()

    gu[slot] = dot_nn(x_turned[...], up_cot).astype(BF)
    down_grad = dot_tn(activated, dc).astype(BF)
    width = dc.shape[1]
    for r in range(part // owned):
        for q in range(pieces):
            at = (r * pieces + q) * owned
            gd[slot, r * owned : (r + 1) * owned, q * width : (q + 1) * width] = down_grad[
                at : at + owned
            ]
    for copy in sends(i, slot):
        copy.start()

    @pl.when(i == last)
    def _():
        for copy in sends(last - 1, 1 - slot) + sends(last, slot):
            copy.wait()


def ffn(x, dc, weights, owned):
    rows, width = x.shape
    hidden_width = FF
    pieces = hidden_width // width
    steps = hidden_width // 512
    block = 512
    part = block // pieces
    packed = weights
    if owned % 16:
        full = stacked(weights[:, :hidden_width], owned, width)
        packed = side_by_side_blocks(full, part, pieces)
    piece = owned if owned % 16 == 0 else part
    y, dx, grads = pl.pallas_call(
        functools.partial(ffn_kernel, piece),
        grid=(steps,),
        in_specs=[
            whole(x.shape),
            whole(x.shape),
            pl.BlockSpec((width, block), lambda i: (0, steps + i)),
            pl.BlockSpec((part, hidden_width), lambda i: (i, 0)),
        ],
        out_specs=[whole(x.shape), whole(x.shape), pl.BlockSpec(memory_space=pl.ANY)],
        out_shape=[
            jax.ShapeDtypeStruct((rows, width), F32),
            jax.ShapeDtypeStruct((rows, width), F32),
            jax.ShapeDtypeStruct((width, 2 * hidden_width), BF),
        ],
        scratch_shapes=[
            pltpu.VMEM((width, rows), BF),
            pltpu.VMEM((block, width), BF),
            pltpu.VMEM((2, width, block), BF),
            pltpu.VMEM((2, part, hidden_width), BF),
            pltpu.SemaphoreType.DMA((2, 2)),
        ],
        compiler_params=params(60),
        cost_estimate=cost(12 * rows * width * hidden_width, 8 * width * hidden_width),
    )(x, dc, weights, packed)
    if owned % 16:
        full = stacked(grads[:, hidden_width:], part, width)
        grads = jnp.concatenate(
            [grads[:, :hidden_width], side_by_side_blocks(full, owned, pieces)], axis=1
        )
    return y, dx, grads


def mid_kernel(count, heads, *refs):
    y_ref, dx_ref, middle_ref, branch_ref, grad_ref, w_ref, mod_ref = refs[:7]
    block_ref, mgrad_ref, bcot_ref, sums_ref = refs[7:11]
    chunk_refs = refs[11:]

    @pl.when(pl.program_id(0) == 0)
    def _():
        sums_ref[...] = jnp.zeros_like(sums_ref)

    y, middle, w = y_ref[...], middle_ref[...], dx_ref[...]
    grad = grad_ref[...].astype(F32)
    block_ref[...] = (middle + mod_ref[5:6] * y).astype(BF)
    normal, inverse = normalise(middle)
    middle_grad = grad + norm_back(normal, inverse, w * (1.0 + mod_ref[4:5]))
    mgrad_ref[...] = middle_grad
    branch_cot = (middle_grad * mod_ref[2:3]).astype(BF)
    bcot_ref[...] = branch_cot
    sums_ref[0:1] += jnp.sum(middle_grad * branch_ref[...], axis=0, keepdims=True)
    sums_ref[1:2] += jnp.sum(w, axis=0, keepdims=True)
    sums_ref[2:3] += jnp.sum(w * normal, axis=0, keepdims=True)
    sums_ref[3:4] += jnp.sum(grad * y, axis=0, keepdims=True)
    attended_grad = dot_nt(branch_cot, w_ref[...]).astype(BF)
    width = heads * DH
    for j in range(chunk_refs[0].shape[0]):
        for c in range(count):
            at = (j * count + c) * width
            chunk_refs[c][j] = attended_grad[:, at : at + width]


def mid_back(y, dx, middle, branch, grad, weight, mod, groups, count, heads, at):
    rows, width = y.shape
    block = min(256, rows)
    row_spec = pl.BlockSpec((block, width), lambda i: (i, 0))
    chunk_spec = pl.BlockSpec((groups, block, heads * DH), lambda i: (0, i, 0))
    return pl.pallas_call(
        functools.partial(mid_kernel, count, heads),
        grid=(rows // block,),
        in_specs=[row_spec] * 5
        + [pl.BlockSpec((width, width), lambda i: (0, at)), whole(mod.shape)],
        out_specs=[row_spec] * 3 + [whole((8, width))] + [chunk_spec] * count,
        out_shape=[
            jax.ShapeDtypeStruct((rows, width), BF),
            jax.ShapeDtypeStruct((rows, width), F32),
            jax.ShapeDtypeStruct((rows, width), BF),
            jax.ShapeDtypeStruct((8, width), F32),
        ]
        + [jax.ShapeDtypeStruct((groups, rows, heads * DH), BF)] * count,
        compiler_params=params(50),
        cost_estimate=cost(2 * rows * width * width, 28 * rows * width + 2 * width * width),
    )(y, dx, middle, branch, grad, weight, mod)


def last_kernel(count, heads, owned, *refs):
    chunk_refs = refs[:count]
    hidden_ref, mgrad_ref, wq_ref, wk_ref, wv_ref, packed_ref, mod_ref = refs[count : count + 7]
    hgrad_ref, frames_ref, skips_ref, sums_ref, wskip_ref, cot_ref = refs[count + 7 :]

    @pl.when(pl.program_id(0) == 0)
    def _():
        sums_ref[...] = jnp.zeros_like(sums_ref)
        stack_rows(packed_ref, wskip_ref, owned)

    width = heads * DH
    model = hidden_ref.shape[1]
    for j in range(chunk_refs[0].shape[0]):
        for c in range(count):
            at = (j * count + c) * width
            for part in range(3):
                cot_ref[:, part * model + at : part * model + at + width] = chunk_refs[c][
                    j, :, part * width : (part + 1) * width
                ]
    w = (
        dot_nt(cot_ref[:, :model], wq_ref[...])
        + dot_nt(cot_ref[:, model : 2 * model], wk_ref[...])
        + dot_nt(cot_ref[:, 2 * model :], wv_ref[...])
    )
    normal, inverse = normalise(hidden_ref[...])
    sums_ref[0:1] += jnp.sum(w, axis=0, keepdims=True)
    sums_ref[1:2] += jnp.sum(w * normal, axis=0, keepdims=True)
    hidden_grad = (
        mgrad_ref[...] + norm_back(normal, inverse, w * (1.0 + mod_ref[1:2]))
    ).astype(BF)
    hgrad_ref[...] = hidden_grad
    frames_ref[...] = dot_nt(hidden_grad, wskip_ref[:model]).astype(BF)
    skips_ref[...] = dot_nt(hidden_grad, wskip_ref[model:]).astype(BF)


def last_back(chunks, heads, hidden, middle_grad, weights, mod, owned):
    rows, width = hidden.shape
    block = min(256, rows)
    row_spec = pl.BlockSpec((block, width), lambda i: (i, 0))
    groups = chunks[0].shape[0]
    chunk_spec = pl.BlockSpec((groups, block, 3 * heads * DH), lambda i: (0, i, 0))
    w_skip, skip_spec, piece = skip_weight(weights, owned, width)

    def part_spec(part):
        return pl.BlockSpec((width, width), lambda i: (0, 2 + part))

    return pl.pallas_call(
        functools.partial(last_kernel, len(chunks), heads, piece),
        grid=(rows // block,),
        in_specs=[chunk_spec] * len(chunks)
        + [row_spec, row_spec, part_spec(0), part_spec(1), part_spec(2)]
        + [skip_spec, whole(mod.shape)],
        out_specs=[
            row_spec,
            row_spec,
            row_spec,
            whole((8, width)),
        ],
        out_shape=[
            jax.ShapeDtypeStruct((rows, width), BF),
            jax.ShapeDtypeStruct((rows, width), BF),
            jax.ShapeDtypeStruct((rows, width), BF),
            jax.ShapeDtypeStruct((8, width), F32),
        ],
        scratch_shapes=[pltpu.VMEM((2 * width, width), BF), pltpu.VMEM((block, 3 * width), BF)],
        compiler_params=params(58),
        cost_estimate=cost(10 * rows * width * width, 26 * rows * width + 10 * width * width),
    )(*chunks, hidden, middle_grad, weights, weights, weights, w_skip, mod)


def qkv_grad_kernel(extra, *refs):
    x_ref, chunk_ref = refs[:2]
    out_ref, x_turned = refs[2 + extra], refs[3 + extra]

    @pl.when(pl.program_id(0) == 0)
    def _():
        x_turned[...] = x_ref[...].T
        if extra:
            refs[4 + extra][...] = refs[2][...].T

    cols = chunk_ref.shape[2]
    out_ref[:, :cols] = dot_nn(x_turned[...], chunk_ref[0]).astype(BF)
    if extra:
        out_ref[:, cols:] = dot_nn(refs[4 + extra][...], refs[3][...]).astype(BF)


def qkv_grad(normed, chunk, *extra):
    groups, rows, cols = chunk.shape
    width = normed.shape[1]
    more = width // groups if extra else 0
    if cols % 128:
        parts = [dot_tn(normed, chunk.transpose(1, 0, 2).reshape(rows, groups * cols))]
        parts += [dot_tn(*extra)] if extra else []
        parts = [p.reshape(width, groups, -1) for p in parts]
        return jnp.concatenate(parts, axis=2).reshape(width, -1).astype(BF)
    extra_specs = [whole((rows, width)), pl.BlockSpec((rows, more), lambda i: (0, i))]
    turned = pltpu.VMEM((width, rows), BF)
    return pl.pallas_call(
        functools.partial(qkv_grad_kernel, len(extra)),
        grid=(groups,),
        in_specs=[whole(normed.shape), pl.BlockSpec((1, rows, cols), lambda i: (i, 0, 0))]
        + extra_specs[: len(extra)],
        out_specs=pl.BlockSpec((width, cols + more), lambda i: (0, i)),
        out_shape=jax.ShapeDtypeStruct((width, groups * (cols + more)), BF),
        scratch_shapes=[turned] * (2 if extra else 1),
        compiler_params=params(30),
        cost_estimate=cost(
            2 * rows * width * groups * (cols + more), 5 * width * groups * (cols + more)
        ),
    )(normed, chunk, *extra)


def bits_of(axis):
    size = lax.axis_size(axis)
    return [(axis, b) for b in reversed(range(size.bit_length() - 1))]


def my_bit(level):
    axis, bit = level
    return (lax.axis_index(axis) >> bit) & 1


def swap(values, level):
    axis, bit = level
    return lax.ppermute(values, axis, [(i, i ^ (1 << bit)) for i in range(lax.axis_size(axis))])


def after(values, *others):
    return lax.optimization_barrier((values, *others))[0]


class ScatterSum:
    def __init__(self, grad, order, dims):
        self.dims, self.order = list(dims), list(order)
        rows, cols = grad.shape
        split = [2] * len(self.dims)
        self.terms = [grad.reshape(split + [rows // 2 ** len(split), cols])]

    def hold(self, *waits):
        if waits:
            self.terms[-1] = after(self.terms[-1], *waits)

    def step(self, *waits):
        self.hold(*waits)
        level = self.order.pop(0)
        at, mine = self.dims.index(level), my_bit(level)
        self.dims.pop(at)

        def halves(side):
            return [lax.dynamic_index_in_dim(t, side, at, keepdims=False) for t in self.terms]

        leaving = halves(1 - mine)
        total = leaving[0]
        if len(leaving) > 1:
            total = sum(t.astype(F32) for t in leaving).astype(total.dtype)
        self.sent = total
        arrived = swap(total, level)
        self.terms = halves(mine) + [arrived]
        return arrived

    def total(self):
        while self.order:
            self.step()
        return sum(t.astype(F32) for t in self.terms)


def exchange(values, axis):
    return lax.all_to_all(values, axis, 0, 0, tiled=True)


def modulation_rows(partial, order):
    dims = bits_of("dp")
    count, cols = partial.shape
    held = partial.reshape([2] * len(dims) + [count // 2 ** len(dims), cols])
    for level in order:
        at, mine = dims.index(level), my_bit(level)
        dims.pop(at)
        leaving = lax.dynamic_index_in_dim(held, 1 - mine, at, keepdims=False)
        held = lax.dynamic_index_in_dim(held, mine, at, keepdims=False) + swap(leaving, level)
    for level in bits_of("seq"):
        held = held + swap(held, level)
    return held


class ModulationCots:
    def __init__(self, own):
        self.own, self.order = own, bits_of("seq") + bits_of("dp")[::-1]

    def step(self, *waits):
        level = self.order.pop(0)
        own = after(self.own, *waits)
        if level[0] == "seq":
            self.own = own + swap(own, level)
        else:
            self.own = gather_pairwise(own, [level])


def side_by_side(own, rows):
    return jnp.concatenate(jnp.split(own, own.shape[0] // rows, axis=0), axis=1)


def stacked(full, rows, cols):
    pieces = full.shape[1] // cols
    blocks = full.reshape(full.shape[0] // rows, rows, pieces, cols)
    return blocks.transpose(0, 2, 1, 3).reshape(full.shape[0] * pieces, cols)


def side_by_side_blocks(full, rows, pieces):
    cols = full.shape[1]
    blocks = full.reshape(full.shape[0] // (rows * pieces), pieces, rows, cols)
    return blocks.transpose(0, 2, 1, 3).reshape(full.shape[0] // pieces, pieces * cols)


def gather_pairwise(own, order, last_wait=None, last_use=None):
    rows, cols = own.shape
    held, bits = own.reshape(1, rows, cols), []
    for level in order:
        if last_wait is not None and len(bits) == len(order) - 1:
            held = after(held, last_wait)
        other = swap(held, level)
        if last_use is not None and len(bits) == len(order) - 1:
            other = after(other, last_use)
        at = sum(1 for bit in bits if bit > level[1])
        bits.append(level[1])
        shape = [2] * (len(bits) - 1)
        own_part = held.reshape(shape + [rows, cols])
        other_part = other.reshape(shape + [rows, cols])
        held = jnp.where(
            my_bit(level) == 0,
            jnp.stack([own_part, other_part], axis=at),
            jnp.stack([other_part, own_part], axis=at),
        ).reshape(2 ** len(bits), rows, cols)
    return held.reshape(-1, cols)


def per_device(
    frames_in,
    skip_in,
    condition,
    flow_time,
    span_start,
    span_length,
    out_grad,
    skip_proj_state,
    attn_qkv_state,
    attn_out_state,
    ffn_up_state,
    ffn_down_state,
    ada_mod_state,
):
    utter_count, rows, width = frames_in.shape
    seq = lax.axis_size("seq")
    everyone = ("dp", "seq")
    owned = attn_qkv_state.shape[1]
    hidden_width = ffn_up_state.shape[2]
    length = rows * seq
    me = lax.axis_index(everyone)
    positions = lax.axis_index("seq") * rows + jnp.arange(rows, dtype=jnp.int32)

    group_heads = HEADS // seq
    heads = min(2, group_heads)
    count = group_heads // heads

    first_full = lax.all_gather(
        jnp.concatenate(
            [side_by_side(skip_proj_state[0].astype(BF), owned), attn_qkv_state[0].astype(BF)],
            axis=1,
        ),
        everyone,
        axis=0,
        tiled=True,
    )
    out_at = 2 * hidden_width // width

    dp_bits, seq_bits = bits_of("dp"), bits_of("seq")
    core, planes = dp_bits[-1], dp_bits[:-1]

    time_code = time_features(flow_time, width).astype(BF)
    time_own = lax.dynamic_slice_in_dim(time_code, me * owned, owned, 1)
    mod_part = jnp.dot(time_own, ada_mod_state[0].astype(BF), preferred_element_type=F32)
    modulation = modulation_rows(mod_part, [core] + planes)

    cos_all, sin_all = rotary_tables(jnp.arange(length, dtype=jnp.int32), heads)
    cos_own, sin_own = rotary_tables(positions, 2)
    span_stop = span_start + span_length

    outs = []
    assert utter_count == 1
    mod = modulation.reshape(6, width)
    inside = (positions >= span_start[0]) & (positions < span_stop[0])
    frames, skips = frames_in[0], skip_in[0]
    cond = jnp.where(inside[:, None], jnp.zeros_like(condition[0]), condition[0])
    grad = jnp.where(inside[:, None], out_grad[0], jnp.zeros_like(out_grad[0]))
    down_cot = (grad.astype(F32) * mod[5:6]).astype(BF)

    hidden, normed = skip_forward(frames, skips, cond, first_full, mod, owned)
    if heads == 2:
        packed = []
        for c in range(count):
            x = after(normed, packed[-1]) if packed else normed
            packed.append(qkv_forward(x, first_full, cos_own, sin_own, c, count))
    else:
        packed = qkv_forward(normed, first_full, cos_own, sin_own, 0, 1)
        packed = packed.reshape(HEADS // 2, rows, 3, 2, DH).transpose(0, 3, 1, 2, 4)
        packed = [packed.reshape(seq, rows, 3 * DH)]
    second_own = jnp.concatenate(
        [
            side_by_side(ffn_down_state[0].astype(BF), owned),
            ffn_up_state[0].astype(BF),
            attn_out_state[0].astype(BF),
        ],
        axis=1,
    )
    second_own = gather_pairwise(after(second_own, modulation), seq_bits, first_full, packed[-1])
    second_full = lax.all_gather(second_own, "dp", axis=0, tiled=True)
    qkv_chunks = [exchange(part, "seq").reshape(length, -1) for part in packed]
    attended = [attend(chunk, heads) for chunk in qkv_chunks]
    o_chunks = [exchange(o.reshape(seq, rows, heads * DH), "seq") for o, _ in attended]

    attended_low, branch, middle, normed_two = out_forward(
        o_chunks, heads, second_full, hidden, mod, out_at
    )
    downward, normed_two_grad, ffn_part = ffn(normed_two, down_cot, second_full, owned)
    mid = mid_back(
        downward,
        normed_two_grad,
        middle,
        branch,
        grad,
        second_full,
        mod,
        seq,
        count,
        heads,
        out_at,
    )
    block_out, middle_grad, branch_cot, mid_sums = mid[:4]
    every_bit = dp_bits + seq_bits
    rising = seq_bits[::-1]
    ffn_part = lax.psum_scatter(ffn_part, "dp", scatter_dimension=0, tiled=True)
    backs = []
    for c in range(count):
        do = exchange(mid[4 + c], "seq").reshape(length, heads * DH)
        o, log_total = attended[c]
        backs.append(attend_back(qkv_chunks[c], do, o, log_total, cos_all, sin_all, heads))
    cot_chunks = [exchange(b.reshape(seq, rows, 3 * heads * DH), "seq") for b in backs]

    sent = [backs[-1]]

    def leave(part):
        part.step(sent[-1])
        sent.append(part.sent)

    ffn_sum = None
    qkv_sums = []
    for c in range(count):
        if c == count - 1:
            ffn_sum = ScatterSum(after(ffn_part, cot_chunks[-1]), rising, seq_bits)
            leave(ffn_sum)
        extra = () if c else (attended_low, branch_cot)
        grad_part = qkv_grad(normed, after(cot_chunks[c], sent[-1]), *extra)
        order = planes if c % 2 else planes[::-1]
        qkv_sums.append(ScatterSum(grad_part, [core] + order + rising, every_bit))
        leave(qkv_sums[-1])
        if c < count - 1:
            leave(qkv_sums[-1])
    for part in qkv_sums:
        leave(part)
    cot_chunks[-1] = after(cot_chunks[-1], sent[-1])
    hidden_grad, frames_grad, skip_grad, last_sums = last_back(
        cot_chunks, heads, hidden, middle_grad, first_full, mod, owned
    )
    skip_part = jnp.concatenate(
        [dot_tn(frames, hidden_grad).astype(BF), dot_tn(skips, hidden_grad).astype(BF)], axis=0
    )
    half = width // 2
    skip_sums = [
        ScatterSum(skip_part[:, :half], [core] + planes[::-1] + rising, every_bit),
        ScatterSum(skip_part[:, half:], [core] + planes + rising, every_bit),
    ]
    mod_cot = jnp.concatenate(
        [last_sums[0], last_sums[1], mid_sums[0], mid_sums[1], mid_sums[2], mid_sums[3]]
    ).reshape(1, 6 * width)
    mod_cots = ModulationCots(mod_cot)
    others = [ffn_sum] + qkv_sums
    marks, finished = [], {}
    for part in others:
        part.hold(hidden_grad)
    while skip_sums[0].order:
        for part in skip_sums:
            leave(part)
        marks.append(sent[-1])
        for part in others:
            if part.order:
                leave(part)
            else:
                finished.setdefault(part, len(marks) - 1)
        if mod_cots.order:
            mod_cots.step(sent[-1])
    for part in others:
        while part.order:
            leave(part)
        part.hold(marks[min(finished.get(part, len(marks)) + 1, len(marks) - 1)])
    while mod_cots.order:
        mod_cots.step()
    mod_cots = mod_cots.own
    ffn_total = ffn_sum.total()
    up_wgrad = ffn_total[:, :hidden_width]
    down_wgrad = stacked(ffn_total[:, hidden_width:], owned, width)
    skip_wgrad = jnp.concatenate([part.total() for part in skip_sums], axis=1)
    qkv_totals = [part.total().reshape(owned, seq, -1) for part in qkv_sums]
    chunk_cols = 3 * heads * DH
    out_wgrad = qkv_totals[0][:, :, chunk_cols:].reshape(owned, width)
    qkv_wgrad = jnp.stack(
        [t[:, :, :chunk_cols].reshape(owned, seq, 3, heads * DH) for t in qkv_totals], axis=3
    )
    qkv_wgrad = qkv_wgrad.transpose(0, 2, 1, 3, 4).reshape(owned, 3 * width)

    mod_wgrad = lax.dot_general(
        time_own.astype(F32),
        mod_cots,
        (((0,), (0,)), ((), ())),
        precision=highest,
        preferred_element_type=F32,
    )

    states = (
        skip_proj_state,
        attn_qkv_state,
        attn_out_state,
        ffn_up_state,
        ffn_down_state,
        ada_mod_state,
    )
    grads = (skip_wgrad, qkv_wgrad, out_wgrad, up_wgrad, down_wgrad, mod_wgrad)
    outs = [block_out[None], frames_grad[None], skip_grad[None]]
    for state, gradient, rate in zip(states, grads, learning_rates()):
        outs.extend(adamw_step(state, gradient, rate))
    return tuple(outs)


def solution(mesh):
    tokens = P("dp", "seq", None)
    state = P(None, ("dp", "seq"), None)
    master = P(("dp", "seq"), None)
    return jax.shard_map(
        per_device,
        mesh=mesh,
        in_specs=(tokens, tokens, tokens, P(), P("dp"), P("dp"), tokens) + (state,) * 6,
        out_specs=(tokens,) * 3 + (master, state) * 6,
        check_vma=False,
    )
```

```python
import functools
import math

import jax
import jax.numpy as jnp
from jax import lax
from jax.experimental import pallas as pl
from jax.experimental.pallas import tpu as pltpu
from jax.sharding import PartitionSpec as P

D = 1024
HEADS = 16
DH = 64
FF = 4096
STEP = 3
LOG2E = 1.4426950408889634
BF = jnp.bfloat16
F32 = jnp.float32
MIB = 2**20
highest = lax.Precision.HIGHEST


def dot_nn(a, b):
    return lax.dot_general(a, b, (((1,), (0,)), ((), ())), preferred_element_type=F32)


def dot_nt(a, b):
    return lax.dot_general(a, b, (((1,), (1,)), ((), ())), preferred_element_type=F32)


def dot_tn(a, b):
    return lax.dot_general(a, b, (((0,), (0,)), ((), ())), preferred_element_type=F32)


def params(mib):
    return pltpu.CompilerParams(vmem_limit_bytes=mib * MIB)


def cost(flops, moved):
    return pl.CostEstimate(flops=int(flops), bytes_accessed=int(moved), transcendentals=0)


def whole(shape):
    return pl.BlockSpec(shape, lambda *_: (0,) * len(shape))


def with_place(grid, in_specs, out_specs, scratch_shapes=()):
    return pltpu.PrefetchScalarGridSpec(
        num_scalar_prefetch=1,
        grid=grid,
        in_specs=in_specs,
        out_specs=out_specs,
        scratch_shapes=scratch_shapes,
    )


def time_features(flow_values, model_width):
    half_size = model_width // 2
    frequency = jnp.exp(-math.log(10000.0) * jnp.arange(half_size, dtype=F32) / half_size)
    angles = 1000.0 * flow_values[:, None] * frequency[None, :]
    return jax.nn.silu(jnp.concatenate([jnp.sin(angles), jnp.cos(angles)], axis=-1))


def rotary_tables(positions, heads):
    half = DH // 2
    frequency = jnp.exp(-math.log(10000.0) * jnp.arange(half, dtype=F32) / half)
    angles = positions.astype(F32)[:, None] * frequency[None, :]
    cosine, sine = jnp.cos(angles), jnp.sin(angles)
    return (
        jnp.concatenate([cosine, cosine] * heads, axis=-1),
        jnp.concatenate([-sine, sine] * heads, axis=-1),
    )


def swap_halves(values):
    width = values.shape[1]
    half = DH // 2
    if width == DH:
        return jnp.concatenate([values[:, half:], values[:, :half]], axis=1)
    lane = lax.broadcasted_iota(jnp.int32, (1, width), 1)
    first = (lane % DH) < half
    return jnp.where(
        first, pltpu.roll(values, width - half, 1), pltpu.roll(values, half, 1)
    )


def normalise(values):
    centre = values - jnp.mean(values, axis=-1, keepdims=True)
    spread = jnp.mean(centre * centre, axis=-1, keepdims=True)
    inverse = lax.rsqrt(spread + 1e-06)
    return centre * inverse, inverse


def norm_back(normal, inverse, scaled):
    return inverse * (
        scaled
        - jnp.mean(scaled, axis=-1, keepdims=True)
        - normal * jnp.mean(scaled * normal, axis=-1, keepdims=True)
    )


def gelu_and_slope(u):
    root = math.sqrt(2.0 / math.pi)
    square = u * u
    t = jnp.tanh(root * u * (1.0 + 0.044715 * square))
    half = 0.5 * (1.0 + t)
    slope = half + 0.5 * u * (1.0 - t * t) * (root * (1.0 + 3.0 * 0.044715 * square))
    return u * half, slope


def learning_rates():
    fans = (2 * D, D, D // 16, D, FF, D // 8)
    return tuple((2.0 * fan_value ** (-0.5) for fan_value in fans))


def adamw_step(state, gradient, rate):
    master, first_moment, second_moment = (state[0], state[1], state[2])
    first_moment = 0.5 * first_moment + 0.5 * gradient
    second_moment = 0.5 * second_moment + 0.5 * gradient * gradient
    correction = 1.0 - 0.5**STEP
    master = master - rate * (
        first_moment / correction / (jnp.sqrt(second_moment / correction) + 1e-08) + 0.01 * master
    )
    return (master, jnp.stack([first_moment, second_moment]))


def stack_rows(packed_ref, out_ref, owned):
    cols = out_ref.shape[1]
    pieces = packed_ref.shape[1] // cols
    for r in range(packed_ref.shape[0] // owned):
        for q in range(pieces):
            at = (r * pieces + q) * owned
            out_ref[at : at + owned] = packed_ref[
                r * owned : (r + 1) * owned, q * cols : (q + 1) * cols
            ]


def skip_kernel(
    owned, fr_ref, sk_ref, cond_ref, packed_ref, mod_ref, hidden_ref, normed_ref, w_ref
):
    @pl.when(pl.program_id(0) == 0)
    def _():
        stack_rows(packed_ref, w_ref, owned)

    width = fr_ref.shape[1]
    hidden = (
        dot_nn(fr_ref[...], w_ref[:width])
        + dot_nn(sk_ref[...], w_ref[width:])
        + cond_ref[...].astype(F32)
    )
    hidden_ref[...] = hidden
    normal, _ = normalise(hidden)
    normed_ref[...] = (normal * (1.0 + mod_ref[1:2]) + mod_ref[0:1]).astype(BF)


def skip_weight(weight, owned, width):
    if owned % 16 == 0:
        return weight, pl.BlockSpec((width, 2 * width), lambda *_: (0, 0)), owned
    full = stacked(weight[:, : 2 * width], owned, width)
    return full, whole(full.shape), 2 * width


def skip_forward(frames, skips, cond, weight, mod, owned):
    rows, width = frames.shape
    block = min(256, rows)
    row_spec = pl.BlockSpec((block, width), lambda i: (i, 0))
    weight, weight_spec, piece = skip_weight(weight, owned, width)
    return pl.pallas_call(
        functools.partial(skip_kernel, piece),
        grid=(rows // block,),
        in_specs=[row_spec, row_spec, row_spec, weight_spec, whole(mod.shape)],
        out_specs=[row_spec, row_spec],
        out_shape=[
            jax.ShapeDtypeStruct((rows, width), F32),
            jax.ShapeDtypeStruct((rows, width), BF),
        ],
        scratch_shapes=[pltpu.VMEM((2 * width, width), BF)],
        compiler_params=params(60),
        cost_estimate=cost(4 * rows * width * width, 12 * rows * width + 4 * width * width),
    )(frames, skips, cond, weight, mod)


def qkv_kernel(stride, me_ref, x_ref, wq_ref, wk_ref, wv_ref, cos_ref, sin_ref, *refs):
    out_refs, w_ref = refs[:-1], refs[-1]
    size = 128 * stride
    for part, ref in enumerate((wq_ref, wk_ref, wv_ref)):
        w_ref[:, part * size : (part + 1) * size] = ref[...]
    packed = dot_nn(x_ref[...], w_ref[...])
    cosine, sine = cos_ref[...], sin_ref[...]
    turned = []
    for at in range(0, 2 * size, 128):
        raw = packed[:, at : at + 128]
        turned.append((raw * cosine + swap_halves(raw) * sine).astype(BF))
    value = packed[:, 2 * size :].astype(BF)
    groups = len(out_refs) // stride
    for d in range(groups):

        @pl.when(pl.program_id(0) == d)
        def _(d=d):
            for c in range(stride):
                out_ref = out_refs[c * groups + d]
                out_ref[:, 0:128] = turned[c]
                out_ref[:, 128:256] = turned[stride + c]
                out_ref[:, 256:384] = value[:, c * 128 : (c + 1) * 128]


def qkv_forward(normed, weight, cosine, sine, stride, me):
    rows, width = normed.shape
    size = 128 * stride
    groups = width // size

    def columns(part):
        return pl.BlockSpec(
            (width, size),
            lambda i, me: (0, (2 + part) * groups + lax.bitwise_xor(i, me[0])),
        )

    outs = pl.pallas_call(
        functools.partial(qkv_kernel, stride),
        grid_spec=with_place(
            (groups,),
            [
                whole(normed.shape),
                columns(0),
                columns(1),
                columns(2),
                whole(cosine.shape),
                whole(sine.shape),
            ],
            [whole((rows, 384))] * (groups * stride),
            [pltpu.VMEM((width, 3 * size), BF)],
        ),
        out_shape=[jax.ShapeDtypeStruct((rows, 384), BF)] * (groups * stride),
        compiler_params=params(60),
        cost_estimate=cost(6 * rows * width * width, 8 * rows * width + 6 * width * width),
    )(me, normed, weight, weight, weight, cosine, sine)
    return [outs[c * groups : (c + 1) * groups] for c in range(stride)]


def attend_kernel(heads, block, count, *refs):
    piece_refs, out_refs = refs[:count], refs[count : 2 * count]
    log_ref, qkv_ref = refs[2 * count :]
    width = heads * DH
    rows = piece_refs[0].shape[0]
    i = pl.program_id(0)

    @pl.when(i == 0)
    def _():
        for d, ref in enumerate(piece_refs):
            qkv_ref[d * rows : (d + 1) * rows] = ref[...]

    q = qkv_ref[pl.ds(pl.multiple_of(i * block, block), block), 0:width]
    k = qkv_ref[:, width : 2 * width]
    v = qkv_ref[:, 2 * width : 3 * width]
    lane = lax.broadcasted_iota(jnp.int32, (1, width), 1) // DH
    outs = []
    for h in range(heads):
        own = jnp.where(lane == h, q, jnp.zeros_like(q)) if heads > 1 else q
        scores = dot_nt(k, own) * (0.125 * LOG2E)
        top = jnp.max(scores, axis=0, keepdims=True)
        probs = jnp.exp2(scores - top)
        total = jnp.sum(probs, axis=0, keepdims=True)
        outs.append(dot_tn(v[:, h * DH : (h + 1) * DH], probs.astype(BF)) * (1.0 / total))
        log_ref[h : h + 1, :] = top + jnp.log2(total)
    out = (jnp.concatenate(outs, axis=0) if heads > 1 else outs[0]).T.astype(BF)
    per = block // rows
    for d, out_ref in enumerate(out_refs):

        @pl.when(i == d // per)
        def _(d=d, out_ref=out_ref):
            out_ref[...] = out[(d % per) * rows : (d % per + 1) * rows]


def attend(pieces, heads):
    count, rows = len(pieces), pieces[0].shape[0]
    length = count * rows
    width = heads * DH
    block = min(512, length)
    outs = pl.pallas_call(
        functools.partial(attend_kernel, heads, block, count),
        grid=(length // block,),
        in_specs=[whole(p.shape) for p in pieces],
        out_specs=[whole((rows, width))] * count
        + [pl.BlockSpec((heads, block), lambda i: (0, i))],
        out_shape=[jax.ShapeDtypeStruct((rows, width), BF)] * count
        + [jax.ShapeDtypeStruct((heads, length), F32)],
        scratch_shapes=[pltpu.VMEM((length, 3 * width), BF)],
        compiler_params=params(60),
        cost_estimate=cost(16 * length * length * DH * heads, 8 * length * width),
    )(*pieces)
    return outs[:count], outs[count]


def attend_back_kernel(heads, block, count, *refs):
    piece_refs, do_refs, o_refs = refs[:count], refs[count : 2 * count], refs[2 * count : 3 * count]
    log_ref, cos_ref, sin_ref = refs[3 * count : 3 * count + 3]
    out_refs = refs[3 * count + 3 : 4 * count + 3]
    qkv_ref, do_ref, dq_sum, delta = refs[4 * count + 3 :]
    width = heads * DH
    rows = piece_refs[0].shape[0]
    i = pl.program_id(0)
    lane = lax.broadcasted_iota(jnp.int32, (1, width), 1) // DH

    @pl.when(i == 0)
    def _():
        dq_sum[...] = jnp.zeros_like(dq_sum)
        for d in range(count):
            at = slice(d * rows, (d + 1) * rows)
            qkv_ref[at] = piece_refs[d][...]
            do_own = do_refs[d][...]
            do_ref[at] = do_own
            product = (do_own.astype(F32) * o_refs[d][...].astype(F32)).T
            for h in range(heads):
                delta[h : h + 1, at] = jnp.sum(
                    product[h * DH : (h + 1) * DH], axis=0, keepdims=True
                )

    here = pl.ds(pl.multiple_of(i * block, block), block)
    q = qkv_ref[:, 0:width]
    k = qkv_ref[here, width : 2 * width]
    v = qkv_ref[here, 2 * width : 3 * width]
    do = do_ref[...]
    k_turned = k.T
    dk = dv = None
    for h in range(heads):
        own = lane == h
        k_own = jnp.where(own, k, jnp.zeros_like(k)) if heads > 1 else k
        v_own = jnp.where(own, v, jnp.zeros_like(v)) if heads > 1 else v
        scores = dot_nt(k_own, q) * (0.125 * LOG2E)
        probs = jnp.exp2(scores - log_ref[h : h + 1, :])
        prob_grad = dot_nt(v_own, do)
        score_grad = (probs * (prob_grad - delta[h : h + 1, :])).astype(BF)
        part = slice(h * DH, (h + 1) * DH)
        dq_sum[part, :] += dot_nn(k_turned[part], score_grad)
        dv_own = dot_nn(probs.astype(BF), do)
        dk_own = dot_nn(score_grad, q)
        dv = dv_own if dv is None else jnp.where(own, dv_own, dv)
        dk = dk_own if dk is None else jnp.where(own, dk_own, dk)
    dk = dk * 0.125
    dk = (dk * cos_ref[here, :] - swap_halves(dk) * sin_ref[here, :]).astype(BF)
    dv = dv.astype(BF)
    per = block // rows
    for d, out_ref in enumerate(out_refs):

        @pl.when(i == d // per)
        def _(d=d, out_ref=out_ref):
            at = slice((d % per) * rows, (d % per + 1) * rows)
            out_ref[:, width : 2 * width] = dk[at]
            out_ref[:, 2 * width : 3 * width] = dv[at]

    @pl.when(i == pl.num_programs(0) - 1)
    def _():
        dq = (dq_sum[...] * 0.125).T
        dq = (dq * cos_ref[...] - swap_halves(dq) * sin_ref[...]).astype(BF)
        for d, out_ref in enumerate(out_refs):
            out_ref[:, 0:width] = dq[d * rows : (d + 1) * rows]


def attend_back(pieces, do, chunk, o, log_total, cosine, sine, heads):
    count, rows = len(pieces), pieces[0].shape[0]
    length = count * rows
    width = heads * DH
    block = min(512, length)
    operands = (*pieces, *do, *o, log_total, cosine, sine)
    return pl.pallas_call(
        functools.partial(attend_back_kernel, heads, block, count),
        grid=(length // block,),
        in_specs=[whole(p.shape) for p in pieces]
        + [pl.BlockSpec((rows, width), lambda i: (0, chunk))] * count
        + [whole(a.shape) for a in operands[2 * count :]],
        out_specs=[whole((rows, 3 * width))] * count,
        out_shape=[jax.ShapeDtypeStruct((rows, 3 * width), BF)] * count,
        scratch_shapes=[
            pltpu.VMEM((length, 3 * width), BF),
            pltpu.VMEM((length, width), BF),
            pltpu.VMEM((width, length), F32),
            pltpu.VMEM((heads, length), F32),
        ],
        compiler_params=params(60),
        cost_estimate=cost(24 * length * length * DH * heads, 20 * length * width),
    )(*operands)


def pieces_at(me_ref, count, groups, width, part=0, parts_width=0):
    for c in range(count):
        for d in range(groups):
            at = (lax.bitwise_xor(me_ref[0], d) * count + c) * width + part * parts_width
            yield c, d, pl.ds(pl.multiple_of(at, 128), width)


def out_kernel(count, groups, me_ref, *refs):
    o_refs = refs[: count * groups]
    w_ref, hidden_ref, mod_ref, attended_ref, branch_ref, middle_ref, normed_ref = refs[
        count * groups :
    ]
    for c, d, columns in pieces_at(me_ref, count, groups, o_refs[0].shape[1]):
        attended_ref[:, columns] = o_refs[c * groups + d][...]
    branch = dot_nn(attended_ref[...], w_ref[...])
    branch_ref[...] = branch
    middle = hidden_ref[...] + mod_ref[2:3] * branch
    middle_ref[...] = middle
    normal, _ = normalise(middle)
    normed_ref[...] = (normal * (1.0 + mod_ref[4:5]) + mod_ref[3:4]).astype(BF)


def out_forward(chunks, weight, hidden, mod, at, me):
    rows, width = hidden.shape
    block = min(256, rows)
    row_spec = pl.BlockSpec((block, width), lambda i, *_: (i, 0))
    count, groups = len(chunks), len(chunks[0])
    o_spec = pl.BlockSpec((block, chunks[0][0].shape[1]), lambda i, *_: (i, 0))
    return pl.pallas_call(
        functools.partial(out_kernel, count, groups),
        grid_spec=with_place(
            (rows // block,),
            [o_spec] * (count * groups)
            + [pl.BlockSpec((width, width), lambda *_: (0, at)), row_spec, whole(mod.shape)],
            [row_spec] * 4,
        ),
        out_shape=[
            jax.ShapeDtypeStruct((rows, width), BF),
            jax.ShapeDtypeStruct((rows, width), F32),
            jax.ShapeDtypeStruct((rows, width), F32),
            jax.ShapeDtypeStruct((rows, width), BF),
        ],
        compiler_params=params(60),
        cost_estimate=cost(2 * rows * width * width, 18 * rows * width + 2 * width * width),
    )(me, *[piece for chunk in chunks for piece in chunk], weight, hidden, mod)


def ffn_kernel(
    owned, x_ref, dc_ref, up_ref, packed_ref, y_ref, dx_ref, activated_ref, up_cot_ref, dn_ref
):
    @pl.when(pl.program_id(0) == 0)
    def _():
        y_ref[...] = jnp.zeros_like(y_ref)
        dx_ref[...] = jnp.zeros_like(dx_ref)

    stack_rows(packed_ref, dn_ref, owned)
    up, dn = up_ref[...], dn_ref[...]
    value, slope = gelu_and_slope(dot_nn(x_ref[...], up))
    activated = value.astype(BF)
    up_cot = (dot_nt(dc_ref[...], dn) * slope).astype(BF)
    activated_ref[...] = activated
    up_cot_ref[...] = up_cot
    y_ref[...] += dot_nn(activated, dn)
    dx_ref[...] += dot_nt(up_cot, up)


def ffn_grad_kernel(
    owned, x_ref, dc_ref, activated_ref, up_cot_ref, grads_ref, x_turned, gu, gd, sems
):
    i, last = pl.program_id(0), pl.num_programs(0) - 1
    slot = lax.rem(i, 2)
    block = up_cot_ref.shape[1]
    part = gd.shape[1]
    pieces = block // part

    def sends(step, at):
        across = pl.ds(pl.multiple_of(step * block, block), block)
        down = pl.ds(pl.multiple_of(step * part, part), part)
        half = grads_ref.shape[1] // 2
        return (
            pltpu.make_async_copy(gu.at[at], grads_ref.at[:, across], sems.at[0, at]),
            pltpu.make_async_copy(gd.at[at], grads_ref.at[down, pl.ds(half, half)], sems.at[1, at]),
        )

    @pl.when(i == 0)
    def _():
        x_turned[...] = x_ref[...].T

    @pl.when(i >= 2)
    def _():
        for copy in sends(i - 2, slot):
            copy.wait()

    dc = dc_ref[...]
    gu[slot] = dot_nn(x_turned[...], up_cot_ref[...]).astype(BF)
    down_grad = dot_tn(activated_ref[...], dc).astype(BF)
    width = dc.shape[1]
    for r in range(part // owned):
        for q in range(pieces):
            at = (r * pieces + q) * owned
            gd[slot, r * owned : (r + 1) * owned, q * width : (q + 1) * width] = down_grad[
                at : at + owned
            ]
    for copy in sends(i, slot):
        copy.start()

    @pl.when(i == last)
    def _():
        for copy in sends(last - 1, 1 - slot) + sends(last, slot):
            copy.wait()


FFN_BLOCK = 512


def ffn(x, dc, weights, owned):
    rows, width = x.shape
    hidden_width = FF
    pieces = hidden_width // width
    block = FFN_BLOCK
    steps = hidden_width // block
    part = block // pieces
    packed, piece = weights, owned
    if owned % 16:
        full = stacked(weights[:, :hidden_width], owned, width)
        packed, piece = side_by_side_blocks(full, part, pieces), part
    across = pl.BlockSpec((rows, block), lambda i: (0, i))
    return pl.pallas_call(
        functools.partial(ffn_kernel, piece),
        grid=(steps,),
        in_specs=[
            whole(x.shape),
            whole(x.shape),
            pl.BlockSpec((width, block), lambda i: (0, steps + i)),
            pl.BlockSpec((part, hidden_width), lambda i: (i, 0)),
        ],
        out_specs=[whole(x.shape), whole(x.shape), across, across],
        out_shape=[
            jax.ShapeDtypeStruct((rows, width), F32),
            jax.ShapeDtypeStruct((rows, width), F32),
            jax.ShapeDtypeStruct((rows, hidden_width), BF),
            jax.ShapeDtypeStruct((rows, hidden_width), BF),
        ],
        scratch_shapes=[pltpu.VMEM((block, width), BF)],
        compiler_params=params(60),
        cost_estimate=cost(8 * rows * width * hidden_width, 8 * width * hidden_width),
    )(x, dc, weights, packed)


def ffn_grad(x, dc, activated, up_cot, owned):
    rows, width = x.shape
    hidden_width = activated.shape[1]
    pieces = hidden_width // width
    block = FFN_BLOCK
    part = block // pieces
    across = pl.BlockSpec((rows, block), lambda i: (0, i))
    grads = pl.pallas_call(
        functools.partial(ffn_grad_kernel, owned if owned % 16 == 0 else part),
        grid=(hidden_width // block,),
        in_specs=[whole(x.shape), whole(x.shape), across, across],
        out_specs=pl.BlockSpec(memory_space=pl.ANY),
        out_shape=jax.ShapeDtypeStruct((width, 2 * hidden_width), BF),
        scratch_shapes=[
            pltpu.VMEM((width, rows), BF),
            pltpu.VMEM((2, width, block), BF),
            pltpu.VMEM((2, part, hidden_width), BF),
            pltpu.SemaphoreType.DMA((2, 2)),
        ],
        compiler_params=params(60),
        cost_estimate=cost(4 * rows * width * hidden_width, 8 * width * hidden_width),
    )(x, dc, activated, up_cot)
    if owned % 16:
        full = stacked(grads[:, hidden_width:], part, width)
        grads = jnp.concatenate(
            [grads[:, :hidden_width], side_by_side_blocks(full, owned, pieces)], axis=1
        )
    return grads


def mid_kernel(groups, me_ref, *refs):
    y_ref, dx_ref, middle_ref, branch_ref, grad_ref, w_ref, mod_ref = refs[:7]
    block_ref, mgrad_ref, bcot_ref, sums_ref = refs[7:11]
    piece_refs, attended_grad = refs[11:-1], refs[-1]

    @pl.when(pl.program_id(0) == 0)
    def _():
        sums_ref[...] = jnp.zeros_like(sums_ref)

    y, middle, w = y_ref[...], middle_ref[...], dx_ref[...]
    grad = grad_ref[...].astype(F32)
    block_ref[...] = (middle + mod_ref[5:6] * y).astype(BF)
    normal, inverse = normalise(middle)
    middle_grad = grad + norm_back(normal, inverse, w * (1.0 + mod_ref[4:5]))
    mgrad_ref[...] = middle_grad
    branch_cot = (middle_grad * mod_ref[2:3]).astype(BF)
    bcot_ref[...] = branch_cot
    sums_ref[0:1] += jnp.sum(middle_grad * branch_ref[...], axis=0, keepdims=True)
    sums_ref[1:2] += jnp.sum(w, axis=0, keepdims=True)
    sums_ref[2:3] += jnp.sum(w * normal, axis=0, keepdims=True)
    sums_ref[3:4] += jnp.sum(grad * y, axis=0, keepdims=True)
    attended_grad[...] = dot_nt(branch_cot, w_ref[...]).astype(BF)
    for _, d, columns in pieces_at(me_ref, 1, groups, piece_refs[0].shape[1]):
        piece_refs[d][...] = attended_grad[:, columns]


def mid_back(y, dx, middle, branch, grad, weight, mod, at, me, groups):
    rows, width = y.shape
    block = min(256, rows)
    cols = width // groups
    row_spec = pl.BlockSpec((block, width), lambda i, *_: (i, 0))
    piece_spec = pl.BlockSpec((block, cols), lambda i, *_: (i, 0))
    return pl.pallas_call(
        functools.partial(mid_kernel, groups),
        grid_spec=with_place(
            (rows // block,),
            [row_spec] * 5 + [pl.BlockSpec((width, width), lambda *_: (0, at)), whole(mod.shape)],
            [row_spec] * 3 + [whole((8, width))] + [piece_spec] * groups,
            [pltpu.VMEM((block, width), BF)],
        ),
        out_shape=[
            jax.ShapeDtypeStruct((rows, width), BF),
            jax.ShapeDtypeStruct((rows, width), F32),
            jax.ShapeDtypeStruct((rows, width), BF),
            jax.ShapeDtypeStruct((8, width), F32),
        ]
        + [jax.ShapeDtypeStruct((rows, cols), BF)] * groups,
        compiler_params=params(60),
        cost_estimate=cost(2 * rows * width * width, 28 * rows * width + 2 * width * width),
    )(me, y, dx, middle, branch, grad, weight, mod)


def last_kernel(count, groups, owned, me_ref, *refs):
    piece_refs = refs[: count * groups]
    rest = refs[count * groups :]
    hidden_ref, mgrad_ref, wq_ref, wk_ref, wv_ref, packed_ref, mod_ref = rest[:7]
    hgrad_ref, frames_ref, skips_ref, sums_ref, wskip_ref, cot_ref = rest[7:]

    @pl.when(pl.program_id(0) == 0)
    def _():
        sums_ref[...] = jnp.zeros_like(sums_ref)
        stack_rows(packed_ref, wskip_ref, owned)

    width = piece_refs[0].shape[1] // 3
    model = hidden_ref.shape[1]
    for part in range(3):
        for c, d, columns in pieces_at(me_ref, count, groups, width, part, model):
            cot_ref[:, columns] = piece_refs[c * groups + d][
                :, part * width : (part + 1) * width
            ]
    w = (
        dot_nt(cot_ref[:, :model], wq_ref[...])
        + dot_nt(cot_ref[:, model : 2 * model], wk_ref[...])
        + dot_nt(cot_ref[:, 2 * model :], wv_ref[...])
    )
    normal, inverse = normalise(hidden_ref[...])
    sums_ref[0:1] += jnp.sum(w, axis=0, keepdims=True)
    sums_ref[1:2] += jnp.sum(w * normal, axis=0, keepdims=True)
    hidden_grad = (
        mgrad_ref[...] + norm_back(normal, inverse, w * (1.0 + mod_ref[1:2]))
    ).astype(BF)
    hgrad_ref[...] = hidden_grad
    frames_ref[...] = dot_nt(hidden_grad, wskip_ref[:model]).astype(BF)
    skips_ref[...] = dot_nt(hidden_grad, wskip_ref[model:]).astype(BF)


def last_back(chunks, hidden, middle_grad, weights, mod, owned, me):
    rows, width = hidden.shape
    block = min(256, rows)
    row_spec = pl.BlockSpec((block, width), lambda i, *_: (i, 0))
    count, groups = len(chunks), len(chunks[0])
    piece_spec = pl.BlockSpec((block, chunks[0][0].shape[1]), lambda i, *_: (i, 0))
    w_skip, skip_spec, piece = skip_weight(weights, owned, width)

    def part_spec(part):
        return pl.BlockSpec((width, width), lambda *_: (0, 2 + part))

    return pl.pallas_call(
        functools.partial(last_kernel, count, groups, piece),
        grid_spec=with_place(
            (rows // block,),
            [piece_spec] * (count * groups)
            + [row_spec, row_spec, part_spec(0), part_spec(1), part_spec(2)]
            + [skip_spec, whole(mod.shape)],
            [row_spec, row_spec, row_spec, whole((8, width))],
            [pltpu.VMEM((2 * width, width), BF), pltpu.VMEM((block, 3 * width), BF)],
        ),
        out_shape=[
            jax.ShapeDtypeStruct((rows, width), BF),
            jax.ShapeDtypeStruct((rows, width), BF),
            jax.ShapeDtypeStruct((rows, width), BF),
            jax.ShapeDtypeStruct((8, width), F32),
        ],
        compiler_params=params(60),
        cost_estimate=cost(2 * rows * width * width, 4 * rows * width),
    )(
        me,
        *[piece for chunk in chunks for piece in chunk],
        hidden,
        middle_grad,
        weights,
        weights,
        weights,
        w_skip,
        mod,
    )


def out_wgrad_kernel(left_ref, right_ref, out_ref):
    out_ref[...] = dot_tn(left_ref[...], right_ref[...]).astype(BF)


def out_wgrad_part(left, right, columns):
    rows, width = left.shape
    block = 512
    first = columns // block - width // block
    return pl.pallas_call(
        out_wgrad_kernel,
        grid=(width // block,),
        in_specs=[whole(left.shape), pl.BlockSpec((rows, block), lambda i: (0, i))],
        out_specs=pl.BlockSpec((width, block), lambda i: (0, first + i)),
        out_shape=jax.ShapeDtypeStruct((width, columns), BF),
        compiler_params=params(60),
        cost_estimate=cost(2 * rows * width * width, 6 * width * width),
    )(left, right)


def qkv_grad_kernel(groups, me_ref, *refs):
    x_ref, piece_refs = refs[0], refs[1 : 1 + groups]
    out_ref, piece, x_turned = refs[-3:]
    i = pl.program_id(0)

    @pl.when(i == 0)
    def _():
        x_turned[...] = x_ref[...].T

    for d, ref in enumerate(piece_refs):

        @pl.when(i == d)
        def _(ref=ref):
            piece[...] = ref[...]

    out_ref[...] = dot_nn(x_turned[...], piece[...]).astype(BF)


def qkv_grad(normed, pieces, me, held=None):
    groups = len(pieces)
    rows, cols = pieces[0].shape
    width = normed.shape[1]
    given = [] if held is None else [held]
    return pl.pallas_call(
        functools.partial(qkv_grad_kernel, groups),
        grid_spec=with_place(
            (groups,),
            [whole(normed.shape)]
            + [whole((rows, cols))] * groups
            + [pl.BlockSpec(memory_space=pl.ANY)] * len(given),
            pl.BlockSpec((width, cols), lambda i, me: (0, lax.bitwise_xor(i, me[0]))),
            [pltpu.VMEM((rows, cols), BF), pltpu.VMEM((width, rows), BF)],
        ),
        out_shape=jax.ShapeDtypeStruct((width, groups * cols) if held is None else held.shape, BF),
        input_output_aliases={2 + groups: 0} if given else {},
        compiler_params=params(60),
        cost_estimate=cost(rows * width, 1024),
    )(me, normed, *pieces, *given)


def update_kernel(grads_of, rates, *refs):
    count = len(rates)
    outs, states, given = refs[-2 * count :], refs[-3 * count : -2 * count], refs[: -3 * count]
    correction = 1.0 - 0.5**STEP
    for at, rows, cols, gradient in grads_of(*given):
        state, new_ref, moments_ref = states[at], outs[2 * at], outs[2 * at + 1]
        master = state[0, rows, cols]
        first = 0.5 * state[1, rows, cols] + 0.5 * gradient
        second = 0.5 * state[2, rows, cols] + 0.5 * gradient * gradient
        moments_ref[0, rows, cols] = first
        moments_ref[1, rows, cols] = second
        new_ref[rows, cols] = master - rates[at] * (
            first / correction / (jnp.sqrt(second / correction) + 1e-08) + 0.01 * master
        )


def update(grads_of, given, states, rates):
    shapes = []
    for state in states:
        _, rows, cols = state.shape
        shapes += [(rows, cols), (2, rows, cols)]
    moved = 6 * sum(state.size for state in states) * 4 // 3
    return pl.pallas_call(
        functools.partial(update_kernel, grads_of, rates),
        grid=(1,),
        in_specs=[whole(a.shape) for a in (*given, *states)],
        out_specs=[whole(shape) for shape in shapes],
        out_shape=[jax.ShapeDtypeStruct(shape, F32) for shape in shapes],
        compiler_params=params(60),
        cost_estimate=cost(moved, moved),
    )(*given, *states)


def skip_grads(*refs):
    half = refs[0].shape[1]
    for side in range(2):
        rest, arrived = refs[2 * side][...], refs[2 * side + 1][...]
        yield 0, slice(None), slice(side * half, (side + 1) * half), rest + arrived.astype(F32)


def ffn_grads(rest_ref, arrived_ref):
    owned, cols = rest_ref.shape
    hidden_width, width = cols // 2, D
    for q in range(cols // width):
        at = slice(q * width, (q + 1) * width)
        gradient = rest_ref[:, at] + arrived_ref[:, at].astype(F32)
        if q * width < hidden_width:
            yield 0, slice(None), at, gradient
        else:
            r = q - hidden_width // width
            yield 1, slice(r * owned, (r + 1) * owned), slice(None), gradient


def attention_columns(count, groups):
    cols = D // (count * groups)
    for c in range(count):
        for j in range(groups):
            for part in range(3):
                yield 0, part * D + (j * count + c) * cols, cols
        if c == 0:
            yield 1, 0, D


def attention_grads(count, groups, rest_ref, arrived_ref):
    at = 0
    for weight, to, cols in attention_columns(count, groups):
        here = slice(at, at + cols)
        gradient = rest_ref[:, here] + arrived_ref[:, here].astype(F32)
        yield weight, slice(None), slice(to, to + cols), gradient
        at += cols


def modulation_grads(time_ref, cots_ref):
    for at in range(0, cots_ref.shape[1], D):
        gradient = lax.dot_general(
            time_ref[...],
            cots_ref[:, at : at + D],
            (((0,), (0,)), ((), ())),
            precision=highest,
            preferred_element_type=F32,
        )
        yield 0, slice(None), slice(at, at + D), gradient


def bits_of(axis):
    size = lax.axis_size(axis)
    return [(axis, b) for b in reversed(range(size.bit_length() - 1))]


def my_bit(level):
    axis, bit = level
    return (lax.axis_index(axis) >> bit) & 1


def swap(values, level):
    axis, bit = level
    return lax.ppermute(values, axis, [(i, i ^ (1 << bit)) for i in range(lax.axis_size(axis))])


def after(values, *others):
    return lax.optimization_barrier((values, *others))[0]


class ModulationCots:
    def __init__(self, own):
        self.own, self.order = own, bits_of("seq")[::-1] + bits_of("dp")[::-1]
        self.arrived = None

    def settle(self, *waits):
        if self.arrived is None:
            return
        level, other = self.arrived
        other = after(other, *waits) if waits else other
        if level[0] == "seq":
            self.own = self.own + other
        else:
            self.own = jnp.where(
                my_bit(level) == 0,
                jnp.concatenate([self.own, other], axis=0),
                jnp.concatenate([other, self.own], axis=0),
            )
        self.arrived = None

    def step(self, *waits):
        self.settle(*waits)
        level = self.order.pop(0)
        self.arrived = (level, swap(self.own, level))


class ScatterSum:
    def __init__(self, grad, order, dims):
        self.dims, self.order = list(dims), list(order)
        rows, cols = grad.shape
        split = [2] * len(self.dims)
        self.terms = [grad.reshape(split + [rows // 2 ** len(split), cols])]

    def hold(self, *waits):
        if waits:
            self.terms[-1] = after(self.terms[-1], *waits)

    def step(self, *waits, late=()):
        self.hold(*waits)
        level = self.order.pop(0)
        at, mine = self.dims.index(level), my_bit(level)
        self.dims.pop(at)

        def halves(side):
            return [lax.dynamic_index_in_dim(t, side, at, keepdims=False) for t in self.terms]

        leaving = halves(1 - mine)
        total = leaving[0]
        if len(leaving) > 1:
            total = sum(t.astype(F32) for t in leaving).astype(total.dtype)
        total = after(total, *late) if late else total
        self.sent = total
        arrived = swap(total, level)
        self.terms = halves(mine) + [arrived]
        return arrived

    def ends(self):
        return [sum(t.astype(F32) for t in self.terms[:-1]), self.terms[-1]]


def exchange(pieces):
    places = range(len(pieces))
    return [pieces[0]] + [
        lax.ppermute(pieces[d], "seq", [(i, i ^ d) for i in places]) for d in places[1:]
    ]


def dot_tn_exact(left, right):
    return lax.dot_general(
        left,
        right,
        (((0,), (0,)), ((), ())),
        precision=highest,
        preferred_element_type=F32,
    )


def attention_total(total, count, groups):
    runs, at = ([], []), 0
    for weight, to, cols in attention_columns(count, groups):
        runs[weight].append((to, total[:, at : at + cols]))
        at += cols
    return [jnp.concatenate([v for _, v in sorted(r, key=lambda v: v[0])], axis=1) for r in runs]


def in_order(pieces, me, parts):
    groups, rows = len(pieces), pieces[0].shape[0]
    stack = jnp.take(jnp.stack(pieces), jnp.arange(groups) ^ me[0], axis=0)
    return stack.reshape(groups, rows, parts, -1).transpose(1, 2, 0, 3).reshape(rows, -1)


def by_place(values, me, groups):
    parts = jnp.split(values, groups, axis=1)
    stack = jnp.take(jnp.stack(parts), jnp.arange(groups) ^ me[0], axis=0)
    return [stack[d] for d in range(groups)]


def modulation_rows(partial, order, wait):
    dims = bits_of("dp")
    count, cols = partial.shape
    held = partial.reshape([2] * len(dims) + [count // 2 ** len(dims), cols])
    for level in order:
        at, mine = dims.index(level), my_bit(level)
        dims.pop(at)
        leaving = lax.dynamic_index_in_dim(held, 1 - mine, at, keepdims=False)
        held = lax.dynamic_index_in_dim(held, mine, at, keepdims=False) + swap(leaving, level)
    held = after(held, wait)
    for level in bits_of("seq"):
        held = held + swap(held, level)
    return held


def side_by_side(own, rows):
    return jnp.concatenate(jnp.split(own, own.shape[0] // rows, axis=0), axis=1)


def stacked(full, rows, cols):
    pieces = full.shape[1] // cols
    blocks = full.reshape(full.shape[0] // rows, rows, pieces, cols)
    return blocks.transpose(0, 2, 1, 3).reshape(full.shape[0] * pieces, cols)


def side_by_side_blocks(full, rows, pieces):
    cols = full.shape[1]
    blocks = full.reshape(full.shape[0] // (rows * pieces), pieces, rows, cols)
    return blocks.transpose(0, 2, 1, 3).reshape(full.shape[0] // pieces, pieces * cols)


def gather_pairwise(own, order, last_waits=(), last_use=()):
    rows, cols = own.shape
    held, bits = own.reshape(1, rows, cols), []
    for level in order:
        last = len(bits) == len(order) - 1
        if last and last_waits:
            held = after(held, *last_waits)
        other = swap(held, level)
        if last and last_use:
            other = after(other, *last_use)
        at = sum(1 for bit in bits if bit > level[1])
        bits.append(level[1])
        shape = [2] * (len(bits) - 1)
        own_part = held.reshape(shape + [rows, cols])
        other_part = other.reshape(shape + [rows, cols])
        held = jnp.where(
            my_bit(level) == 0,
            jnp.stack([own_part, other_part], axis=at),
            jnp.stack([other_part, own_part], axis=at),
        ).reshape(2 ** len(bits), rows, cols)
    return held.reshape(-1, cols)


def per_device(
    frames_in,
    skip_in,
    condition,
    flow_time,
    span_start,
    span_length,
    out_grad,
    skip_proj_state,
    attn_qkv_state,
    attn_out_state,
    ffn_up_state,
    ffn_down_state,
    ada_mod_state,
):
    utter_count, rows, width = frames_in.shape
    seq = lax.axis_size("seq")
    everyone = ("dp", "seq")
    owned = attn_qkv_state.shape[1]
    hidden_width = ffn_up_state.shape[2]
    length = rows * seq
    me = lax.axis_index(everyone)
    positions = lax.axis_index("seq") * rows + jnp.arange(rows, dtype=jnp.int32)

    group_heads = HEADS // seq
    heads = min(2, group_heads)
    count = group_heads // heads

    first_own = jnp.concatenate(
        [side_by_side(skip_proj_state[0].astype(BF), owned), attn_qkv_state[0].astype(BF)],
        axis=1,
    )
    first_part = gather_pairwise(first_own, bits_of("seq"))
    first_full = lax.all_gather(first_part, "dp", axis=0, tiled=True)
    out_at = 2 * hidden_width // width

    dp_bits, seq_bits = bits_of("dp"), bits_of("seq")
    core, planes = dp_bits[-1], dp_bits[:-1]

    time_code = time_features(flow_time, width).astype(BF)
    time_own = lax.dynamic_slice_in_dim(time_code, me * owned, owned, 1)
    mod_part = jnp.dot(time_own, ada_mod_state[0].astype(BF), preferred_element_type=F32)
    modulation = modulation_rows(mod_part, [core] + planes, first_part)

    place = lax.axis_index("seq").astype(jnp.int32).reshape(1)
    frame = jnp.arange(length, dtype=jnp.int32)
    frame = ((frame // rows) ^ place) * rows + frame % rows
    cos_all, sin_all = rotary_tables(frame, heads)
    wide = heads == 2
    cos_own, sin_own = rotary_tables(positions, 2)
    span_stop = span_start + span_length

    outs = []
    assert utter_count == 1
    mod = modulation.reshape(6, width)
    inside = (positions >= span_start[0]) & (positions < span_stop[0])
    frames, skips = frames_in[0], skip_in[0]
    cond = jnp.where(inside[:, None], jnp.zeros_like(condition[0]), condition[0])
    grad = jnp.where(inside[:, None], out_grad[0], jnp.zeros_like(out_grad[0]))
    down_cot = (grad.astype(F32) * mod[5:6]).astype(BF)

    hidden, normed = skip_forward(frames, skips, cond, first_full, mod, owned)
    if wide:
        packed = qkv_forward(normed, first_full, cos_own, sin_own, count, place)
    else:
        (pairs,) = qkv_forward(normed, first_full, cos_own, sin_own, 1, 0 * place)
        split = jnp.concatenate(
            [p.reshape(rows, 3, 2, DH).transpose(0, 2, 1, 3).reshape(rows, -1) for p in pairs],
            axis=1,
        )
        packed = [by_place(split, place, seq)]
    arrived = [exchange(part) for part in packed]
    second_own = jnp.concatenate(
        [
            side_by_side(ffn_down_state[0].astype(BF), owned),
            ffn_up_state[0].astype(BF),
            attn_out_state[0].astype(BF),
        ],
        axis=1,
    )
    early = (cos_all, sin_all, cos_own, sin_own, cond, grad, down_cot)
    second_own = gather_pairwise(after(second_own, modulation), seq_bits, early, (normed,))
    second_full = lax.all_gather(second_own, "dp", axis=0, tiled=True)
    qkv_chunks, attended = [], []
    for pieces in arrived:
        waits = attended[-1][0][:1] if attended else [second_own]
        pieces[1:] = [after(piece, *waits) for piece in pieces[1:]]
        qkv_chunks.append(pieces)
        attended.append(attend(pieces, heads))
    o_chunks = []
    for c, (o, _) in enumerate(attended):
        pieces = exchange(o)
        if c < count - 1:
            pieces[1:] = [after(piece, attended[c + 1][0][0]) for piece in pieces[1:]]
        o_chunks.append(pieces)
    here = place
    if not wide:
        o_chunks, here = [[in_order(o_chunks[0], place, 1)]], 0 * place

    attended_low, branch, middle, normed_two = out_forward(
        o_chunks, second_full, hidden, mod, out_at, here
    )
    downward, normed_two_grad, *ffn_kept = ffn(normed_two, down_cot, second_full, owned)
    mid = mid_back(
        downward,
        normed_two_grad,
        middle,
        branch,
        grad,
        second_full,
        mod,
        out_at,
        here,
        seq if wide else 1,
    )
    do_pieces = exchange(mid[4:] if wide else by_place(mid[4], place, seq))
    block_out, middle_grad, branch_cot, mid_sums = mid[:4]
    every_bit = dp_bits + seq_bits
    rising = seq_bits[::-1]
    columns = 3 * width // count + width
    qkv_part = out_wgrad_part(attended_low, branch_cot, columns) if wide else mid[4]
    ffn_whole = ffn_grad(after(normed_two, qkv_part), down_cot, *ffn_kept, owned)
    ffn_whole = after(ffn_whole, *do_pieces[1:])
    ffn_part = lax.psum_scatter(ffn_whole, "dp", scatter_dimension=0, tiled=True)
    do_pieces[1:] = [after(piece, ffn_whole) for piece in do_pieces[1:]]
    backs = []
    for c in range(count):
        o, log_total = attended[c]
        backs.append(
            attend_back(qkv_chunks[c], do_pieces, c, o, log_total, cos_all, sin_all, heads)
        )
    cot_chunks = [exchange(b) for b in backs]

    sent = [backs[-1][0]]

    def leave(part):
        part.step(sent[-1])
        sent.append(part.sent)

    def wait_in_turn(pieces):
        return pieces[:1] + [after(piece, sent[-1]) for piece in pieces[1:]]

    def full_sum(grad_part, planes_first):
        return ScatterSum(grad_part, [core] + planes_first, every_bit)

    qkv_sums = []
    for c in range(count):
        pieces = cot_chunks[c] = wait_in_turn(cot_chunks[c])
        if not wide:
            cot_chunks = [[in_order(pieces, place, 3)]]
            qkv_part = jnp.concatenate(
                [dot_tn(normed, cot_chunks[0][0]), dot_tn(attended_low, branch_cot)], axis=1
            ).astype(BF)
        else:
            qkv_part = qkv_grad(normed, pieces, place, None if c else qkv_part)
        qkv_sums.append(full_sum(qkv_part, planes[::-1]))
        leave(qkv_sums[-1])
        if c < count - 1:
            leave(qkv_sums[-1])
    ffn_sum = ScatterSum(ffn_part, rising, seq_bits)
    ffn_sum.step(late=(cot_chunks[-1][-1],))
    sent.append(ffn_sum.sent)
    for part in qkv_sums:
        leave(part)
    cot_chunks[-1] = [after(piece, sent[-1]) for piece in cot_chunks[-1]]
    hidden_grad, frames_grad, skip_grad, last_sums = last_back(
        cot_chunks, hidden, middle_grad, first_full, mod, owned, here
    )
    skip_cot = after(hidden_grad, *[part.terms[-1] for part in qkv_sums])
    skip_part = jnp.concatenate(
        [dot_tn(frames, skip_cot).astype(BF), dot_tn(skips, skip_cot).astype(BF)], axis=0
    )
    skip_part = after(skip_part, ffn_sum.terms[-1])
    half = width // 2
    skip_sums = [
        ScatterSum(skip_part[:, :half], [core] + planes[::-1] + rising, every_bit),
        ScatterSum(skip_part[:, half:], [core] + planes + rising, every_bit),
    ]
    mod_cot = jnp.concatenate(
        [last_sums[0], last_sums[1], mid_sums[0], mid_sums[1], mid_sums[2], mid_sums[3]]
    ).reshape(1, 6 * width)
    mod_cots = ModulationCots(mod_cot)
    time_rows = time_own.astype(F32)
    qkv_sum, marks = None, []
    rows_held = owned * seq
    for part in [ffn_sum] + qkv_sums:
        part.hold(hidden_grad)
    mod_cots.step()
    while skip_sums[0].order or qkv_sum is None or qkv_sum.order:
        for part in skip_sums:
            if part.order:
                leave(part)
        marks.append(sent[-1])
        if mod_cots.order:
            mod_cots.step(sent[-1])
        later = [part for part in qkv_sums if part.order]
        for part in later + ([ffn_sum] if ffn_sum.order else []):
            leave(part)
        if qkv_sum is not None and qkv_sum.order and len(marks) > 3:
            leave(qkv_sum)
        if not later and qkv_sum is None:
            for part in qkv_sums:
                part.hold(sent[-1])
            qkv_done = [sum(p.ends()).astype(BF).reshape(rows_held, -1) for p in qkv_sums]
            qkv_sum = ScatterSum(jnp.concatenate(qkv_done, axis=1), rising, seq_bits)
            leave(qkv_sum)
    while ffn_sum.order:
        leave(ffn_sum)
    while mod_cots.order:
        mod_cots.step()
    mod_cots.settle(marks[-1])
    mod_cots = mod_cots.own
    ffn_sum.hold(marks[-3])

    rates = learning_rates()
    outs = [block_out[None], frames_grad[None], skip_grad[None]]
    if owned % 16:
        ffn_total, qkv_total = sum(ffn_sum.ends()), sum(qkv_sum.ends())
        skip_total = jnp.concatenate([sum(part.ends()) for part in skip_sums], axis=1)
        mod_total = dot_tn_exact(time_rows, mod_cots)
        qkv_total, out_total = attention_total(
            qkv_total, count if wide else 1, seq if wide else 1
        )
        grads = (
            skip_total.reshape(2 * owned, width),
            qkv_total,
            out_total,
            ffn_total[:, :hidden_width],
            stacked(ffn_total[:, hidden_width:], owned, width),
            mod_total,
        )
        states = (
            skip_proj_state,
            attn_qkv_state,
            attn_out_state,
            ffn_up_state,
            ffn_down_state,
            ada_mod_state,
        )
        for state, gradient, rate in zip(states, grads, rates):
            outs.extend(adamw_step(state, gradient, rate))
        return tuple(outs)
    ffn_new = update(ffn_grads, ffn_sum.ends(), [ffn_up_state, ffn_down_state], rates[3:5])
    qkv_new = update(
        functools.partial(attention_grads, count if wide else 1, seq if wide else 1),
        qkv_sum.ends(),
        [attn_qkv_state, attn_out_state],
        rates[1:3],
    )
    mod_new = update(
        modulation_grads, [time_rows, after(mod_cots, marks[-1])], [ada_mod_state], rates[5:6]
    )
    skip_new = update(
        skip_grads,
        skip_sums[0].ends() + skip_sums[1].ends(),
        [skip_proj_state],
        rates[:1],
    )
    outs += [*skip_new, *qkv_new, *ffn_new, *mod_new]
    return tuple(outs)


def solution(mesh):
    tokens = P("dp", "seq", None)
    state = P(None, ("dp", "seq"), None)
    master = P(("dp", "seq"), None)
    return jax.shard_map(
        per_device,
        mesh=mesh,
        in_specs=(tokens, tokens, tokens, P(), P("dp"), P("dp"), tokens) + (state,) * 6,
        out_specs=(tokens,) * 3 + (master, state) * 6,
        check_vma=False,
    )
```

```python
import functools
import math

import jax
import jax.numpy as jnp
from jax import lax
from jax.experimental import pallas as pl
from jax.experimental.pallas import tpu as pltpu
from jax.sharding import PartitionSpec as P

D = 1024
HEADS = 16
DH = 64
FF = 4096
STEP = 3
LOG2E = 1.4426950408889634
BF = jnp.bfloat16
F32 = jnp.float32
MIB = 2**20
highest = lax.Precision.HIGHEST


def dot_nn(a, b):
    return lax.dot_general(a, b, (((1,), (0,)), ((), ())), preferred_element_type=F32)


def dot_nt(a, b):
    return lax.dot_general(a, b, (((1,), (1,)), ((), ())), preferred_element_type=F32)


def dot_tn(a, b):
    return lax.dot_general(a, b, (((0,), (0,)), ((), ())), preferred_element_type=F32)


def params(mib):
    return pltpu.CompilerParams(vmem_limit_bytes=mib * MIB)


def cost(flops, moved):
    return pl.CostEstimate(flops=int(flops), bytes_accessed=int(moved), transcendentals=0)


def whole(shape):
    return pl.BlockSpec(shape, lambda *_: (0,) * len(shape))


def with_place(grid, in_specs, out_specs, scratch_shapes=()):
    return pltpu.PrefetchScalarGridSpec(
        num_scalar_prefetch=1,
        grid=grid,
        in_specs=in_specs,
        out_specs=out_specs,
        scratch_shapes=scratch_shapes,
    )


def time_features(flow_values, model_width):
    half_size = model_width // 2
    frequency = jnp.exp(-math.log(10000.0) * jnp.arange(half_size, dtype=F32) / half_size)
    angles = 1000.0 * flow_values[:, None] * frequency[None, :]
    return jax.nn.silu(jnp.concatenate([jnp.sin(angles), jnp.cos(angles)], axis=-1))


def rotary_tables(positions, heads):
    half = DH // 2
    frequency = jnp.exp(-math.log(10000.0) * jnp.arange(half, dtype=F32) / half)
    angles = positions.astype(F32)[:, None] * frequency[None, :]
    cosine, sine = jnp.cos(angles), jnp.sin(angles)
    return (
        jnp.concatenate([cosine, cosine] * heads, axis=-1),
        jnp.concatenate([-sine, sine] * heads, axis=-1),
    )


def swap_halves(values):
    width = values.shape[1]
    half = DH // 2
    if width == DH:
        return jnp.concatenate([values[:, half:], values[:, :half]], axis=1)
    lane = lax.broadcasted_iota(jnp.int32, (1, width), 1)
    first = (lane % DH) < half
    return jnp.where(
        first, pltpu.roll(values, width - half, 1), pltpu.roll(values, half, 1)
    )


def normalise(values):
    centre = values - jnp.mean(values, axis=-1, keepdims=True)
    spread = jnp.mean(centre * centre, axis=-1, keepdims=True)
    inverse = lax.rsqrt(spread + 1e-06)
    return centre * inverse, inverse


def norm_back(normal, inverse, scaled):
    return inverse * (
        scaled
        - jnp.mean(scaled, axis=-1, keepdims=True)
        - normal * jnp.mean(scaled * normal, axis=-1, keepdims=True)
    )


def gelu_and_slope(u):
    root = math.sqrt(2.0 / math.pi)
    square = u * u
    t = jnp.tanh(root * u * (1.0 + 0.044715 * square))
    half = 0.5 * (1.0 + t)
    slope = half + 0.5 * u * (1.0 - t * t) * (root * (1.0 + 3.0 * 0.044715 * square))
    return u * half, slope


def learning_rates():
    fans = (2 * D, D, D // 16, D, FF, D // 8)
    return tuple((2.0 * fan_value ** (-0.5) for fan_value in fans))


def adamw_step(state, gradient, rate):
    master, first_moment, second_moment = (state[0], state[1], state[2])
    first_moment = 0.5 * first_moment + 0.5 * gradient
    second_moment = 0.5 * second_moment + 0.5 * gradient * gradient
    correction = 1.0 - 0.5**STEP
    master = master - rate * (
        first_moment / correction / (jnp.sqrt(second_moment / correction) + 1e-08) + 0.01 * master
    )
    return (master, jnp.stack([first_moment, second_moment]))


def stack_rows(packed_ref, out_ref, owned):
    cols = out_ref.shape[1]
    pieces = packed_ref.shape[1] // cols
    for r in range(packed_ref.shape[0] // owned):
        for q in range(pieces):
            at = (r * pieces + q) * owned
            out_ref[at : at + owned] = packed_ref[
                r * owned : (r + 1) * owned, q * cols : (q + 1) * cols
            ]


def skip_kernel(
    owned, fr_ref, sk_ref, cond_ref, packed_ref, mod_ref, hidden_ref, normed_ref, w_ref
):
    @pl.when(pl.program_id(0) == 0)
    def _():
        stack_rows(packed_ref, w_ref, owned)

    width = fr_ref.shape[1]
    hidden = (
        dot_nn(fr_ref[...], w_ref[:width])
        + dot_nn(sk_ref[...], w_ref[width:])
        + cond_ref[...].astype(F32)
    )
    hidden_ref[...] = hidden
    normal, _ = normalise(hidden)
    normed_ref[...] = (normal * (1.0 + mod_ref[1:2]) + mod_ref[0:1]).astype(BF)


def skip_weight(weight, owned, width):
    if owned % 16 == 0:
        return weight, pl.BlockSpec((width, 2 * width), lambda *_: (0, 0)), owned
    full = stacked(weight[:, : 2 * width], owned, width)
    return full, whole(full.shape), 2 * width


def skip_forward(frames, skips, cond, weight, mod, owned):
    rows, width = frames.shape
    block = min(256, rows)
    row_spec = pl.BlockSpec((block, width), lambda i: (i, 0))
    weight, weight_spec, piece = skip_weight(weight, owned, width)
    return pl.pallas_call(
        functools.partial(skip_kernel, piece),
        grid=(rows // block,),
        in_specs=[row_spec, row_spec, row_spec, weight_spec, whole(mod.shape)],
        out_specs=[row_spec, row_spec],
        out_shape=[
            jax.ShapeDtypeStruct((rows, width), F32),
            jax.ShapeDtypeStruct((rows, width), BF),
        ],
        scratch_shapes=[pltpu.VMEM((2 * width, width), BF)],
        compiler_params=params(60),
        cost_estimate=cost(4 * rows * width * width, 12 * rows * width + 4 * width * width),
    )(frames, skips, cond, weight, mod)


def qkv_kernel(stride, me_ref, x_ref, wq_ref, wk_ref, wv_ref, cos_ref, sin_ref, *refs):
    out_refs, w_ref = refs[:-1], refs[-1]
    size = 128 * stride
    for part, ref in enumerate((wq_ref, wk_ref, wv_ref)):
        w_ref[:, part * size : (part + 1) * size] = ref[...]
    packed = dot_nn(x_ref[...], w_ref[...])
    cosine, sine = cos_ref[...], sin_ref[...]
    turned = []
    for at in range(0, 2 * size, 128):
        raw = packed[:, at : at + 128]
        turned.append((raw * cosine + swap_halves(raw) * sine).astype(BF))
    value = packed[:, 2 * size :].astype(BF)
    groups = len(out_refs) // stride
    for d in range(groups):

        @pl.when(pl.program_id(0) == d)
        def _(d=d):
            for c in range(stride):
                out_ref = out_refs[c * groups + d]
                out_ref[:, 0:128] = turned[c]
                out_ref[:, 128:256] = turned[stride + c]
                out_ref[:, 256:384] = value[:, c * 128 : (c + 1) * 128]


def qkv_forward(normed, weight, cosine, sine, stride, me):
    rows, width = normed.shape
    size = 128 * stride
    groups = width // size

    def columns(part):
        return pl.BlockSpec(
            (width, size),
            lambda i, me: (0, (2 + part) * groups + lax.bitwise_xor(i, me[0])),
        )

    outs = pl.pallas_call(
        functools.partial(qkv_kernel, stride),
        grid_spec=with_place(
            (groups,),
            [
                whole(normed.shape),
                columns(0),
                columns(1),
                columns(2),
                whole(cosine.shape),
                whole(sine.shape),
            ],
            [whole((rows, 384))] * (groups * stride),
            [pltpu.VMEM((width, 3 * size), BF)],
        ),
        out_shape=[jax.ShapeDtypeStruct((rows, 384), BF)] * (groups * stride),
        compiler_params=params(60),
        cost_estimate=cost(6 * rows * width * width, 8 * rows * width + 6 * width * width),
    )(me, normed, weight, weight, weight, cosine, sine)
    return [outs[c * groups : (c + 1) * groups] for c in range(stride)]


def attend_kernel(heads, block, count, *refs):
    piece_refs, out_refs = refs[:count], refs[count : 2 * count]
    log_ref, qkv_ref = refs[2 * count :]
    width = heads * DH
    rows = piece_refs[0].shape[0]
    i = pl.program_id(0)

    @pl.when(i == 0)
    def _():
        for d, ref in enumerate(piece_refs):
            qkv_ref[d * rows : (d + 1) * rows] = ref[...]

    q = qkv_ref[pl.ds(pl.multiple_of(i * block, block), block), 0:width]
    k = qkv_ref[:, width : 2 * width]
    v = qkv_ref[:, 2 * width : 3 * width]
    lane = lax.broadcasted_iota(jnp.int32, (1, width), 1) // DH
    outs = []
    for h in range(heads):
        own = jnp.where(lane == h, q, jnp.zeros_like(q)) if heads > 1 else q
        scores = dot_nt(k, own) * (0.125 * LOG2E)
        top = jnp.max(scores, axis=0, keepdims=True)
        probs = jnp.exp2(scores - top)
        total = jnp.sum(probs, axis=0, keepdims=True)
        outs.append(dot_tn(v[:, h * DH : (h + 1) * DH], probs.astype(BF)) * (1.0 / total))
        log_ref[h : h + 1, :] = top + jnp.log2(total)
    out = (jnp.concatenate(outs, axis=0) if heads > 1 else outs[0]).T.astype(BF)
    per = block // rows
    for d, out_ref in enumerate(out_refs):

        @pl.when(i == d // per)
        def _(d=d, out_ref=out_ref):
            out_ref[...] = out[(d % per) * rows : (d % per + 1) * rows]


def attend(pieces, heads):
    count, rows = len(pieces), pieces[0].shape[0]
    length = count * rows
    width = heads * DH
    block = min(512, length)
    outs = pl.pallas_call(
        functools.partial(attend_kernel, heads, block, count),
        grid=(length // block,),
        in_specs=[whole(p.shape) for p in pieces],
        out_specs=[whole((rows, width))] * count
        + [pl.BlockSpec((heads, block), lambda i: (0, i))],
        out_shape=[jax.ShapeDtypeStruct((rows, width), BF)] * count
        + [jax.ShapeDtypeStruct((heads, length), F32)],
        scratch_shapes=[pltpu.VMEM((length, 3 * width), BF)],
        compiler_params=params(50),
        cost_estimate=cost(16 * length * length * DH * heads, 8 * length * width),
    )(*pieces)
    return outs[:count], outs[count]


def attend_back_kernel(heads, block, count, *refs):
    piece_refs, do_refs, o_refs = refs[:count], refs[count : 2 * count], refs[2 * count : 3 * count]
    log_ref, cos_ref, sin_ref = refs[3 * count : 3 * count + 3]
    out_refs = refs[3 * count + 3 : 4 * count + 3]
    qkv_ref, do_ref, dq_sum, delta = refs[4 * count + 3 :]
    width = heads * DH
    rows = piece_refs[0].shape[0]
    i = pl.program_id(0)
    lane = lax.broadcasted_iota(jnp.int32, (1, width), 1) // DH

    @pl.when(i == 0)
    def _():
        dq_sum[...] = jnp.zeros_like(dq_sum)
        for d in range(count):
            at = slice(d * rows, (d + 1) * rows)
            qkv_ref[at] = piece_refs[d][...]
            do_own = do_refs[d][...]
            do_ref[at] = do_own
            product = (do_own.astype(F32) * o_refs[d][...].astype(F32)).T
            for h in range(heads):
                delta[h : h + 1, at] = jnp.sum(
                    product[h * DH : (h + 1) * DH], axis=0, keepdims=True
                )

    here = pl.ds(pl.multiple_of(i * block, block), block)
    q = qkv_ref[:, 0:width]
    k = qkv_ref[here, width : 2 * width]
    v = qkv_ref[here, 2 * width : 3 * width]
    do = do_ref[...]
    k_turned = k.T
    dk = dv = None
    for h in range(heads):
        own = lane == h
        k_own = jnp.where(own, k, jnp.zeros_like(k)) if heads > 1 else k
        v_own = jnp.where(own, v, jnp.zeros_like(v)) if heads > 1 else v
        scores = dot_nt(k_own, q) * (0.125 * LOG2E)
        probs = jnp.exp2(scores - log_ref[h : h + 1, :])
        prob_grad = dot_nt(v_own, do)
        score_grad = (probs * (prob_grad - delta[h : h + 1, :])).astype(BF)
        part = slice(h * DH, (h + 1) * DH)
        dq_sum[part, :] += dot_nn(k_turned[part], score_grad)
        dv_own = dot_nn(probs.astype(BF), do)
        dk_own = dot_nn(score_grad, q)
        dv = dv_own if dv is None else jnp.where(own, dv_own, dv)
        dk = dk_own if dk is None else jnp.where(own, dk_own, dk)
    dk = dk * 0.125
    dk = (dk * cos_ref[here, :] - swap_halves(dk) * sin_ref[here, :]).astype(BF)
    dv = dv.astype(BF)
    per = block // rows
    for d, out_ref in enumerate(out_refs):

        @pl.when(i == d // per)
        def _(d=d, out_ref=out_ref):
            at = slice((d % per) * rows, (d % per + 1) * rows)
            out_ref[:, width : 2 * width] = dk[at]
            out_ref[:, 2 * width : 3 * width] = dv[at]

    @pl.when(i == pl.num_programs(0) - 1)
    def _():
        dq = (dq_sum[...] * 0.125).T
        dq = (dq * cos_ref[...] - swap_halves(dq) * sin_ref[...]).astype(BF)
        for d, out_ref in enumerate(out_refs):
            out_ref[:, 0:width] = dq[d * rows : (d + 1) * rows]


def attend_back(pieces, do, chunk, o, log_total, cosine, sine, heads):
    count, rows = len(pieces), pieces[0].shape[0]
    length = count * rows
    width = heads * DH
    block = min(512, length)
    operands = (*pieces, *do, *o, log_total, cosine, sine)
    return pl.pallas_call(
        functools.partial(attend_back_kernel, heads, block, count),
        grid=(length // block,),
        in_specs=[whole(p.shape) for p in pieces]
        + [pl.BlockSpec((rows, width), lambda i: (0, chunk))] * count
        + [whole(a.shape) for a in operands[2 * count :]],
        out_specs=[whole((rows, 3 * width))] * count,
        out_shape=[jax.ShapeDtypeStruct((rows, 3 * width), BF)] * count,
        scratch_shapes=[
            pltpu.VMEM((length, 3 * width), BF),
            pltpu.VMEM((length, width), BF),
            pltpu.VMEM((width, length), F32),
            pltpu.VMEM((heads, length), F32),
        ],
        compiler_params=params(60),
        cost_estimate=cost(24 * length * length * DH * heads, 20 * length * width),
    )(*operands)


def pieces_at(me_ref, count, groups, width, part=0, parts_width=0):
    for c in range(count):
        for d in range(groups):
            at = (lax.bitwise_xor(me_ref[0], d) * count + c) * width + part * parts_width
            yield c, d, pl.ds(pl.multiple_of(at, 128), width)


def out_kernel(count, groups, me_ref, *refs):
    o_refs = refs[: count * groups]
    w_ref, hidden_ref, mod_ref, attended_ref, branch_ref, middle_ref, normed_ref = refs[
        count * groups :
    ]
    for c, d, columns in pieces_at(me_ref, count, groups, o_refs[0].shape[1]):
        attended_ref[:, columns] = o_refs[c * groups + d][...]
    branch = dot_nn(attended_ref[...], w_ref[...])
    branch_ref[...] = branch
    middle = hidden_ref[...] + mod_ref[2:3] * branch
    middle_ref[...] = middle
    normal, _ = normalise(middle)
    normed_ref[...] = (normal * (1.0 + mod_ref[4:5]) + mod_ref[3:4]).astype(BF)


def out_forward(chunks, weight, hidden, mod, at, me):
    rows, width = hidden.shape
    block = min(256, rows)
    row_spec = pl.BlockSpec((block, width), lambda i, *_: (i, 0))
    count, groups = len(chunks), len(chunks[0])
    o_spec = pl.BlockSpec((block, chunks[0][0].shape[1]), lambda i, *_: (i, 0))
    return pl.pallas_call(
        functools.partial(out_kernel, count, groups),
        grid_spec=with_place(
            (rows // block,),
            [o_spec] * (count * groups)
            + [pl.BlockSpec((width, width), lambda *_: (0, at)), row_spec, whole(mod.shape)],
            [row_spec] * 4,
        ),
        out_shape=[
            jax.ShapeDtypeStruct((rows, width), BF),
            jax.ShapeDtypeStruct((rows, width), F32),
            jax.ShapeDtypeStruct((rows, width), F32),
            jax.ShapeDtypeStruct((rows, width), BF),
        ],
        compiler_params=params(60),
        cost_estimate=cost(2 * rows * width * width, 18 * rows * width + 2 * width * width),
    )(me, *[piece for chunk in chunks for piece in chunk], weight, hidden, mod)


def ffn_kernel(
    owned, x_ref, dc_ref, up_ref, packed_ref, y_ref, dx_ref, activated_ref, up_cot_ref, dn_ref
):
    @pl.when(pl.program_id(0) == 0)
    def _():
        y_ref[...] = jnp.zeros_like(y_ref)
        dx_ref[...] = jnp.zeros_like(dx_ref)

    stack_rows(packed_ref, dn_ref, owned)
    up, dn = up_ref[...], dn_ref[...]
    value, slope = gelu_and_slope(dot_nn(x_ref[...], up))
    activated = value.astype(BF)
    up_cot = (dot_nt(dc_ref[...], dn) * slope).astype(BF)
    activated_ref[...] = activated
    up_cot_ref[...] = up_cot
    y_ref[...] += dot_nn(activated, dn)
    dx_ref[...] += dot_nt(up_cot, up)


def ffn_grad_kernel(
    owned, x_ref, dc_ref, activated_ref, up_cot_ref, grads_ref, x_turned, gu, gd, sems
):
    i, last = pl.program_id(0), pl.num_programs(0) - 1
    slot = lax.rem(i, 2)
    block = up_cot_ref.shape[1]
    part = gd.shape[1]
    pieces = block // part

    def sends(step, at):
        across = pl.ds(pl.multiple_of(step * block, block), block)
        down = pl.ds(pl.multiple_of(step * part, part), part)
        half = grads_ref.shape[1] // 2
        return (
            pltpu.make_async_copy(gu.at[at], grads_ref.at[:, across], sems.at[0, at]),
            pltpu.make_async_copy(gd.at[at], grads_ref.at[down, pl.ds(half, half)], sems.at[1, at]),
        )

    @pl.when(i == 0)
    def _():
        x_turned[...] = x_ref[...].T

    @pl.when(i >= 2)
    def _():
        for copy in sends(i - 2, slot):
            copy.wait()

    dc = dc_ref[...]
    gu[slot] = dot_nn(x_turned[...], up_cot_ref[...]).astype(BF)
    down_grad = dot_tn(activated_ref[...], dc).astype(BF)
    width = dc.shape[1]
    for r in range(part // owned):
        for q in range(pieces):
            at = (r * pieces + q) * owned
            gd[slot, r * owned : (r + 1) * owned, q * width : (q + 1) * width] = down_grad[
                at : at + owned
            ]
    for copy in sends(i, slot):
        copy.start()

    @pl.when(i == last)
    def _():
        for copy in sends(last - 1, 1 - slot) + sends(last, slot):
            copy.wait()


FFN_BLOCK = 512


def ffn(x, dc, weights, owned):
    rows, width = x.shape
    hidden_width = FF
    pieces = hidden_width // width
    block = FFN_BLOCK
    steps = hidden_width // block
    part = block // pieces
    packed, piece = weights, owned
    if owned % 16:
        full = stacked(weights[:, :hidden_width], owned, width)
        packed, piece = side_by_side_blocks(full, part, pieces), part
    across = pl.BlockSpec((rows, block), lambda i: (0, i))
    return pl.pallas_call(
        functools.partial(ffn_kernel, piece),
        grid=(steps,),
        in_specs=[
            whole(x.shape),
            whole(x.shape),
            pl.BlockSpec((width, block), lambda i: (0, steps + i)),
            pl.BlockSpec((part, hidden_width), lambda i: (i, 0)),
        ],
        out_specs=[whole(x.shape), whole(x.shape), across, across],
        out_shape=[
            jax.ShapeDtypeStruct((rows, width), F32),
            jax.ShapeDtypeStruct((rows, width), F32),
            jax.ShapeDtypeStruct((rows, hidden_width), BF),
            jax.ShapeDtypeStruct((rows, hidden_width), BF),
        ],
        scratch_shapes=[pltpu.VMEM((block, width), BF)],
        compiler_params=params(60),
        cost_estimate=cost(8 * rows * width * hidden_width, 8 * width * hidden_width),
    )(x, dc, weights, packed)


def ffn_grad(x, dc, activated, up_cot, owned):
    rows, width = x.shape
    hidden_width = activated.shape[1]
    pieces = hidden_width // width
    block = FFN_BLOCK
    part = block // pieces
    across = pl.BlockSpec((rows, block), lambda i: (0, i))
    grads = pl.pallas_call(
        functools.partial(ffn_grad_kernel, owned if owned % 16 == 0 else part),
        grid=(hidden_width // block,),
        in_specs=[whole(x.shape), whole(x.shape), across, across],
        out_specs=pl.BlockSpec(memory_space=pl.ANY),
        out_shape=jax.ShapeDtypeStruct((width, 2 * hidden_width), BF),
        scratch_shapes=[
            pltpu.VMEM((width, rows), BF),
            pltpu.VMEM((2, width, block), BF),
            pltpu.VMEM((2, part, hidden_width), BF),
            pltpu.SemaphoreType.DMA((2, 2)),
        ],
        compiler_params=params(60),
        cost_estimate=cost(4 * rows * width * hidden_width, 8 * width * hidden_width),
    )(x, dc, activated, up_cot)
    if owned % 16:
        full = stacked(grads[:, hidden_width:], part, width)
        grads = jnp.concatenate(
            [grads[:, :hidden_width], side_by_side_blocks(full, owned, pieces)], axis=1
        )
    return grads


def mid_kernel(groups, me_ref, *refs):
    y_ref, dx_ref, middle_ref, branch_ref, grad_ref, w_ref, mod_ref = refs[:7]
    block_ref, mgrad_ref, bcot_ref, sums_ref = refs[7:11]
    piece_refs, attended_grad = refs[11:-1], refs[-1]

    @pl.when(pl.program_id(0) == 0)
    def _():
        sums_ref[...] = jnp.zeros_like(sums_ref)

    y, middle, w = y_ref[...], middle_ref[...], dx_ref[...]
    grad = grad_ref[...].astype(F32)
    block_ref[...] = (middle + mod_ref[5:6] * y).astype(BF)
    normal, inverse = normalise(middle)
    middle_grad = grad + norm_back(normal, inverse, w * (1.0 + mod_ref[4:5]))
    mgrad_ref[...] = middle_grad
    branch_cot = (middle_grad * mod_ref[2:3]).astype(BF)
    bcot_ref[...] = branch_cot
    sums_ref[0:1] += jnp.sum(middle_grad * branch_ref[...], axis=0, keepdims=True)
    sums_ref[1:2] += jnp.sum(w, axis=0, keepdims=True)
    sums_ref[2:3] += jnp.sum(w * normal, axis=0, keepdims=True)
    sums_ref[3:4] += jnp.sum(grad * y, axis=0, keepdims=True)
    attended_grad[...] = dot_nt(branch_cot, w_ref[...]).astype(BF)
    for _, d, columns in pieces_at(me_ref, 1, groups, piece_refs[0].shape[1]):
        piece_refs[d][...] = attended_grad[:, columns]


def mid_back(y, dx, middle, branch, grad, weight, mod, at, me, groups):
    rows, width = y.shape
    block = min(256, rows)
    cols = width // groups
    row_spec = pl.BlockSpec((block, width), lambda i, *_: (i, 0))
    piece_spec = pl.BlockSpec((block, cols), lambda i, *_: (i, 0))
    return pl.pallas_call(
        functools.partial(mid_kernel, groups),
        grid_spec=with_place(
            (rows // block,),
            [row_spec] * 5 + [pl.BlockSpec((width, width), lambda *_: (0, at)), whole(mod.shape)],
            [row_spec] * 3 + [whole((8, width))] + [piece_spec] * groups,
            [pltpu.VMEM((block, width), BF)],
        ),
        out_shape=[
            jax.ShapeDtypeStruct((rows, width), BF),
            jax.ShapeDtypeStruct((rows, width), F32),
            jax.ShapeDtypeStruct((rows, width), BF),
            jax.ShapeDtypeStruct((8, width), F32),
        ]
        + [jax.ShapeDtypeStruct((rows, cols), BF)] * groups,
        compiler_params=params(60),
        cost_estimate=cost(2 * rows * width * width, 28 * rows * width + 2 * width * width),
    )(me, y, dx, middle, branch, grad, weight, mod)


def last_kernel(count, groups, owned, me_ref, *refs):
    piece_refs = refs[: count * groups]
    rest = refs[count * groups :]
    hidden_ref, mgrad_ref, wq_ref, wk_ref, wv_ref, packed_ref, mod_ref = rest[:7]
    hgrad_ref, frames_ref, skips_ref, sums_ref, wskip_ref, cot_ref = rest[7:]

    @pl.when(pl.program_id(0) == 0)
    def _():
        sums_ref[...] = jnp.zeros_like(sums_ref)
        stack_rows(packed_ref, wskip_ref, owned)

    width = piece_refs[0].shape[1] // 3
    model = hidden_ref.shape[1]
    for part in range(3):
        for c, d, columns in pieces_at(me_ref, count, groups, width, part, model):
            cot_ref[:, columns] = piece_refs[c * groups + d][
                :, part * width : (part + 1) * width
            ]
    w = (
        dot_nt(cot_ref[:, :model], wq_ref[...])
        + dot_nt(cot_ref[:, model : 2 * model], wk_ref[...])
        + dot_nt(cot_ref[:, 2 * model :], wv_ref[...])
    )
    normal, inverse = normalise(hidden_ref[...])
    sums_ref[0:1] += jnp.sum(w, axis=0, keepdims=True)
    sums_ref[1:2] += jnp.sum(w * normal, axis=0, keepdims=True)
    hidden_grad = (
        mgrad_ref[...] + norm_back(normal, inverse, w * (1.0 + mod_ref[1:2]))
    ).astype(BF)
    hgrad_ref[...] = hidden_grad
    frames_ref[...] = dot_nt(hidden_grad, wskip_ref[:model]).astype(BF)
    skips_ref[...] = dot_nt(hidden_grad, wskip_ref[model:]).astype(BF)


def last_back(chunks, hidden, middle_grad, weights, mod, owned, me):
    rows, width = hidden.shape
    block = min(256, rows)
    row_spec = pl.BlockSpec((block, width), lambda i, *_: (i, 0))
    count, groups = len(chunks), len(chunks[0])
    piece_spec = pl.BlockSpec((block, chunks[0][0].shape[1]), lambda i, *_: (i, 0))
    w_skip, skip_spec, piece = skip_weight(weights, owned, width)

    def part_spec(part):
        return pl.BlockSpec((width, width), lambda *_: (0, 2 + part))

    return pl.pallas_call(
        functools.partial(last_kernel, count, groups, piece),
        grid_spec=with_place(
            (rows // block,),
            [piece_spec] * (count * groups)
            + [row_spec, row_spec, part_spec(0), part_spec(1), part_spec(2)]
            + [skip_spec, whole(mod.shape)],
            [row_spec, row_spec, row_spec, whole((8, width))],
            [pltpu.VMEM((2 * width, width), BF), pltpu.VMEM((block, 3 * width), BF)],
        ),
        out_shape=[
            jax.ShapeDtypeStruct((rows, width), BF),
            jax.ShapeDtypeStruct((rows, width), BF),
            jax.ShapeDtypeStruct((rows, width), BF),
            jax.ShapeDtypeStruct((8, width), F32),
        ],
        compiler_params=params(60),
        cost_estimate=cost(2 * rows * width * width, 4 * rows * width),
    )(
        me,
        *[piece for chunk in chunks for piece in chunk],
        hidden,
        middle_grad,
        weights,
        weights,
        weights,
        w_skip,
        mod,
    )


def out_wgrad_kernel(left_ref, right_ref, out_ref):
    out_ref[...] = dot_tn(left_ref[...], right_ref[...]).astype(BF)


def out_wgrad_part(left, right, columns):
    rows, width = left.shape
    block = 512
    first = columns // block - width // block
    return pl.pallas_call(
        out_wgrad_kernel,
        grid=(width // block,),
        in_specs=[whole(left.shape), pl.BlockSpec((rows, block), lambda i: (0, i))],
        out_specs=pl.BlockSpec((width, block), lambda i: (0, first + i)),
        out_shape=jax.ShapeDtypeStruct((width, columns), BF),
        compiler_params=params(60),
        cost_estimate=cost(2 * rows * width * width, 6 * width * width),
    )(left, right)


def qkv_grad_kernel(groups, me_ref, *refs):
    x_ref, piece_refs = refs[0], refs[1 : 1 + groups]
    out_ref, piece, x_turned = refs[-3:]
    i = pl.program_id(0)

    @pl.when(i == 0)
    def _():
        x_turned[...] = x_ref[...].T

    for d, ref in enumerate(piece_refs):

        @pl.when(i == d)
        def _(ref=ref):
            piece[...] = ref[...]

    out_ref[...] = dot_nn(x_turned[...], piece[...]).astype(BF)


def qkv_grad(normed, pieces, me, held=None):
    groups = len(pieces)
    rows, cols = pieces[0].shape
    width = normed.shape[1]
    given = [] if held is None else [held]
    return pl.pallas_call(
        functools.partial(qkv_grad_kernel, groups),
        grid_spec=with_place(
            (groups,),
            [whole(normed.shape)]
            + [whole((rows, cols))] * groups
            + [pl.BlockSpec(memory_space=pl.ANY)] * len(given),
            pl.BlockSpec((width, cols), lambda i, me: (0, lax.bitwise_xor(i, me[0]))),
            [pltpu.VMEM((rows, cols), BF), pltpu.VMEM((width, rows), BF)],
        ),
        out_shape=jax.ShapeDtypeStruct((width, groups * cols) if held is None else held.shape, BF),
        input_output_aliases={2 + groups: 0} if given else {},
        compiler_params=params(40),
        cost_estimate=cost(rows * width, 1024),
    )(me, normed, *pieces, *given)


def update_kernel(grads_of, rates, *refs):
    count = len(rates)
    outs, states, given = refs[-2 * count :], refs[-3 * count : -2 * count], refs[: -3 * count]
    correction = 1.0 - 0.5**STEP
    for at, rows, cols, gradient in grads_of(*given):
        state, new_ref, moments_ref = states[at], outs[2 * at], outs[2 * at + 1]
        master = state[0, rows, cols]
        first = 0.5 * state[1, rows, cols] + 0.5 * gradient
        second = 0.5 * state[2, rows, cols] + 0.5 * gradient * gradient
        moments_ref[0, rows, cols] = first
        moments_ref[1, rows, cols] = second
        new_ref[rows, cols] = master - rates[at] * (
            first / correction / (jnp.sqrt(second / correction) + 1e-08) + 0.01 * master
        )


def update(grads_of, given, states, rates):
    shapes = []
    for state in states:
        _, rows, cols = state.shape
        shapes += [(rows, cols), (2, rows, cols)]
    moved = 6 * sum(state.size for state in states) * 4 // 3
    return pl.pallas_call(
        functools.partial(update_kernel, grads_of, rates),
        grid=(1,),
        in_specs=[whole(a.shape) for a in (*given, *states)],
        out_specs=[whole(shape) for shape in shapes],
        out_shape=[jax.ShapeDtypeStruct(shape, F32) for shape in shapes],
        compiler_params=params(40),
        cost_estimate=cost(moved, moved),
    )(*given, *states)


def skip_grads(*refs):
    half = refs[0].shape[1]
    for side in range(2):
        rest, arrived = refs[2 * side][...], refs[2 * side + 1][...]
        yield 0, slice(None), slice(side * half, (side + 1) * half), rest + arrived.astype(F32)


def ffn_grads(rest_ref, arrived_ref):
    owned, cols = rest_ref.shape
    hidden_width, width = cols // 2, D
    for q in range(cols // width):
        at = slice(q * width, (q + 1) * width)
        gradient = rest_ref[:, at] + arrived_ref[:, at].astype(F32)
        if q * width < hidden_width:
            yield 0, slice(None), at, gradient
        else:
            r = q - hidden_width // width
            yield 1, slice(r * owned, (r + 1) * owned), slice(None), gradient


def attention_columns(count, groups):
    cols = D // (count * groups)
    for c in range(count):
        for j in range(groups):
            for part in range(3):
                yield 0, part * D + (j * count + c) * cols, cols
        if c == 0:
            yield 1, 0, D


def attention_grads(count, groups, rest_ref, arrived_ref):
    at = 0
    for weight, to, cols in attention_columns(count, groups):
        here = slice(at, at + cols)
        gradient = rest_ref[:, here] + arrived_ref[:, here].astype(F32)
        yield weight, slice(None), slice(to, to + cols), gradient
        at += cols


def modulation_grads(time_ref, cots_ref):
    for at in range(0, cots_ref.shape[1], D):
        gradient = lax.dot_general(
            time_ref[...],
            cots_ref[:, at : at + D],
            (((0,), (0,)), ((), ())),
            precision=highest,
            preferred_element_type=F32,
        )
        yield 0, slice(None), slice(at, at + D), gradient


def bits_of(axis):
    size = lax.axis_size(axis)
    return [(axis, b) for b in reversed(range(size.bit_length() - 1))]


def my_bit(level):
    axis, bit = level
    return (lax.axis_index(axis) >> bit) & 1


def swap(values, level):
    axis, bit = level
    return lax.ppermute(values, axis, [(i, i ^ (1 << bit)) for i in range(lax.axis_size(axis))])


def after(values, *others):
    return lax.optimization_barrier((values, *others))[0]


class ModulationCots:
    def __init__(self, own):
        self.own, self.order = own, bits_of("seq")[::-1] + bits_of("dp")[::-1]
        self.arrived = None

    def settle(self, *waits):
        if self.arrived is None:
            return
        level, other = self.arrived
        other = after(other, *waits) if waits else other
        if level[0] == "seq":
            self.own = self.own + other
        else:
            self.own = jnp.where(
                my_bit(level) == 0,
                jnp.concatenate([self.own, other], axis=0),
                jnp.concatenate([other, self.own], axis=0),
            )
        self.arrived = None

    def step(self, *waits):
        self.settle(*waits)
        level = self.order.pop(0)
        self.arrived = (level, swap(self.own, level))


class ScatterSum:
    def __init__(self, grad, order, dims):
        self.dims, self.order = list(dims), list(order)
        rows, cols = grad.shape
        split = [2] * len(self.dims)
        self.terms = [grad.reshape(split + [rows // 2 ** len(split), cols])]

    def hold(self, *waits):
        if waits:
            self.terms[-1] = after(self.terms[-1], *waits)

    def step(self, *waits, late=()):
        self.hold(*waits)
        level = self.order.pop(0)
        at, mine = self.dims.index(level), my_bit(level)
        self.dims.pop(at)

        def halves(side):
            return [lax.dynamic_index_in_dim(t, side, at, keepdims=False) for t in self.terms]

        leaving = halves(1 - mine)
        total = leaving[0]
        if len(leaving) > 1:
            total = sum(t.astype(F32) for t in leaving).astype(total.dtype)
        total = after(total, *late) if late else total
        self.sent = total
        arrived = swap(total, level)
        self.terms = halves(mine) + [arrived]
        return arrived

    def ends(self):
        return [sum(t.astype(F32) for t in self.terms[:-1]), self.terms[-1]]


def exchange(pieces):
    places = range(len(pieces))
    return [pieces[0]] + [
        lax.ppermute(pieces[d], "seq", [(i, i ^ d) for i in places]) for d in places[1:]
    ]


def dot_tn_exact(left, right):
    return lax.dot_general(
        left,
        right,
        (((0,), (0,)), ((), ())),
        precision=highest,
        preferred_element_type=F32,
    )


def attention_total(total, count, groups):
    runs, at = ([], []), 0
    for weight, to, cols in attention_columns(count, groups):
        runs[weight].append((to, total[:, at : at + cols]))
        at += cols
    return [jnp.concatenate([v for _, v in sorted(r, key=lambda v: v[0])], axis=1) for r in runs]


def in_order(pieces, me, parts):
    groups, rows = len(pieces), pieces[0].shape[0]
    stack = jnp.take(jnp.stack(pieces), jnp.arange(groups) ^ me[0], axis=0)
    return stack.reshape(groups, rows, parts, -1).transpose(1, 2, 0, 3).reshape(rows, -1)


def by_place(values, me, groups):
    parts = jnp.split(values, groups, axis=1)
    stack = jnp.take(jnp.stack(parts), jnp.arange(groups) ^ me[0], axis=0)
    return [stack[d] for d in range(groups)]


def modulation_rows(partial, order, wait):
    dims = bits_of("dp")
    count, cols = partial.shape
    held = partial.reshape([2] * len(dims) + [count // 2 ** len(dims), cols])
    for level in order:
        at, mine = dims.index(level), my_bit(level)
        dims.pop(at)
        leaving = lax.dynamic_index_in_dim(held, 1 - mine, at, keepdims=False)
        held = lax.dynamic_index_in_dim(held, mine, at, keepdims=False) + swap(leaving, level)
    held = after(held, wait)
    for level in bits_of("seq"):
        held = held + swap(held, level)
    return held


def side_by_side(own, rows):
    return jnp.concatenate(jnp.split(own, own.shape[0] // rows, axis=0), axis=1)


def stacked(full, rows, cols):
    pieces = full.shape[1] // cols
    blocks = full.reshape(full.shape[0] // rows, rows, pieces, cols)
    return blocks.transpose(0, 2, 1, 3).reshape(full.shape[0] * pieces, cols)


def side_by_side_blocks(full, rows, pieces):
    cols = full.shape[1]
    blocks = full.reshape(full.shape[0] // (rows * pieces), pieces, rows, cols)
    return blocks.transpose(0, 2, 1, 3).reshape(full.shape[0] // pieces, pieces * cols)


def gather_pairwise(own, order, last_waits=(), last_use=()):
    rows, cols = own.shape
    held, bits = own.reshape(1, rows, cols), []
    for level in order:
        last = len(bits) == len(order) - 1
        if last and last_waits:
            held = after(held, *last_waits)
        other = swap(held, level)
        if last and last_use:
            other = after(other, *last_use)
        at = sum(1 for bit in bits if bit > level[1])
        bits.append(level[1])
        shape = [2] * (len(bits) - 1)
        own_part = held.reshape(shape + [rows, cols])
        other_part = other.reshape(shape + [rows, cols])
        held = jnp.where(
            my_bit(level) == 0,
            jnp.stack([own_part, other_part], axis=at),
            jnp.stack([other_part, own_part], axis=at),
        ).reshape(2 ** len(bits), rows, cols)
    return held.reshape(-1, cols)


def per_device(
    frames_in,
    skip_in,
    condition,
    flow_time,
    span_start,
    span_length,
    out_grad,
    skip_proj_state,
    attn_qkv_state,
    attn_out_state,
    ffn_up_state,
    ffn_down_state,
    ada_mod_state,
):
    utter_count, rows, width = frames_in.shape
    seq = lax.axis_size("seq")
    everyone = ("dp", "seq")
    owned = attn_qkv_state.shape[1]
    hidden_width = ffn_up_state.shape[2]
    length = rows * seq
    me = lax.axis_index(everyone)
    positions = lax.axis_index("seq") * rows + jnp.arange(rows, dtype=jnp.int32)

    group_heads = HEADS // seq
    heads = min(2, group_heads)
    count = group_heads // heads

    first_own = jnp.concatenate(
        [side_by_side(skip_proj_state[0].astype(BF), owned), attn_qkv_state[0].astype(BF)],
        axis=1,
    )
    first_part = gather_pairwise(first_own, bits_of("seq"))
    first_full = lax.all_gather(first_part, "dp", axis=0, tiled=True)
    out_at = 2 * hidden_width // width

    dp_bits, seq_bits = bits_of("dp"), bits_of("seq")
    core, planes = dp_bits[-1], dp_bits[:-1]

    time_code = time_features(flow_time, width).astype(BF)
    time_own = lax.dynamic_slice_in_dim(time_code, me * owned, owned, 1)
    mod_part = jnp.dot(time_own, ada_mod_state[0].astype(BF), preferred_element_type=F32)
    modulation = modulation_rows(mod_part, [core] + planes, first_part)

    place = lax.axis_index("seq").astype(jnp.int32).reshape(1)
    frame = jnp.arange(length, dtype=jnp.int32)
    frame = ((frame // rows) ^ place) * rows + frame % rows
    cos_all, sin_all = rotary_tables(frame, heads)
    wide = heads == 2
    cos_own, sin_own = rotary_tables(positions, 2)
    span_stop = span_start + span_length

    outs = []
    assert utter_count == 1
    mod = modulation.reshape(6, width)
    inside = (positions >= span_start[0]) & (positions < span_stop[0])
    frames, skips = frames_in[0], skip_in[0]
    cond = jnp.where(inside[:, None], jnp.zeros_like(condition[0]), condition[0])
    grad = jnp.where(inside[:, None], out_grad[0], jnp.zeros_like(out_grad[0]))
    down_cot = (grad.astype(F32) * mod[5:6]).astype(BF)

    hidden, normed = skip_forward(frames, skips, cond, first_full, mod, owned)
    if wide:
        packed = qkv_forward(normed, first_full, cos_own, sin_own, count, place)
    else:
        (pairs,) = qkv_forward(normed, first_full, cos_own, sin_own, 1, 0 * place)
        split = jnp.concatenate(
            [p.reshape(rows, 3, 2, DH).transpose(0, 2, 1, 3).reshape(rows, -1) for p in pairs],
            axis=1,
        )
        packed = [by_place(split, place, seq)]
    arrived = [exchange(part) for part in packed]
    second_own = jnp.concatenate(
        [
            side_by_side(ffn_down_state[0].astype(BF), owned),
            ffn_up_state[0].astype(BF),
            attn_out_state[0].astype(BF),
        ],
        axis=1,
    )
    early = (cos_all, sin_all, cos_own, sin_own, cond, grad, down_cot)
    second_own = gather_pairwise(after(second_own, modulation), seq_bits, early, (packed[0][0],))
    second_full = lax.all_gather(second_own, "dp", axis=0, tiled=True)
    qkv_chunks, attended = [], []
    for pieces in arrived:
        waits = attended[-1][0][:1] if attended else [second_own]
        pieces[1:] = [after(piece, *waits) for piece in pieces[1:]]
        qkv_chunks.append(pieces)
        attended.append(attend(pieces, heads))
    o_chunks = []
    for c, (o, _) in enumerate(attended):
        pieces = exchange(o)
        if c < count - 1:
            pieces[1:] = [after(piece, attended[c + 1][0][0]) for piece in pieces[1:]]
        o_chunks.append(pieces)
    here = place
    if not wide:
        o_chunks, here = [[in_order(o_chunks[0], place, 1)]], 0 * place

    attended_low, branch, middle, normed_two = out_forward(
        o_chunks, second_full, hidden, mod, out_at, here
    )
    downward, normed_two_grad, *ffn_kept = ffn(normed_two, down_cot, second_full, owned)
    mid = mid_back(
        downward,
        normed_two_grad,
        middle,
        branch,
        grad,
        second_full,
        mod,
        out_at,
        here,
        seq if wide else 1,
    )
    do_pieces = exchange(mid[4:] if wide else by_place(mid[4], place, seq))
    block_out, middle_grad, branch_cot, mid_sums = mid[:4]
    every_bit = dp_bits + seq_bits
    rising = seq_bits[::-1]
    columns = 3 * width // count + width
    qkv_part = out_wgrad_part(attended_low, branch_cot, columns) if wide else mid[4]
    ffn_whole = ffn_grad(after(normed_two, qkv_part), down_cot, *ffn_kept, owned)
    ffn_whole = after(ffn_whole, *do_pieces[1:])
    ffn_part = lax.psum_scatter(ffn_whole, "dp", scatter_dimension=0, tiled=True)
    do_pieces[1:] = [after(piece, ffn_whole) for piece in do_pieces[1:]]
    backs = []
    for c in range(count):
        o, log_total = attended[c]
        backs.append(
            attend_back(qkv_chunks[c], do_pieces, c, o, log_total, cos_all, sin_all, heads)
        )
    cot_chunks = [exchange(b) for b in backs]

    sent = [backs[-1][0]]

    def leave(part):
        part.step(sent[-1])
        sent.append(part.sent)

    def wait_in_turn(pieces):
        return pieces[:1] + [after(piece, sent[-1]) for piece in pieces[1:]]

    def full_sum(grad_part, planes_first):
        return ScatterSum(grad_part, [core] + planes_first, every_bit)

    qkv_sums = []
    for c in range(count):
        pieces = cot_chunks[c] = wait_in_turn(cot_chunks[c])
        if not wide:
            cot_chunks = [[in_order(pieces, place, 3)]]
            qkv_part = jnp.concatenate(
                [dot_tn(normed, cot_chunks[0][0]), dot_tn(attended_low, branch_cot)], axis=1
            ).astype(BF)
        else:
            qkv_part = qkv_grad(normed, pieces, place, None if c else qkv_part)
        qkv_sums.append(full_sum(qkv_part, planes if c % 2 else planes[::-1]))
        sent.append(qkv_part)
    for part in qkv_sums:
        part.hold(*cot_chunks[-1][1:])
        leave(part)
    for part in qkv_sums:
        leave(part)
    ffn_sum = ScatterSum(ffn_part, rising, seq_bits)
    leave(ffn_sum)
    cot_chunks[-1] = [after(piece, sent[-1]) for piece in cot_chunks[-1]]
    hidden_grad, frames_grad, skip_grad, last_sums = last_back(
        cot_chunks, hidden, middle_grad, first_full, mod, owned, here
    )
    skip_cot = after(hidden_grad, qkv_sums[-1].terms[-1])
    skip_later = after(skip_cot, qkv_sums[0].terms[-1])
    skip_part = jnp.concatenate(
        [dot_tn(frames, skip_cot).astype(BF), dot_tn(skips, skip_later).astype(BF)], axis=0
    )
    skip_part = after(skip_part, ffn_sum.terms[-1])
    half = width // 2
    skip_sums = [
        ScatterSum(skip_part[:, :half], [core] + planes[::-1] + rising, every_bit),
        ScatterSum(skip_part[:, half:], [core] + planes + rising, every_bit),
    ]
    mod_cot = jnp.concatenate(
        [last_sums[0], last_sums[1], mid_sums[0], mid_sums[1], mid_sums[2], mid_sums[3]]
    ).reshape(1, 6 * width)
    mod_cots = ModulationCots(mod_cot)
    while mod_cots.order[0][0] == "seq":
        mod_cots.step(skip_part)
    mod_cots.settle()
    time_rows = time_own.astype(F32)
    qkv_sum, marks = None, []
    rows_held = owned * seq
    for part in [ffn_sum] + qkv_sums:
        part.hold(hidden_grad)
    ffn_sum.hold(mod_cots.own)
    while skip_sums[0].order or qkv_sum is None or qkv_sum.order:
        for part in skip_sums:
            if part.order:
                leave(part)
        marks.append(sent[-1])
        if mod_cots.order:
            mod_cots.step(sent[-1])
        later = [part for part in qkv_sums if part.order]
        for part in ([ffn_sum] if ffn_sum.order else []) + later:
            leave(part)
        if qkv_sum is not None and qkv_sum.order and len(marks) > 3:
            leave(qkv_sum)
        if not later and qkv_sum is None:
            for part in qkv_sums:
                part.hold(sent[-1])
            qkv_done = [sum(p.ends()).astype(BF).reshape(rows_held, -1) for p in qkv_sums]
            qkv_sum = ScatterSum(jnp.concatenate(qkv_done, axis=1), rising, seq_bits)
            leave(qkv_sum)
    while ffn_sum.order:
        leave(ffn_sum)
    while mod_cots.order:
        mod_cots.step()
    mod_cots.settle(marks[-1])
    mod_cots = mod_cots.own
    ffn_sum.hold(marks[-3])

    rates = learning_rates()
    outs = [block_out[None], frames_grad[None], skip_grad[None]]
    if owned % 16:
        ffn_total, qkv_total = sum(ffn_sum.ends()), sum(qkv_sum.ends())
        skip_total = jnp.concatenate([sum(part.ends()) for part in skip_sums], axis=1)
        mod_total = dot_tn_exact(time_rows, mod_cots)
        qkv_total, out_total = attention_total(
            qkv_total, count if wide else 1, seq if wide else 1
        )
        grads = (
            skip_total.reshape(2 * owned, width),
            qkv_total,
            out_total,
            ffn_total[:, :hidden_width],
            stacked(ffn_total[:, hidden_width:], owned, width),
            mod_total,
        )
        states = (
            skip_proj_state,
            attn_qkv_state,
            attn_out_state,
            ffn_up_state,
            ffn_down_state,
            ada_mod_state,
        )
        for state, gradient, rate in zip(states, grads, rates):
            outs.extend(adamw_step(state, gradient, rate))
        return tuple(outs)
    ffn_new = update(ffn_grads, ffn_sum.ends(), [ffn_up_state, ffn_down_state], rates[3:5])
    qkv_new = update(
        functools.partial(attention_grads, count if wide else 1, seq if wide else 1),
        qkv_sum.ends(),
        [attn_qkv_state, attn_out_state],
        rates[1:3],
    )
    mod_new = update(
        modulation_grads, [time_rows, after(mod_cots, marks[-1])], [ada_mod_state], rates[5:6]
    )
    skip_new = update(
        skip_grads,
        skip_sums[0].ends() + skip_sums[1].ends(),
        [skip_proj_state],
        rates[:1],
    )
    outs += [*skip_new, *qkv_new, *ffn_new, *mod_new]
    return tuple(outs)


def solution(mesh):
    tokens = P("dp", "seq", None)
    state = P(None, ("dp", "seq"), None)
    master = P(("dp", "seq"), None)
    return jax.shard_map(
        per_device,
        mesh=mesh,
        in_specs=(tokens, tokens, tokens, P(), P("dp"), P("dp"), tokens) + (state,) * 6,
        out_specs=(tokens,) * 3 + (master, state) * 6,
        check_vma=False,
    )
```

```python
import functools
import math

import jax
import jax.numpy as jnp
from jax import lax
from jax.experimental import pallas as pl
from jax.experimental.pallas import tpu as pltpu
from jax.sharding import PartitionSpec as P

D = 1024
HEADS = 16
DH = 64
FF = 4096
STEP = 3
LOG2E = 1.4426950408889634
BF = jnp.bfloat16
F32 = jnp.float32
MIB = 2**20
highest = lax.Precision.HIGHEST


def dot_nn(a, b):
    return lax.dot_general(a, b, (((1,), (0,)), ((), ())), preferred_element_type=F32)


def dot_nt(a, b):
    return lax.dot_general(a, b, (((1,), (1,)), ((), ())), preferred_element_type=F32)


def dot_tn(a, b):
    return lax.dot_general(a, b, (((0,), (0,)), ((), ())), preferred_element_type=F32)


def params(mib):
    return pltpu.CompilerParams(vmem_limit_bytes=mib * MIB)


def cost(flops, moved):
    return pl.CostEstimate(flops=int(flops), bytes_accessed=int(moved), transcendentals=0)


def whole(shape):
    return pl.BlockSpec(shape, lambda *_: (0,) * len(shape))


def with_place(grid, in_specs, out_specs, scratch_shapes=()):
    return pltpu.PrefetchScalarGridSpec(
        num_scalar_prefetch=1,
        grid=grid,
        in_specs=in_specs,
        out_specs=out_specs,
        scratch_shapes=scratch_shapes,
    )


def time_features(flow_values, model_width):
    half_size = model_width // 2
    frequency = jnp.exp(-math.log(10000.0) * jnp.arange(half_size, dtype=F32) / half_size)
    angles = 1000.0 * flow_values[:, None] * frequency[None, :]
    return jax.nn.silu(jnp.concatenate([jnp.sin(angles), jnp.cos(angles)], axis=-1))


def rotary_tables(positions, heads):
    half = DH // 2
    frequency = jnp.exp(-math.log(10000.0) * jnp.arange(half, dtype=F32) / half)
    angles = positions.astype(F32)[:, None] * frequency[None, :]
    cosine, sine = jnp.cos(angles), jnp.sin(angles)
    return (
        jnp.concatenate([cosine, cosine] * heads, axis=-1),
        jnp.concatenate([-sine, sine] * heads, axis=-1),
    )


def swap_halves(values):
    width = values.shape[1]
    half = DH // 2
    if width == DH:
        return jnp.concatenate([values[:, half:], values[:, :half]], axis=1)
    lane = lax.broadcasted_iota(jnp.int32, (1, width), 1)
    first = (lane % DH) < half
    return jnp.where(
        first, pltpu.roll(values, width - half, 1), pltpu.roll(values, half, 1)
    )


def normalise(values):
    centre = values - jnp.mean(values, axis=-1, keepdims=True)
    spread = jnp.mean(centre * centre, axis=-1, keepdims=True)
    inverse = lax.rsqrt(spread + 1e-06)
    return centre * inverse, inverse


def norm_back(normal, inverse, scaled):
    return inverse * (
        scaled
        - jnp.mean(scaled, axis=-1, keepdims=True)
        - normal * jnp.mean(scaled * normal, axis=-1, keepdims=True)
    )


def gelu_and_slope(u):
    root = math.sqrt(2.0 / math.pi)
    square = u * u
    t = jnp.tanh(root * u * (1.0 + 0.044715 * square))
    half = 0.5 * (1.0 + t)
    slope = half + 0.5 * u * (1.0 - t * t) * (root * (1.0 + 3.0 * 0.044715 * square))
    return u * half, slope


def learning_rates():
    fans = (2 * D, D, D // 16, D, FF, D // 8)
    return tuple((2.0 * fan_value ** (-0.5) for fan_value in fans))


def adamw_step(state, gradient, rate):
    master, first_moment, second_moment = (state[0], state[1], state[2])
    first_moment = 0.5 * first_moment + 0.5 * gradient
    second_moment = 0.5 * second_moment + 0.5 * gradient * gradient
    correction = 1.0 - 0.5**STEP
    master = master - rate * (
        first_moment / correction / (jnp.sqrt(second_moment / correction) + 1e-08) + 0.01 * master
    )
    return (master, jnp.stack([first_moment, second_moment]))


def stack_rows(packed_ref, out_ref, owned):
    cols = out_ref.shape[1]
    pieces = packed_ref.shape[1] // cols
    for r in range(packed_ref.shape[0] // owned):
        for q in range(pieces):
            at = (r * pieces + q) * owned
            out_ref[at : at + owned] = packed_ref[
                r * owned : (r + 1) * owned, q * cols : (q + 1) * cols
            ]


def skip_kernel(
    owned, fr_ref, sk_ref, cond_ref, packed_ref, mod_ref, hidden_ref, normed_ref, w_ref
):
    @pl.when(pl.program_id(0) == 0)
    def _():
        stack_rows(packed_ref, w_ref, owned)

    width = fr_ref.shape[1]
    hidden = (
        dot_nn(fr_ref[...], w_ref[:width])
        + dot_nn(sk_ref[...], w_ref[width:])
        + cond_ref[...].astype(F32)
    )
    hidden_ref[...] = hidden
    normal, _ = normalise(hidden)
    normed_ref[...] = (normal * (1.0 + mod_ref[1:2]) + mod_ref[0:1]).astype(BF)


def skip_weight(weight, owned, width):
    if owned % 16 == 0:
        return weight, pl.BlockSpec((width, 2 * width), lambda *_: (0, 0)), owned
    full = stacked(weight[:, : 2 * width], owned, width)
    return full, whole(full.shape), 2 * width


def skip_forward(frames, skips, cond, weight, mod, owned):
    rows, width = frames.shape
    block = min(256, rows)
    row_spec = pl.BlockSpec((block, width), lambda i: (i, 0))
    weight, weight_spec, piece = skip_weight(weight, owned, width)
    return pl.pallas_call(
        functools.partial(skip_kernel, piece),
        grid=(rows // block,),
        in_specs=[row_spec, row_spec, row_spec, weight_spec, whole(mod.shape)],
        out_specs=[row_spec, row_spec],
        out_shape=[
            jax.ShapeDtypeStruct((rows, width), F32),
            jax.ShapeDtypeStruct((rows, width), BF),
        ],
        scratch_shapes=[pltpu.VMEM((2 * width, width), BF)],
        compiler_params=params(60),
        cost_estimate=cost(4 * rows * width * width, 12 * rows * width + 4 * width * width),
    )(frames, skips, cond, weight, mod)


def qkv_kernel(stride, me_ref, x_ref, wq_ref, wk_ref, wv_ref, cos_ref, sin_ref, *refs):
    out_refs, w_ref = refs[:-1], refs[-1]
    size = 128 * stride
    for part, ref in enumerate((wq_ref, wk_ref, wv_ref)):
        w_ref[:, part * size : (part + 1) * size] = ref[...]
    packed = dot_nn(x_ref[...], w_ref[...])
    cosine, sine = cos_ref[...], sin_ref[...]
    turned = []
    for at in range(0, 2 * size, 128):
        raw = packed[:, at : at + 128]
        turned.append((raw * cosine + swap_halves(raw) * sine).astype(BF))
    value = packed[:, 2 * size :].astype(BF)
    groups = len(out_refs) // stride
    for d in range(groups):

        @pl.when(pl.program_id(0) == d)
        def _(d=d):
            for c in range(stride):
                out_ref = out_refs[c * groups + d]
                out_ref[:, 0:128] = turned[c]
                out_ref[:, 128:256] = turned[stride + c]
                out_ref[:, 256:384] = value[:, c * 128 : (c + 1) * 128]


def qkv_forward(normed, weight, cosine, sine, stride, me):
    rows, width = normed.shape
    size = 128 * stride
    groups = width // size

    def columns(part):
        return pl.BlockSpec(
            (width, size),
            lambda i, me: (0, (2 + part) * groups + lax.bitwise_xor(i, me[0])),
        )

    outs = pl.pallas_call(
        functools.partial(qkv_kernel, stride),
        grid_spec=with_place(
            (groups,),
            [
                whole(normed.shape),
                columns(0),
                columns(1),
                columns(2),
                whole(cosine.shape),
                whole(sine.shape),
            ],
            [whole((rows, 384))] * (groups * stride),
            [pltpu.VMEM((width, 3 * size), BF)],
        ),
        out_shape=[jax.ShapeDtypeStruct((rows, 384), BF)] * (groups * stride),
        compiler_params=params(60),
        cost_estimate=cost(6 * rows * width * width, 8 * rows * width + 6 * width * width),
    )(me, normed, weight, weight, weight, cosine, sine)
    return [outs[c * groups : (c + 1) * groups] for c in range(stride)]


def attend_kernel(heads, block, count, *refs):
    piece_refs, out_refs = refs[:count], refs[count : 2 * count]
    log_ref, qkv_ref = refs[2 * count :]
    width = heads * DH
    rows = piece_refs[0].shape[0]
    i = pl.program_id(0)

    @pl.when(i == 0)
    def _():
        for d, ref in enumerate(piece_refs):
            qkv_ref[d * rows : (d + 1) * rows] = ref[...]

    q = qkv_ref[pl.ds(pl.multiple_of(i * block, block), block), 0:width]
    k = qkv_ref[:, width : 2 * width]
    v = qkv_ref[:, 2 * width : 3 * width]
    lane = lax.broadcasted_iota(jnp.int32, (1, width), 1) // DH
    outs = []
    for h in range(heads):
        own = jnp.where(lane == h, q, jnp.zeros_like(q)) if heads > 1 else q
        scores = dot_nt(k, own) * (0.125 * LOG2E)
        top = jnp.max(scores, axis=0, keepdims=True)
        probs = jnp.exp2(scores - top)
        total = jnp.sum(probs, axis=0, keepdims=True)
        outs.append(dot_tn(v[:, h * DH : (h + 1) * DH], probs.astype(BF)) * (1.0 / total))
        log_ref[h : h + 1, :] = top + jnp.log2(total)
    out = (jnp.concatenate(outs, axis=0) if heads > 1 else outs[0]).T.astype(BF)
    per = block // rows
    for d, out_ref in enumerate(out_refs):

        @pl.when(i == d // per)
        def _(d=d, out_ref=out_ref):
            out_ref[...] = out[(d % per) * rows : (d % per + 1) * rows]


def attend(pieces, heads):
    count, rows = len(pieces), pieces[0].shape[0]
    length = count * rows
    width = heads * DH
    block = min(512, length)
    outs = pl.pallas_call(
        functools.partial(attend_kernel, heads, block, count),
        grid=(length // block,),
        in_specs=[whole(p.shape) for p in pieces],
        out_specs=[whole((rows, width))] * count
        + [pl.BlockSpec((heads, block), lambda i: (0, i))],
        out_shape=[jax.ShapeDtypeStruct((rows, width), BF)] * count
        + [jax.ShapeDtypeStruct((heads, length), F32)],
        scratch_shapes=[pltpu.VMEM((length, 3 * width), BF)],
        compiler_params=params(50),
        cost_estimate=cost(16 * length * length * DH * heads, 8 * length * width),
    )(*pieces)
    return outs[:count], outs[count]


def attend_back_kernel(heads, block, count, *refs):
    piece_refs, do_refs, o_refs = refs[:count], refs[count : 2 * count], refs[2 * count : 3 * count]
    log_ref, cos_ref, sin_ref = refs[3 * count : 3 * count + 3]
    out_refs = refs[3 * count + 3 : 4 * count + 3]
    qkv_ref, do_ref, dq_sum, delta = refs[4 * count + 3 :]
    width = heads * DH
    rows = piece_refs[0].shape[0]
    i = pl.program_id(0)
    lane = lax.broadcasted_iota(jnp.int32, (1, width), 1) // DH

    @pl.when(i == 0)
    def _():
        dq_sum[...] = jnp.zeros_like(dq_sum)
        for d in range(count):
            at = slice(d * rows, (d + 1) * rows)
            qkv_ref[at] = piece_refs[d][...]
            do_own = do_refs[d][...]
            do_ref[at] = do_own
            product = (do_own.astype(F32) * o_refs[d][...].astype(F32)).T
            for h in range(heads):
                delta[h : h + 1, at] = jnp.sum(
                    product[h * DH : (h + 1) * DH], axis=0, keepdims=True
                )

    here = pl.ds(pl.multiple_of(i * block, block), block)
    q = qkv_ref[:, 0:width]
    k = qkv_ref[here, width : 2 * width]
    v = qkv_ref[here, 2 * width : 3 * width]
    do = do_ref[...]
    k_turned = k.T
    dk = dv = None
    for h in range(heads):
        own = lane == h
        k_own = jnp.where(own, k, jnp.zeros_like(k)) if heads > 1 else k
        v_own = jnp.where(own, v, jnp.zeros_like(v)) if heads > 1 else v
        scores = dot_nt(k_own, q) * (0.125 * LOG2E)
        probs = jnp.exp2(scores - log_ref[h : h + 1, :])
        prob_grad = dot_nt(v_own, do)
        score_grad = (probs * (prob_grad - delta[h : h + 1, :])).astype(BF)
        part = slice(h * DH, (h + 1) * DH)
        dq_sum[part, :] += dot_nn(k_turned[part], score_grad)
        dv_own = dot_nn(probs.astype(BF), do)
        dk_own = dot_nn(score_grad, q)
        dv = dv_own if dv is None else jnp.where(own, dv_own, dv)
        dk = dk_own if dk is None else jnp.where(own, dk_own, dk)
    dk = dk * 0.125
    dk = (dk * cos_ref[here, :] - swap_halves(dk) * sin_ref[here, :]).astype(BF)
    dv = dv.astype(BF)
    per = block // rows
    for d, out_ref in enumerate(out_refs):

        @pl.when(i == d // per)
        def _(d=d, out_ref=out_ref):
            at = slice((d % per) * rows, (d % per + 1) * rows)
            out_ref[:, width : 2 * width] = dk[at]
            out_ref[:, 2 * width : 3 * width] = dv[at]

    @pl.when(i == pl.num_programs(0) - 1)
    def _():
        dq = (dq_sum[...] * 0.125).T
        dq = (dq * cos_ref[...] - swap_halves(dq) * sin_ref[...]).astype(BF)
        for d, out_ref in enumerate(out_refs):
            out_ref[:, 0:width] = dq[d * rows : (d + 1) * rows]


def attend_back(pieces, do, chunk, o, log_total, cosine, sine, heads):
    count, rows = len(pieces), pieces[0].shape[0]
    length = count * rows
    width = heads * DH
    block = min(512, length)
    operands = (*pieces, *do, *o, log_total, cosine, sine)
    return pl.pallas_call(
        functools.partial(attend_back_kernel, heads, block, count),
        grid=(length // block,),
        in_specs=[whole(p.shape) for p in pieces]
        + [pl.BlockSpec((rows, width), lambda i: (0, chunk))] * count
        + [whole(a.shape) for a in operands[2 * count :]],
        out_specs=[whole((rows, 3 * width))] * count,
        out_shape=[jax.ShapeDtypeStruct((rows, 3 * width), BF)] * count,
        scratch_shapes=[
            pltpu.VMEM((length, 3 * width), BF),
            pltpu.VMEM((length, width), BF),
            pltpu.VMEM((width, length), F32),
            pltpu.VMEM((heads, length), F32),
        ],
        compiler_params=params(60),
        cost_estimate=cost(24 * length * length * DH * heads, 20 * length * width),
    )(*operands)


def pieces_at(me_ref, count, groups, width, part=0, parts_width=0):
    for c in range(count):
        for d in range(groups):
            at = (lax.bitwise_xor(me_ref[0], d) * count + c) * width + part * parts_width
            yield c, d, pl.ds(pl.multiple_of(at, 128), width)


def out_kernel(count, groups, me_ref, *refs):
    o_refs = refs[: count * groups]
    w_ref, hidden_ref, mod_ref, attended_ref, branch_ref, middle_ref, normed_ref = refs[
        count * groups :
    ]
    for c, d, columns in pieces_at(me_ref, count, groups, o_refs[0].shape[1]):
        attended_ref[:, columns] = o_refs[c * groups + d][...]
    branch = dot_nn(attended_ref[...], w_ref[...])
    branch_ref[...] = branch
    middle = hidden_ref[...] + mod_ref[2:3] * branch
    middle_ref[...] = middle
    normal, _ = normalise(middle)
    normed_ref[...] = (normal * (1.0 + mod_ref[4:5]) + mod_ref[3:4]).astype(BF)


def out_forward(chunks, weight, hidden, mod, at, me):
    rows, width = hidden.shape
    block = min(256, rows)
    row_spec = pl.BlockSpec((block, width), lambda i, *_: (i, 0))
    count, groups = len(chunks), len(chunks[0])
    o_spec = pl.BlockSpec((block, chunks[0][0].shape[1]), lambda i, *_: (i, 0))
    return pl.pallas_call(
        functools.partial(out_kernel, count, groups),
        grid_spec=with_place(
            (rows // block,),
            [o_spec] * (count * groups)
            + [pl.BlockSpec((width, width), lambda *_: (0, at)), row_spec, whole(mod.shape)],
            [row_spec] * 4,
        ),
        out_shape=[
            jax.ShapeDtypeStruct((rows, width), BF),
            jax.ShapeDtypeStruct((rows, width), F32),
            jax.ShapeDtypeStruct((rows, width), F32),
            jax.ShapeDtypeStruct((rows, width), BF),
        ],
        compiler_params=params(60),
        cost_estimate=cost(2 * rows * width * width, 18 * rows * width + 2 * width * width),
    )(me, *[piece for chunk in chunks for piece in chunk], weight, hidden, mod)


def ffn_kernel(
    owned, x_ref, dc_ref, up_ref, packed_ref, y_ref, dx_ref, activated_ref, up_cot_ref, dn_ref
):
    @pl.when(pl.program_id(0) == 0)
    def _():
        y_ref[...] = jnp.zeros_like(y_ref)
        dx_ref[...] = jnp.zeros_like(dx_ref)

    stack_rows(packed_ref, dn_ref, owned)
    up, dn = up_ref[...], dn_ref[...]
    value, slope = gelu_and_slope(dot_nn(x_ref[...], up))
    activated = value.astype(BF)
    up_cot = (dot_nt(dc_ref[...], dn) * slope).astype(BF)
    activated_ref[...] = activated
    up_cot_ref[...] = up_cot
    y_ref[...] += dot_nn(activated, dn)
    dx_ref[...] += dot_nt(up_cot, up)


def ffn_grad_kernel(
    owned, x_ref, dc_ref, activated_ref, up_cot_ref, grads_ref, x_turned, gu, gd, sems
):
    i, last = pl.program_id(0), pl.num_programs(0) - 1
    slot = lax.rem(i, 2)
    block = up_cot_ref.shape[1]
    part = gd.shape[1]
    pieces = block // part

    def sends(step, at):
        across = pl.ds(pl.multiple_of(step * block, block), block)
        down = pl.ds(pl.multiple_of(step * part, part), part)
        half = grads_ref.shape[1] // 2
        return (
            pltpu.make_async_copy(gu.at[at], grads_ref.at[:, across], sems.at[0, at]),
            pltpu.make_async_copy(gd.at[at], grads_ref.at[down, pl.ds(half, half)], sems.at[1, at]),
        )

    @pl.when(i == 0)
    def _():
        x_turned[...] = x_ref[...].T

    @pl.when(i >= 2)
    def _():
        for copy in sends(i - 2, slot):
            copy.wait()

    dc = dc_ref[...]
    gu[slot] = dot_nn(x_turned[...], up_cot_ref[...]).astype(BF)
    down_grad = dot_tn(activated_ref[...], dc).astype(BF)
    width = dc.shape[1]
    for r in range(part // owned):
        for q in range(pieces):
            at = (r * pieces + q) * owned
            gd[slot, r * owned : (r + 1) * owned, q * width : (q + 1) * width] = down_grad[
                at : at + owned
            ]
    for copy in sends(i, slot):
        copy.start()

    @pl.when(i == last)
    def _():
        for copy in sends(last - 1, 1 - slot) + sends(last, slot):
            copy.wait()


FFN_BLOCK = 512


def ffn(x, dc, weights, owned):
    rows, width = x.shape
    hidden_width = FF
    pieces = hidden_width // width
    block = FFN_BLOCK
    steps = hidden_width // block
    part = block // pieces
    packed, piece = weights, owned
    if owned % 16:
        full = stacked(weights[:, :hidden_width], owned, width)
        packed, piece = side_by_side_blocks(full, part, pieces), part
    across = pl.BlockSpec((rows, block), lambda i: (0, i))
    return pl.pallas_call(
        functools.partial(ffn_kernel, piece),
        grid=(steps,),
        in_specs=[
            whole(x.shape),
            whole(x.shape),
            pl.BlockSpec((width, block), lambda i: (0, steps + i)),
            pl.BlockSpec((part, hidden_width), lambda i: (i, 0)),
        ],
        out_specs=[whole(x.shape), whole(x.shape), across, across],
        out_shape=[
            jax.ShapeDtypeStruct((rows, width), F32),
            jax.ShapeDtypeStruct((rows, width), F32),
            jax.ShapeDtypeStruct((rows, hidden_width), BF),
            jax.ShapeDtypeStruct((rows, hidden_width), BF),
        ],
        scratch_shapes=[pltpu.VMEM((block, width), BF)],
        compiler_params=params(60),
        cost_estimate=cost(8 * rows * width * hidden_width, 8 * width * hidden_width),
    )(x, dc, weights, packed)


def ffn_grad(x, dc, activated, up_cot, owned):
    rows, width = x.shape
    hidden_width = activated.shape[1]
    pieces = hidden_width // width
    block = FFN_BLOCK
    part = block // pieces
    across = pl.BlockSpec((rows, block), lambda i: (0, i))
    grads = pl.pallas_call(
        functools.partial(ffn_grad_kernel, owned if owned % 16 == 0 else part),
        grid=(hidden_width // block,),
        in_specs=[whole(x.shape), whole(x.shape), across, across],
        out_specs=pl.BlockSpec(memory_space=pl.ANY),
        out_shape=jax.ShapeDtypeStruct((width, 2 * hidden_width), BF),
        scratch_shapes=[
            pltpu.VMEM((width, rows), BF),
            pltpu.VMEM((2, width, block), BF),
            pltpu.VMEM((2, part, hidden_width), BF),
            pltpu.SemaphoreType.DMA((2, 2)),
        ],
        compiler_params=params(60),
        cost_estimate=cost(4 * rows * width * hidden_width, 8 * width * hidden_width),
    )(x, dc, activated, up_cot)
    if owned % 16:
        full = stacked(grads[:, hidden_width:], part, width)
        grads = jnp.concatenate(
            [grads[:, :hidden_width], side_by_side_blocks(full, owned, pieces)], axis=1
        )
    return grads


def mid_kernel(groups, me_ref, *refs):
    y_ref, dx_ref, middle_ref, branch_ref, grad_ref, w_ref, mod_ref = refs[:7]
    block_ref, mgrad_ref, bcot_ref, sums_ref = refs[7:11]
    piece_refs, attended_grad = refs[11:-1], refs[-1]

    @pl.when(pl.program_id(0) == 0)
    def _():
        sums_ref[...] = jnp.zeros_like(sums_ref)

    y, middle, w = y_ref[...], middle_ref[...], dx_ref[...]
    grad = grad_ref[...].astype(F32)
    block_ref[...] = (middle + mod_ref[5:6] * y).astype(BF)
    normal, inverse = normalise(middle)
    middle_grad = grad + norm_back(normal, inverse, w * (1.0 + mod_ref[4:5]))
    mgrad_ref[...] = middle_grad
    branch_cot = (middle_grad * mod_ref[2:3]).astype(BF)
    bcot_ref[...] = branch_cot
    sums_ref[0:1] += jnp.sum(middle_grad * branch_ref[...], axis=0, keepdims=True)
    sums_ref[1:2] += jnp.sum(w, axis=0, keepdims=True)
    sums_ref[2:3] += jnp.sum(w * normal, axis=0, keepdims=True)
    sums_ref[3:4] += jnp.sum(grad * y, axis=0, keepdims=True)
    attended_grad[...] = dot_nt(branch_cot, w_ref[...]).astype(BF)
    for _, d, columns in pieces_at(me_ref, 1, groups, piece_refs[0].shape[1]):
        piece_refs[d][...] = attended_grad[:, columns]


def mid_back(y, dx, middle, branch, grad, weight, mod, at, me, groups):
    rows, width = y.shape
    block = min(256, rows)
    cols = width // groups
    row_spec = pl.BlockSpec((block, width), lambda i, *_: (i, 0))
    piece_spec = pl.BlockSpec((block, cols), lambda i, *_: (i, 0))
    return pl.pallas_call(
        functools.partial(mid_kernel, groups),
        grid_spec=with_place(
            (rows // block,),
            [row_spec] * 5 + [pl.BlockSpec((width, width), lambda *_: (0, at)), whole(mod.shape)],
            [row_spec] * 3 + [whole((8, width))] + [piece_spec] * groups,
            [pltpu.VMEM((block, width), BF)],
        ),
        out_shape=[
            jax.ShapeDtypeStruct((rows, width), BF),
            jax.ShapeDtypeStruct((rows, width), F32),
            jax.ShapeDtypeStruct((rows, width), BF),
            jax.ShapeDtypeStruct((8, width), F32),
        ]
        + [jax.ShapeDtypeStruct((rows, cols), BF)] * groups,
        compiler_params=params(60),
        cost_estimate=cost(2 * rows * width * width, 28 * rows * width + 2 * width * width),
    )(me, y, dx, middle, branch, grad, weight, mod)


def last_kernel(count, groups, owned, me_ref, *refs):
    piece_refs = refs[: count * groups]
    rest = refs[count * groups :]
    hidden_ref, mgrad_ref, wq_ref, wk_ref, wv_ref, packed_ref, mod_ref = rest[:7]
    hgrad_ref, frames_ref, skips_ref, sums_ref, wskip_ref, cot_ref = rest[7:]

    @pl.when(pl.program_id(0) == 0)
    def _():
        sums_ref[...] = jnp.zeros_like(sums_ref)
        stack_rows(packed_ref, wskip_ref, owned)

    width = piece_refs[0].shape[1] // 3
    model = hidden_ref.shape[1]
    for part in range(3):
        for c, d, columns in pieces_at(me_ref, count, groups, width, part, model):
            cot_ref[:, columns] = piece_refs[c * groups + d][
                :, part * width : (part + 1) * width
            ]
    w = (
        dot_nt(cot_ref[:, :model], wq_ref[...])
        + dot_nt(cot_ref[:, model : 2 * model], wk_ref[...])
        + dot_nt(cot_ref[:, 2 * model :], wv_ref[...])
    )
    normal, inverse = normalise(hidden_ref[...])
    sums_ref[0:1] += jnp.sum(w, axis=0, keepdims=True)
    sums_ref[1:2] += jnp.sum(w * normal, axis=0, keepdims=True)
    hidden_grad = (
        mgrad_ref[...] + norm_back(normal, inverse, w * (1.0 + mod_ref[1:2]))
    ).astype(BF)
    hgrad_ref[...] = hidden_grad
    frames_ref[...] = dot_nt(hidden_grad, wskip_ref[:model]).astype(BF)
    skips_ref[...] = dot_nt(hidden_grad, wskip_ref[model:]).astype(BF)


def last_back(chunks, hidden, middle_grad, weights, mod, owned, me):
    rows, width = hidden.shape
    block = min(256, rows)
    row_spec = pl.BlockSpec((block, width), lambda i, *_: (i, 0))
    count, groups = len(chunks), len(chunks[0])
    piece_spec = pl.BlockSpec((block, chunks[0][0].shape[1]), lambda i, *_: (i, 0))
    w_skip, skip_spec, piece = skip_weight(weights, owned, width)

    def part_spec(part):
        return pl.BlockSpec((width, width), lambda *_: (0, 2 + part))

    return pl.pallas_call(
        functools.partial(last_kernel, count, groups, piece),
        grid_spec=with_place(
            (rows // block,),
            [piece_spec] * (count * groups)
            + [row_spec, row_spec, part_spec(0), part_spec(1), part_spec(2)]
            + [skip_spec, whole(mod.shape)],
            [row_spec, row_spec, row_spec, whole((8, width))],
            [pltpu.VMEM((2 * width, width), BF), pltpu.VMEM((block, 3 * width), BF)],
        ),
        out_shape=[
            jax.ShapeDtypeStruct((rows, width), BF),
            jax.ShapeDtypeStruct((rows, width), BF),
            jax.ShapeDtypeStruct((rows, width), BF),
            jax.ShapeDtypeStruct((8, width), F32),
        ],
        compiler_params=params(60),
        cost_estimate=cost(2 * rows * width * width, 4 * rows * width),
    )(
        me,
        *[piece for chunk in chunks for piece in chunk],
        hidden,
        middle_grad,
        weights,
        weights,
        weights,
        w_skip,
        mod,
    )


def out_wgrad_kernel(left_ref, right_ref, out_ref):
    out_ref[...] = dot_tn(left_ref[...], right_ref[...]).astype(BF)


def out_wgrad_part(left, right, columns):
    rows, width = left.shape
    block = 512
    first = columns // block - width // block
    return pl.pallas_call(
        out_wgrad_kernel,
        grid=(width // block,),
        in_specs=[whole(left.shape), pl.BlockSpec((rows, block), lambda i: (0, i))],
        out_specs=pl.BlockSpec((width, block), lambda i: (0, first + i)),
        out_shape=jax.ShapeDtypeStruct((width, columns), BF),
        compiler_params=params(60),
        cost_estimate=cost(2 * rows * width * width, 6 * width * width),
    )(left, right)


def qkv_grad_kernel(groups, me_ref, *refs):
    x_ref, piece_refs = refs[0], refs[1 : 1 + groups]
    out_ref, piece, x_turned = refs[-3:]
    i = pl.program_id(0)

    @pl.when(i == 0)
    def _():
        x_turned[...] = x_ref[...].T

    for d, ref in enumerate(piece_refs):

        @pl.when(i == d)
        def _(ref=ref):
            piece[...] = ref[...]

    out_ref[...] = dot_nn(x_turned[...], piece[...]).astype(BF)


def qkv_grad(normed, pieces, me, held=None):
    groups = len(pieces)
    rows, cols = pieces[0].shape
    width = normed.shape[1]
    given = [] if held is None else [held]
    return pl.pallas_call(
        functools.partial(qkv_grad_kernel, groups),
        grid_spec=with_place(
            (groups,),
            [whole(normed.shape)]
            + [whole((rows, cols))] * groups
            + [pl.BlockSpec(memory_space=pl.ANY)] * len(given),
            pl.BlockSpec((width, cols), lambda i, me: (0, lax.bitwise_xor(i, me[0]))),
            [pltpu.VMEM((rows, cols), BF), pltpu.VMEM((width, rows), BF)],
        ),
        out_shape=jax.ShapeDtypeStruct((width, groups * cols) if held is None else held.shape, BF),
        input_output_aliases={2 + groups: 0} if given else {},
        compiler_params=params(40),
        cost_estimate=cost(rows * width, 1024),
    )(me, normed, *pieces, *given)


def update_kernel(grads_of, rates, *refs):
    count = len(rates)
    outs, states, given = refs[-2 * count :], refs[-3 * count : -2 * count], refs[: -3 * count]
    correction = 1.0 - 0.5**STEP
    for at, rows, cols, gradient in grads_of(*given):
        state, new_ref, moments_ref = states[at], outs[2 * at], outs[2 * at + 1]
        master = state[0, rows, cols]
        first = 0.5 * state[1, rows, cols] + 0.5 * gradient
        second = 0.5 * state[2, rows, cols] + 0.5 * gradient * gradient
        moments_ref[0, rows, cols] = first
        moments_ref[1, rows, cols] = second
        new_ref[rows, cols] = master - rates[at] * (
            first / correction / (jnp.sqrt(second / correction) + 1e-08) + 0.01 * master
        )


def update(grads_of, given, states, rates):
    shapes = []
    for state in states:
        _, rows, cols = state.shape
        shapes += [(rows, cols), (2, rows, cols)]
    moved = 6 * sum(state.size for state in states) * 4 // 3
    return pl.pallas_call(
        functools.partial(update_kernel, grads_of, rates),
        grid=(1,),
        in_specs=[whole(a.shape) for a in (*given, *states)],
        out_specs=[whole(shape) for shape in shapes],
        out_shape=[jax.ShapeDtypeStruct(shape, F32) for shape in shapes],
        compiler_params=params(40),
        cost_estimate=cost(moved, moved),
    )(*given, *states)


def skip_grads(*refs):
    half = refs[0].shape[1]
    for side in range(2):
        rest, arrived = refs[2 * side][...], refs[2 * side + 1][...]
        yield 0, slice(None), slice(side * half, (side + 1) * half), rest + arrived.astype(F32)


def ffn_grads(rest_ref, arrived_ref):
    owned, cols = rest_ref.shape
    hidden_width, width = cols // 2, D
    for q in range(cols // width):
        at = slice(q * width, (q + 1) * width)
        gradient = rest_ref[:, at] + arrived_ref[:, at].astype(F32)
        if q * width < hidden_width:
            yield 0, slice(None), at, gradient
        else:
            r = q - hidden_width // width
            yield 1, slice(r * owned, (r + 1) * owned), slice(None), gradient


def attention_columns(count, groups):
    cols = D // (count * groups)
    for c in range(count):
        for j in range(groups):
            for part in range(3):
                yield 0, part * D + (j * count + c) * cols, cols
        if c == 0:
            yield 1, 0, D


def attention_grads(count, groups, rest_ref, arrived_ref):
    at = 0
    for weight, to, cols in attention_columns(count, groups):
        here = slice(at, at + cols)
        gradient = rest_ref[:, here] + arrived_ref[:, here].astype(F32)
        yield weight, slice(None), slice(to, to + cols), gradient
        at += cols


def modulation_grads(time_ref, cots_ref):
    for at in range(0, cots_ref.shape[1], D):
        gradient = lax.dot_general(
            time_ref[...],
            cots_ref[:, at : at + D],
            (((0,), (0,)), ((), ())),
            precision=highest,
            preferred_element_type=F32,
        )
        yield 0, slice(None), slice(at, at + D), gradient


def bits_of(axis):
    size = lax.axis_size(axis)
    return [(axis, b) for b in reversed(range(size.bit_length() - 1))]


def my_bit(level):
    axis, bit = level
    return (lax.axis_index(axis) >> bit) & 1


def swap(values, level):
    axis, bit = level
    return lax.ppermute(values, axis, [(i, i ^ (1 << bit)) for i in range(lax.axis_size(axis))])


def after(values, *others):
    return lax.optimization_barrier((values, *others))[0]


class ModulationCots:
    def __init__(self, own):
        self.own, self.order = own, bits_of("seq")[::-1] + bits_of("dp")[::-1]
        self.arrived = None

    def settle(self, *waits):
        if self.arrived is None:
            return
        level, other = self.arrived
        other = after(other, *waits) if waits else other
        if level[0] == "seq":
            self.own = self.own + other
        else:
            self.own = jnp.where(
                my_bit(level) == 0,
                jnp.concatenate([self.own, other], axis=0),
                jnp.concatenate([other, self.own], axis=0),
            )
        self.arrived = None

    def step(self, *waits):
        self.settle(*waits)
        level = self.order.pop(0)
        self.arrived = (level, swap(self.own, level))


class ScatterSum:
    def __init__(self, grad, order, dims):
        self.dims, self.order = list(dims), list(order)
        rows, cols = grad.shape
        split = [2] * len(self.dims)
        self.terms = [grad.reshape(split + [rows // 2 ** len(split), cols])]

    def hold(self, *waits):
        if waits:
            self.terms[-1] = after(self.terms[-1], *waits)

    def step(self, *waits, late=()):
        self.hold(*waits)
        level = self.order.pop(0)
        at, mine = self.dims.index(level), my_bit(level)
        self.dims.pop(at)

        def halves(side):
            return [lax.dynamic_index_in_dim(t, side, at, keepdims=False) for t in self.terms]

        leaving = halves(1 - mine)
        total = leaving[0]
        if len(leaving) > 1:
            total = sum(t.astype(F32) for t in leaving).astype(total.dtype)
        total = after(total, *late) if late else total
        self.sent = total
        arrived = swap(total, level)
        self.terms = halves(mine) + [arrived]
        return arrived

    def ends(self):
        return [sum(t.astype(F32) for t in self.terms[:-1]), self.terms[-1]]


def exchange(pieces):
    places = range(len(pieces))
    return [pieces[0]] + [
        lax.ppermute(pieces[d], "seq", [(i, i ^ d) for i in places]) for d in places[1:]
    ]


def dot_tn_exact(left, right):
    return lax.dot_general(
        left,
        right,
        (((0,), (0,)), ((), ())),
        precision=highest,
        preferred_element_type=F32,
    )


def attention_total(total, count, groups):
    runs, at = ([], []), 0
    for weight, to, cols in attention_columns(count, groups):
        runs[weight].append((to, total[:, at : at + cols]))
        at += cols
    return [jnp.concatenate([v for _, v in sorted(r, key=lambda v: v[0])], axis=1) for r in runs]


def in_order(pieces, me, parts):
    groups, rows = len(pieces), pieces[0].shape[0]
    stack = jnp.take(jnp.stack(pieces), jnp.arange(groups) ^ me[0], axis=0)
    return stack.reshape(groups, rows, parts, -1).transpose(1, 2, 0, 3).reshape(rows, -1)


def by_place(values, me, groups):
    parts = jnp.split(values, groups, axis=1)
    stack = jnp.take(jnp.stack(parts), jnp.arange(groups) ^ me[0], axis=0)
    return [stack[d] for d in range(groups)]


def modulation_rows(partial, order, wait):
    dims = bits_of("dp")
    count, cols = partial.shape
    held = partial.reshape([2] * len(dims) + [count // 2 ** len(dims), cols])
    for level in order:
        at, mine = dims.index(level), my_bit(level)
        dims.pop(at)
        leaving = lax.dynamic_index_in_dim(held, 1 - mine, at, keepdims=False)
        held = lax.dynamic_index_in_dim(held, mine, at, keepdims=False) + swap(leaving, level)
    held = after(held, wait)
    for level in bits_of("seq"):
        held = held + swap(held, level)
    return held


def side_by_side(own, rows):
    return jnp.concatenate(jnp.split(own, own.shape[0] // rows, axis=0), axis=1)


def stacked(full, rows, cols):
    pieces = full.shape[1] // cols
    blocks = full.reshape(full.shape[0] // rows, rows, pieces, cols)
    return blocks.transpose(0, 2, 1, 3).reshape(full.shape[0] * pieces, cols)


def side_by_side_blocks(full, rows, pieces):
    cols = full.shape[1]
    blocks = full.reshape(full.shape[0] // (rows * pieces), pieces, rows, cols)
    return blocks.transpose(0, 2, 1, 3).reshape(full.shape[0] // pieces, pieces * cols)


def gather_pairwise(own, order, last_waits=(), last_use=()):
    rows, cols = own.shape
    held, bits = own.reshape(1, rows, cols), []
    for level in order:
        last = len(bits) == len(order) - 1
        if last and last_waits:
            held = after(held, *last_waits)
        other = swap(held, level)
        if last and last_use:
            other = after(other, *last_use)
        at = sum(1 for bit in bits if bit > level[1])
        bits.append(level[1])
        shape = [2] * (len(bits) - 1)
        own_part = held.reshape(shape + [rows, cols])
        other_part = other.reshape(shape + [rows, cols])
        held = jnp.where(
            my_bit(level) == 0,
            jnp.stack([own_part, other_part], axis=at),
            jnp.stack([other_part, own_part], axis=at),
        ).reshape(2 ** len(bits), rows, cols)
    return held.reshape(-1, cols)


def per_device(
    frames_in,
    skip_in,
    condition,
    flow_time,
    span_start,
    span_length,
    out_grad,
    skip_proj_state,
    attn_qkv_state,
    attn_out_state,
    ffn_up_state,
    ffn_down_state,
    ada_mod_state,
):
    utter_count, rows, width = frames_in.shape
    seq = lax.axis_size("seq")
    everyone = ("dp", "seq")
    owned = attn_qkv_state.shape[1]
    hidden_width = ffn_up_state.shape[2]
    length = rows * seq
    me = lax.axis_index(everyone)
    positions = lax.axis_index("seq") * rows + jnp.arange(rows, dtype=jnp.int32)

    group_heads = HEADS // seq
    heads = min(2, group_heads)
    count = group_heads // heads

    first_own = jnp.concatenate(
        [side_by_side(skip_proj_state[0].astype(BF), owned), attn_qkv_state[0].astype(BF)],
        axis=1,
    )
    first_part = gather_pairwise(first_own, bits_of("seq"))
    first_full = lax.all_gather(first_part, "dp", axis=0, tiled=True)
    out_at = 2 * hidden_width // width

    dp_bits, seq_bits = bits_of("dp"), bits_of("seq")
    core, planes = dp_bits[-1], dp_bits[:-1]

    time_code = time_features(flow_time, width).astype(BF)
    time_own = lax.dynamic_slice_in_dim(time_code, me * owned, owned, 1)
    mod_part = jnp.dot(time_own, ada_mod_state[0].astype(BF), preferred_element_type=F32)
    modulation = modulation_rows(mod_part, [core] + planes, first_part)

    place = lax.axis_index("seq").astype(jnp.int32).reshape(1)
    frame = jnp.arange(length, dtype=jnp.int32)
    frame = ((frame // rows) ^ place) * rows + frame % rows
    cos_all, sin_all = rotary_tables(frame, heads)
    wide = heads == 2
    cos_own, sin_own = rotary_tables(positions, 2)
    span_stop = span_start + span_length

    outs = []
    assert utter_count == 1
    mod = modulation.reshape(6, width)
    inside = (positions >= span_start[0]) & (positions < span_stop[0])
    frames, skips = frames_in[0], skip_in[0]
    cond = jnp.where(inside[:, None], jnp.zeros_like(condition[0]), condition[0])
    grad = jnp.where(inside[:, None], out_grad[0], jnp.zeros_like(out_grad[0]))
    down_cot = (grad.astype(F32) * mod[5:6]).astype(BF)

    hidden, normed = skip_forward(frames, skips, cond, first_full, mod, owned)
    if wide:
        packed = qkv_forward(normed, first_full, cos_own, sin_own, count, place)
    else:
        (pairs,) = qkv_forward(normed, first_full, cos_own, sin_own, 1, 0 * place)
        split = jnp.concatenate(
            [p.reshape(rows, 3, 2, DH).transpose(0, 2, 1, 3).reshape(rows, -1) for p in pairs],
            axis=1,
        )
        packed = [by_place(split, place, seq)]
    arrived = [exchange(part) for part in packed]
    second_own = jnp.concatenate(
        [
            side_by_side(ffn_down_state[0].astype(BF), owned),
            ffn_up_state[0].astype(BF),
            attn_out_state[0].astype(BF),
        ],
        axis=1,
    )
    early = (cos_all, sin_all, cos_own, sin_own, cond, grad, down_cot)
    second_own = gather_pairwise(after(second_own, modulation), seq_bits, early, (packed[0][0],))
    second_full = lax.all_gather(second_own, "dp", axis=0, tiled=True)
    qkv_chunks, attended = [], []
    for pieces in arrived:
        waits = attended[-1][0][:1] if attended else [second_own]
        pieces[1:] = [after(piece, *waits) for piece in pieces[1:]]
        qkv_chunks.append(pieces)
        attended.append(attend(pieces, heads))
    o_chunks = []
    for c, (o, _) in enumerate(attended):
        pieces = exchange(o)
        if c < count - 1:
            pieces[1:] = [after(piece, attended[c + 1][0][0]) for piece in pieces[1:]]
        o_chunks.append(pieces)
    here = place
    if not wide:
        o_chunks, here = [[in_order(o_chunks[0], place, 1)]], 0 * place

    attended_low, branch, middle, normed_two = out_forward(
        o_chunks, second_full, hidden, mod, out_at, here
    )
    downward, normed_two_grad, *ffn_kept = ffn(normed_two, down_cot, second_full, owned)
    mid = mid_back(
        downward,
        normed_two_grad,
        middle,
        branch,
        grad,
        second_full,
        mod,
        out_at,
        here,
        seq if wide else 1,
    )
    do_pieces = exchange(mid[4:] if wide else by_place(mid[4], place, seq))
    block_out, middle_grad, branch_cot, mid_sums = mid[:4]
    every_bit = dp_bits + seq_bits
    rising = seq_bits[::-1]
    ffn_whole = ffn_grad(after(normed_two, mid[4]), down_cot, *ffn_kept, owned)
    ffn_whole = after(ffn_whole, *do_pieces[1:])
    ffn_part = lax.psum_scatter(ffn_whole, "dp", scatter_dimension=0, tiled=True)
    do_pieces[1:] = [after(piece, ffn_whole) for piece in do_pieces[1:]]
    backs = []
    for c in range(count):
        o, log_total = attended[c]
        backs.append(
            attend_back(qkv_chunks[c], do_pieces, c, o, log_total, cos_all, sin_all, heads)
        )
    cot_chunks = [exchange(b) for b in backs]
    qkv_part = None
    if wide:
        qkv_part = out_wgrad_part(
            after(attended_low, backs[-1][0]), branch_cot, 3 * width // count + width
        )

    sent = [backs[-1][0]]

    def leave(part):
        part.step(sent[-1])
        sent.append(part.sent)

    def wait_in_turn(pieces):
        return pieces[:1] + [after(piece, sent[-1]) for piece in pieces[1:]]

    def full_sum(grad_part, planes_first):
        return ScatterSum(grad_part, [core] + planes_first, every_bit)

    qkv_sums = []
    for c in range(count):
        pieces = cot_chunks[c] = wait_in_turn(cot_chunks[c])
        if not wide:
            cot_chunks = [[in_order(pieces, place, 3)]]
            qkv_part = jnp.concatenate(
                [dot_tn(normed, cot_chunks[0][0]), dot_tn(attended_low, branch_cot)], axis=1
            ).astype(BF)
        else:
            qkv_part = qkv_grad(normed, pieces, place, None if c else qkv_part)
        qkv_sums.append(full_sum(qkv_part, planes if c % 2 else planes[::-1]))
        sent.append(qkv_part)
    for part in qkv_sums:
        part.hold(*cot_chunks[-1][1:])
        leave(part)
    for part in qkv_sums:
        leave(part)
    ffn_sum = ScatterSum(ffn_part, rising, seq_bits)
    leave(ffn_sum)
    cot_chunks[-1] = [after(piece, sent[-1]) for piece in cot_chunks[-1]]
    hidden_grad, frames_grad, skip_grad, last_sums = last_back(
        cot_chunks, hidden, middle_grad, first_full, mod, owned, here
    )
    skip_cot = after(hidden_grad, qkv_sums[-1].terms[-1])
    skip_part = jnp.concatenate(
        [dot_tn(frames, skip_cot).astype(BF), dot_tn(skips, skip_cot).astype(BF)], axis=0
    )
    skip_part = after(skip_part, ffn_sum.terms[-1])
    half = width // 2
    skip_sums = [
        ScatterSum(skip_part[:, :half], [core] + planes[::-1] + rising, every_bit),
        ScatterSum(skip_part[:, half:], [core] + planes + rising, every_bit),
    ]
    mod_cot = jnp.concatenate(
        [last_sums[0], last_sums[1], mid_sums[0], mid_sums[1], mid_sums[2], mid_sums[3]]
    ).reshape(1, 6 * width)
    mod_cots = ModulationCots(mod_cot)
    while mod_cots.order[0][0] == "seq":
        mod_cots.step(skip_part)
    mod_cots.settle()
    time_rows = time_own.astype(F32)
    qkv_sum, marks = None, []
    rows_held = owned * seq
    for part in [ffn_sum] + qkv_sums:
        part.hold(hidden_grad)
    ffn_sum.hold(mod_cots.own)
    while skip_sums[0].order or qkv_sum is None or qkv_sum.order:
        for part in skip_sums:
            if part.order:
                leave(part)
        marks.append(sent[-1])
        if mod_cots.order:
            mod_cots.step(sent[-1])
        later = [part for part in qkv_sums if part.order]
        for part in ([ffn_sum] if ffn_sum.order else []) + later:
            leave(part)
        if qkv_sum is not None and qkv_sum.order and len(marks) > 3:
            leave(qkv_sum)
        if not later and qkv_sum is None:
            for part in qkv_sums:
                part.hold(sent[-1])
            qkv_done = [sum(p.ends()).astype(BF).reshape(rows_held, -1) for p in qkv_sums]
            qkv_sum = ScatterSum(jnp.concatenate(qkv_done, axis=1), rising, seq_bits)
            leave(qkv_sum)
    while ffn_sum.order:
        leave(ffn_sum)
    while mod_cots.order:
        mod_cots.step()
    mod_cots.settle(marks[-1])
    mod_cots = mod_cots.own
    ffn_sum.hold(marks[-3])

    rates = learning_rates()
    outs = [block_out[None], frames_grad[None], skip_grad[None]]
    if owned % 16:
        ffn_total, qkv_total = sum(ffn_sum.ends()), sum(qkv_sum.ends())
        skip_total = jnp.concatenate([sum(part.ends()) for part in skip_sums], axis=1)
        mod_total = dot_tn_exact(time_rows, mod_cots)
        qkv_total, out_total = attention_total(
            qkv_total, count if wide else 1, seq if wide else 1
        )
        grads = (
            skip_total.reshape(2 * owned, width),
            qkv_total,
            out_total,
            ffn_total[:, :hidden_width],
            stacked(ffn_total[:, hidden_width:], owned, width),
            mod_total,
        )
        states = (
            skip_proj_state,
            attn_qkv_state,
            attn_out_state,
            ffn_up_state,
            ffn_down_state,
            ada_mod_state,
        )
        for state, gradient, rate in zip(states, grads, rates):
            outs.extend(adamw_step(state, gradient, rate))
        return tuple(outs)
    ffn_new = update(ffn_grads, ffn_sum.ends(), [ffn_up_state, ffn_down_state], rates[3:5])
    qkv_new = update(
        functools.partial(attention_grads, count if wide else 1, seq if wide else 1),
        qkv_sum.ends(),
        [attn_qkv_state, attn_out_state],
        rates[1:3],
    )
    mod_new = update(
        modulation_grads, [time_rows, after(mod_cots, marks[-1])], [ada_mod_state], rates[5:6]
    )
    skip_new = update(
        skip_grads,
        skip_sums[0].ends() + skip_sums[1].ends(),
        [skip_proj_state],
        rates[:1],
    )
    outs += [*skip_new, *qkv_new, *ffn_new, *mod_new]
    return tuple(outs)


def solution(mesh):
    tokens = P("dp", "seq", None)
    state = P(None, ("dp", "seq"), None)
    master = P(("dp", "seq"), None)
    return jax.shard_map(
        per_device,
        mesh=mesh,
        in_specs=(tokens, tokens, tokens, P(), P("dp"), P("dp"), tokens) + (state,) * 6,
        out_specs=(tokens,) * 3 + (master, state) * 6,
        check_vma=False,
    )
```
